32 devices in a mesh: dp: 16 (over z, y, x), shard: 2 (over core).
Axes of the slice: x: 2, y: 2, z: 4, core: 2. Of those that a mesh axis runs over, the one named last changes fastest.
Arguments:
- images: bfloat16 [512, 197, 384], P(('dp', 'shard')), may hold values from -6 to 6
- counts: int32 [32], P(('dp', 'shard')), may hold values from 8 to 16, as said below
- cotangent: bfloat16 [512, 197, 384], P(('dp', 'shard')), may hold values from -6 to 6
- attn_gain: bfloat16 [384], P('shard'), may hold values from 0.5 to 1.5
- attn_shift: bfloat16 [384], P('shard'), may hold values from -3 to 3
- qkv_weight: bfloat16 [384, 1152], P('shard'), may hold values from -0.3125 to 0.3125
- query_bias: bfloat16 [384], P('shard'), may hold values from -4 to 4
- value_bias: bfloat16 [384], P('shard'), may hold values from -4 to 4
- proj_weight: bfloat16 [384, 384], P('shard'), may hold values from -1.25 to 1.25
- proj_bias: bfloat16 [384], P('shard'), may hold values from -3 to 3
- mlp_gain: bfloat16 [384], P('shard'), may hold values from 0.5 to 1.5
- mlp_shift: bfloat16 [384], P('shard'), may hold values from -3 to 3
- up_weight: bfloat16 [384, 1536], P('shard'), may hold values from -0.3125 to 0.3125
- up_bias: bfloat16 [1536], P('shard'), may hold values from -4 to 4
- down_weight: bfloat16 [1536, 384], P('shard'), may hold values from -0.15625 to 0.15625
- down_bias: bfloat16 [384], P('shard'), may hold values from -3 to 3
Outputs:
- layer_out: bfloat16 [512, 197, 384], P(('dp', 'shard'))
- images_grad: float32 [512, 197, 384], P(('dp', 'shard'))
- attn_gain_grad: float32 [384], P('shard')
- attn_shift_grad: float32 [384], P('shard')
- qkv_weight_grad: float32 [384, 1152], P('shard')
- query_bias_grad: float32 [384], P('shard')
- value_bias_grad: float32 [384], P('shard')
- proj_weight_grad: float32 [384, 384], P('shard')
- proj_bias_grad: float32 [384], P('shard')
- mlp_gain_grad: float32 [384], P('shard')
- mlp_shift_grad: float32 [384], P('shard')
- up_weight_grad: float32 [384, 1536], P('shard')
- up_bias_grad: float32 [1536], P('shard')
- down_weight_grad: float32 [1536, 384], P('shard')
- down_bias_grad: float32 [384], P('shard')
The draws below stay inside these ranges and needn't reach their ends.
Inputs may be any that keep to these rules, and one draw needn't show every extreme that they name: `counts`: live images of each device's 16 slots; live slots come first.
All inputs are finite; a program needn't handle non-finite values.
Results may differ from the reference program's by a relative error of at most 0.014.
Values may be sent and summed in bfloat16 or wider, within the bound.
No kernel may reach another device: no remote copies, remote signals or barrier semaphores. Data moves between devices by JAX's collectives and lax.ppermute only.
A program may use at most 256 MiB of HBM per device.

```python
import math
import jax
import jax.numpy as jnp
from jax import lax

D = 384
HEADS = 6
HEAD = 64
FF = 1536
SEQ = 197
IMG_CAP = 16
IMAGES = 512
DEVICES = 32


def draw_counts(key, part):
    key = jax.random.fold_in(key, 11)
    key_one, key_two = jax.random.split(key)
    smallest = IMG_CAP // 2
    drawn = jax.random.randint(key_one, (DEVICES,), smallest, IMG_CAP + 1, dtype=jnp.int32)
    chosen = jax.random.randint(key_two, (), 0, DEVICES, dtype=jnp.int32)
    drawn = drawn.at[chosen].set(IMG_CAP)
    drawn = drawn.at[(chosen + 1) % DEVICES].set(smallest)
    return drawn


def steps_of(key, shape, cuts, least, top_value):
    def one(dim, parts):
        draws = jax.random.uniform(jax.random.fold_in(jax.random.fold_in(key, 6), dim), (parts,), jnp.float32, least / len(cuts), top_value / len(cuts))
        return jnp.repeat(jnp.exp(draws), shape[dim] // parts).reshape((-1,) + (1,) * (len(shape) - dim - 1))

    factor_of = one(*cuts[0])
    for cut in cuts[1:]:
        factor_of = factor_of * one(*cut)
    return factor_of


def scatter_about(stream_key, dims, scale, most, cuts=(), kind=jnp.bfloat16):
    array = jax.random.normal(stream_key, dims, jnp.float32) * scale
    if len(cuts) > 0:
        array = steps_of(stream_key, dims, cuts, -0.22, 0.18) * array
    return jnp.clip(array, min=-most, max=most).astype(kind)


def setup_inputs(seed: int = 0) -> dict:
    key_of = jax.random.split(jax.random.key(seed), 17)
    images = scatter_about(key_of[0], (IMAGES, SEQ, D), 1.0, 6.0, ((0, 32),))
    counts = draw_counts(jax.random.fold_in(key_of[16], 71), 0)
    cotangent = scatter_about(key_of[2], (IMAGES, SEQ, D), 1.0, 6.0, ((0, 32),))
    attn_gain = jnp.clip(0.5 + 1.0 * jax.random.uniform(key_of[3], (D,), jnp.float32) ** steps_of(key_of[3], (D,), ((0, 2),), -0.2, 0.2), 0.5, 1.5).astype(jnp.bfloat16)
    attn_shift = scatter_about(key_of[4], (D,), 0.3, 3.0, ((0, 2),))
    qkv_weight = scatter_about(key_of[5], (D, 3 * D), D ** -0.5, 0.3125, ((0, 2),))
    query_bias = scatter_about(key_of[6], (D,), 0.5, 4.0, ((0, 2),))
    value_bias = scatter_about(key_of[7], (D,), 0.5, 4.0, ((0, 2),))
    proj_weight = scatter_about(key_of[8], (D, D), (D // 16) ** -0.5, 1.25, ((0, 2),))
    proj_bias = scatter_about(key_of[9], (D,), 0.3, 3.0, ((0, 2),))
    mlp_gain = jnp.clip(0.5 + 1.0 * jax.random.uniform(key_of[10], (D,), jnp.float32) ** steps_of(key_of[10], (D,), ((0, 2),), -0.2, 0.2), 0.5, 1.5).astype(jnp.bfloat16)
    mlp_shift = scatter_about(key_of[11], (D,), 0.3, 3.0, ((0, 2),))
    up_weight = scatter_about(key_of[12], (D, FF), D ** -0.5, 0.3125, ((0, 2),))
    up_bias = scatter_about(key_of[13], (FF,), 0.5, 4.0, ((0, 2),))
    down_weight = scatter_about(key_of[14], (FF, D), FF ** -0.5, 0.15625, ((0, 2),))
    down_bias = scatter_about(key_of[15], (D,), 0.3, 3.0, ((0, 2),))
    return dict(images=images, counts=counts, cotangent=cotangent, attn_gain=attn_gain, attn_shift=attn_shift, qkv_weight=qkv_weight, query_bias=query_bias, value_bias=value_bias, proj_weight=proj_weight, proj_bias=proj_bias, mlp_gain=mlp_gain, mlp_shift=mlp_shift, up_weight=up_weight, up_bias=up_bias, down_weight=down_weight, down_bias=down_bias)


@jax.custom_vjp
def low(v):
    return lax.optimization_barrier(v.astype(jnp.bfloat16)).astype(jnp.float32)

@jax.custom_vjp
def low_back(v):
    return v

def low_keep(v):
    return (low(v), None)

def low_pass(kept, grad):
    return (grad,)

def back_keep(v):
    return (v, None)

def back_low(kept, grad):
    return (low(grad),)
low.defvjp(low_keep, low_pass)
low_back.defvjp(back_keep, back_low)
HIGH = lax.Precision.HIGHEST

def layer_norm(values, gain, offset):
    center = lax.optimization_barrier(jnp.mean(values, axis=-1, keepdims=True))
    centered = values - center
    spread = lax.optimization_barrier(jnp.mean(centered * centered, axis=-1, keepdims=True))
    return centered * lax.rsqrt(spread + 1e-06) * gain + offset

def matmul(left_side, right_side):
    return jnp.dot(left_side, right_side, precision=HIGH, preferred_element_type=jnp.float32)

def forward(params, inputs):
    attn_gain, attn_shift, qkv_weight, query_bias, value_bias, proj_weight, proj_bias, mlp_gain, mlp_shift, up_weight, up_bias, down_weight, down_bias = params
    blocks, length, width = inputs.shape
    flat_rows = inputs.reshape(blocks * length, width)
    normed = low(layer_norm(flat_rows, attn_gain, attn_shift))
    mixed = matmul(normed, qkv_weight)
    query = low(low_back(mixed[:, :width] + query_bias)).reshape(blocks, length, HEADS, HEAD)
    keys = low(low_back(mixed[:, width:2 * width])).reshape(blocks, length, HEADS, HEAD)
    values = low(low_back(mixed[:, 2 * width:] + value_bias)).reshape(blocks, length, HEADS, HEAD)
    scores = low_back(jnp.einsum('bqhd,bkhd->bhqk', query, keys, precision=HIGH) * 0.125)
    peak = lax.optimization_barrier(jnp.max(scores, axis=-1, keepdims=True))
    expos = jnp.exp(scores - peak)
    probs = expos / lax.optimization_barrier(jnp.sum(expos, axis=-1, keepdims=True))
    context = jnp.einsum('bhqk,bkhd->bqhd', low(probs), values, precision=HIGH)
    context = low(low_back(context.reshape(blocks * length, width)))
    resid = flat_rows + low_back(matmul(context, proj_weight) + proj_bias)
    normed_two = low(layer_norm(resid, mlp_gain, mlp_shift))
    hidden = low_back(matmul(normed_two, up_weight) + up_bias)
    active = low(jax.nn.gelu(hidden, approximate=False))
    branch = low_back(matmul(active, down_weight) + down_bias)
    return (resid + branch).reshape(blocks, length, width)

def reference(images, counts, cotangent, attn_gain, attn_shift, qkv_weight, query_bias, value_bias, proj_weight, proj_bias, mlp_gain, mlp_shift, up_weight, up_bias, down_weight, down_bias):
    params = tuple((weight.astype(jnp.float32) for weight in (attn_gain, attn_shift, qkv_weight, query_bias, value_bias, proj_weight, proj_bias, mlp_gain, mlp_shift, up_weight, up_bias, down_weight, down_bias)))
    slot_ids = jnp.arange(IMG_CAP, dtype=jnp.int32)

    def step_block(totals, block):
        inputs, live_count, cot_block = block
        live = (slot_ids < live_count).astype(jnp.float32)[:, None, None]
        result, pull = jax.vjp(forward, params, inputs.astype(jnp.float32))
        grads, input_grad = pull(cot_block.astype(jnp.float32) * live)
        totals = jax.tree.map(jnp.add, totals, grads)
        return (totals, ((result * live).astype(jnp.bfloat16), input_grad))
    starts = tuple((jnp.zeros_like(weight) for weight in params))
    totals, (layer_out, images_grad) = lax.scan(step_block, starts, (images.reshape(DEVICES, IMG_CAP, SEQ, D), counts, cotangent.reshape(DEVICES, IMG_CAP, SEQ, D)))
    factor = 1.0 / math.sqrt(IMAGES * SEQ)
    scaled = tuple((total * factor for total in totals))
    return (layer_out.reshape(IMAGES, SEQ, D), images_grad.reshape(IMAGES, SEQ, D), scaled[0], scaled[1], scaled[2], scaled[3], scaled[4], scaled[5], scaled[6], scaled[7], scaled[8], scaled[9], scaled[10], scaled[11], scaled[12])
```

```python
import functools
import math

import jax
import jax.numpy as jnp
from jax import lax
from jax.experimental import pallas as pl
from jax.experimental.pallas import tpu as pltpu
from jax.sharding import PartitionSpec as P

HEADS = 6
HEAD = 64
PAIR = 2 * HEAD
EPS = 1e-06
AHEAD3 = 2
LAG3 = 1
AHEAD = 2
LAG = 1
F32 = jnp.float32
BF16 = jnp.bfloat16
INV_SQRT_2PI = 1.0 / math.sqrt(2.0 * math.pi)


def up_to(size, step):
    return -(-size // step) * step


def nn(a, b):
    return lax.dot_general(a, b, (((1,), (0,)), ((), ())), preferred_element_type=F32)


def nt(a, b):
    return lax.dot_general(a, b, (((1,), (1,)), ((), ())), preferred_element_type=F32)


def tn(a, b):
    return lax.dot_general(a, b, (((0,), (0,)), ((), ())), preferred_element_type=F32)


def normalize(rows):
    center = jnp.mean(rows, axis=-1, keepdims=True)
    centered = rows - center
    inv = lax.rsqrt(jnp.mean(centered * centered, axis=-1, keepdims=True) + EPS)
    return centered * inv, inv


def normalize_back(hat, inv, dhat):
    first = jnp.mean(dhat, axis=-1, keepdims=True)
    second = jnp.mean(dhat * hat, axis=-1, keepdims=True)
    return inv * (dhat - first - hat * second)


def column_sum(rows):
    return jnp.sum(rows, axis=0, keepdims=True)


def pair_masks(dtype):
    lane = lax.broadcasted_iota(jnp.int32, (1, PAIR), 1)
    low = jnp.where(lane < HEAD, 1.0, 0.0)
    return low.astype(dtype), (1.0 - low).astype(dtype)


def gelu_parts(hidden):
    cdf = 0.5 + 0.5 * lax.erf(hidden * math.sqrt(0.5))
    return hidden * cdf, cdf + hidden * jnp.exp(hidden * hidden * -0.5) * INV_SQRT_2PI


def join_halves(whole, mine, other, me):
    half = mine.shape[0]
    whole[pl.ds(pl.multiple_of(me * half, 16), half), :] = mine[...]
    whole[pl.ds(pl.multiple_of((1 - me) * half, 16), half), :] = other[...]


def once(shape):
    return pl.BlockSpec(shape, lambda i: (0,) * len(shape), pipeline_mode=pl.Buffered(1))


SCALARS = pl.BlockSpec(memory_space=pltpu.SMEM)
PARAMS = pltpu.CompilerParams(vmem_limit_bytes=56 * 2**20)


def attend_kernel(length, group, facts, x_ref, vec_ref, mine_ref, other_ref,
                  mixed_ref, probs_ref, context_ref, rows, qpad, weight):
    padded = rows.shape[0] // group
    width = rows.shape[1]

    @pl.when(pl.program_id(0) == 0)
    def _():
        rows[...] = jnp.zeros_like(rows)
        qpad[...] = jnp.zeros_like(qpad)
        join_halves(weight, mine_ref, other_ref, facts[1])

    for g in range(group):
        rows[g * padded : g * padded + length, :] = x_ref[g].astype(F32)
    hat, _ = normalize(rows[...])
    normed = (hat * vec_ref[0:1, :] + vec_ref[1:2, :]).astype(BF16)
    bias = jnp.concatenate([vec_ref[2:3, :], jnp.zeros((1, width), F32), vec_ref[3:4, :]], axis=1)
    mixed = (nn(normed, weight[...]) + bias).astype(BF16)
    mixed_ref[...] = mixed
    low, high = pair_masks(BF16)
    cut = length // 8 * 8
    live_key = lax.broadcasted_iota(jnp.int32, (padded - cut, 1), 0) < length - cut

    def scores_of(g, h):
        at = h // 2 * PAIR
        key = mixed[g * padded : (g + 1) * padded, width + at : width + at + PAIR] * (low if h % 2 == 0 else high)
        return nt(key, qpad[g, :, at : at + PAIR]) * 0.125

    def probs_of(g, h, scores):
        top = scores[:cut]
        rest = jnp.where(live_key, scores[cut:], -jnp.inf)
        peak = jnp.maximum(jnp.max(top, axis=0, keepdims=True), jnp.max(rest, axis=0, keepdims=True))
        top = jnp.exp(top - peak)
        rest = jnp.exp(rest - peak)
        scale = 1.0 / (column_sum(top) + column_sum(rest))
        probs = jnp.concatenate([top * scale, rest * scale], axis=0).astype(BF16)
        probs_ref[g, h] = probs
        return probs

    for g in range(group):
        qpad[g, :padded, :] = mixed[g * padded : (g + 1) * padded, :width]
    values_t = [mixed[g * padded : (g + 1) * padded, 2 * width :].T for g in range(group)]
    jobs = [(g, h) for g in range(group) for h in range(HEADS)]
    scores = {job: scores_of(*job) for job in jobs[:AHEAD]}
    outs, done = {}, {}
    for i, (g, h) in enumerate(jobs):
        if i + AHEAD < len(jobs):
            scores[jobs[i + AHEAD]] = scores_of(*jobs[i + AHEAD])
        done[g, h] = probs_of(g, h, scores.pop((g, h)))
        if i >= LAG:
            pg, ph = jobs[i - LAG]
            outs[pg, ph] = nn(values_t[pg][ph * HEAD : (ph + 1) * HEAD], done.pop((pg, ph)))
    for pg, ph in jobs[len(jobs) - LAG :]:
        outs[pg, ph] = nn(values_t[pg][ph * HEAD : (ph + 1) * HEAD], done.pop((pg, ph)))
    for g in range(group):
        context_t = jnp.concatenate([outs[g, h] for h in range(HEADS)], axis=0).astype(BF16)
        context_ref[g * padded : (g + 1) * padded, :] = context_t.T[:padded]


def attend(facts, images, vectors, mine, other, group):
    blocks, length, width = images.shape
    padded = up_to(length, 16)
    lanes = up_to(length, 128)
    return pl.pallas_call(
        functools.partial(attend_kernel, length, group),
        grid=(blocks // group,),
        in_specs=[
            SCALARS,
            pl.BlockSpec((group, length, width), lambda i: (i, 0, 0)),
            once(vectors.shape),
            once(mine.shape),
            once(other.shape),
        ],
        out_specs=[
            pl.BlockSpec((group * padded, 3 * width), lambda i: (i, 0)),
            pl.BlockSpec((group, HEADS, padded, lanes), lambda i: (i, 0, 0, 0)),
            pl.BlockSpec((group * padded, width), lambda i: (i, 0)),
        ],
        out_shape=[
            jax.ShapeDtypeStruct((blocks * padded, 3 * width), BF16),
            jax.ShapeDtypeStruct((blocks, HEADS, padded, lanes), BF16),
            jax.ShapeDtypeStruct((blocks * padded, width), BF16),
        ],
        scratch_shapes=[
            pltpu.VMEM((group * padded, width), F32),
            pltpu.VMEM((group, lanes, width), BF16),
            pltpu.VMEM((width, 3 * width), BF16),
        ],
        compiler_params=PARAMS,
        cost_estimate=pl.CostEstimate(flops=10**10, bytes_accessed=3 * 10**7, transcendentals=0),
        name="attend",
    )(facts, images, vectors, mine, other)


def feed_kernel(length, group, facts, x_ref, cot_ref, context_ref, vec_ref, up_bias_ref,
                proj_mine, proj_other, up_mine, up_other, down_mine, down_other,
                resid_ref, active_ref, dresid_ref, dcontext_ref, pack_ref,
                rows, cots, proj, up, down, up_g, down_g, proj_g, sums, up_sum):
    padded = rows.shape[0] // group
    width = rows.shape[1]
    hidden_size = up.shape[1]
    step = pl.program_id(0)

    @pl.when(step == 0)
    def _():
        for ref in (rows, cots, up_g, down_g, proj_g, sums, up_sum):
            ref[...] = jnp.zeros_like(ref)
        join_halves(proj, proj_mine, proj_other, facts[1])
        join_halves(up, up_mine, up_other, facts[1])
        join_halves(down, down_mine, down_other, facts[1])

    for g in range(group):
        live = jnp.where(step * group + g < facts[0], 1.0, 0.0)
        rows[g * padded : g * padded + length, :] = x_ref[g].astype(F32)
        cots[g * padded : g * padded + length, :] = cot_ref[g].astype(F32) * live
    context = context_ref[...]
    resid = rows[...] + nn(context, proj[...]) + vec_ref[4:5, :]
    resid_ref[...] = resid
    hat, inv = normalize(resid)
    gain = vec_ref[5:6, :]
    normed = (hat * gain + vec_ref[6:7, :]).astype(BF16)
    hidden = nn(normed, up[...]) + up_bias_ref[...]
    active, slope = gelu_parts(hidden)
    active = active.astype(BF16)
    active_ref[...] = active
    dout = cots[...]
    dout_low = dout.astype(BF16)
    dhidden = nt(dout_low, down[...]) * slope
    up_sum[0:1, :] += column_sum(dhidden)
    dhidden = dhidden.astype(BF16)
    dnormed = nt(dhidden, up[...])
    dresid = dout + normalize_back(hat, inv, dnormed * gain)
    dresid_ref[...] = dresid
    dresid_low = dresid.astype(BF16)
    dcontext_ref[...] = nt(dresid_low, proj[...]).astype(BF16)
    sums[0:1, :] += column_sum(dresid)
    sums[1:2, :] += column_sum(dnormed * hat)
    sums[2:3, :] += column_sum(dnormed)
    sums[3:4, :] += column_sum(dout)
    up_g[...] += tn(normed, dhidden)
    down_g[...] += tn(dout_low, active)
    proj_g[...] += tn(context, dresid_low)

    @pl.when(step == pl.num_programs(0) - 1)
    def _():
        half, part = width // 2, hidden_size // 4 * 3
        extra, third = hidden_size - part, width // 6
        for k in range(2):
            mine = slice(k * half, (k + 1) * half)
            pack_ref[k, :half, :part] = up_g[mine, :part].astype(BF16)
            for j in range(3):
                strip = slice(k * half + j * third, k * half + (j + 1) * third)
                pack_ref[k, half:, j * extra : (j + 1) * extra] = up_g[strip, part:].astype(BF16)
            own = hidden_size // 2
            cols = slice(k * own, (k + 1) * own)
            tall = half + third
            pack_ref[k, :, part : part + own] = down_g[:tall, cols].astype(BF16)
            split = width - tall
            for j in range(2):
                pack_ref[k, j * split : (j + 1) * split, part + own : part + own + width] = down_g[
                    tall:, k * own + j * width : k * own + (j + 1) * width
                ].astype(BF16)
            last = part + own + width
            pack_ref[k, :half, last:] = proj_g[mine, :].astype(BF16)
            totals = jnp.concatenate(
                [sums[0:4, :]]
                + [up_sum[0:1, j * width : (j + 1) * width] for j in range(hidden_size // width)]
                + [jnp.zeros((third - 4 - hidden_size // width, width), F32)],
                axis=0,
            )
            pack_ref[k, half:, last:] = totals.astype(BF16)


def feed(facts, images, cotangent, context, vectors, up_bias, weights, group):
    blocks, length, width = images.shape
    padded = up_to(length, 16)
    hidden = up_bias.shape[1]
    row = lambda cols: pl.BlockSpec((group * padded, cols), lambda i: (i, 0))
    image = pl.BlockSpec((group, length, width), lambda i: (i, 0, 0))
    pack = (2, width // 2 + width // 6, hidden // 4 * 3 + hidden // 2 + 2 * width)
    return pl.pallas_call(
        functools.partial(feed_kernel, length, group),
        grid=(blocks // group,),
        in_specs=[SCALARS, image, image, row(width), once(vectors.shape), once(up_bias.shape)]
        + [once(weight.shape) for weight in weights],
        out_specs=[row(width), row(hidden), row(width), row(width), once(pack)],
        out_shape=[
            jax.ShapeDtypeStruct((blocks * padded, width), F32),
            jax.ShapeDtypeStruct((blocks * padded, hidden), BF16),
            jax.ShapeDtypeStruct((blocks * padded, width), F32),
            jax.ShapeDtypeStruct((blocks * padded, width), BF16),
            jax.ShapeDtypeStruct(pack, BF16),
        ],
        scratch_shapes=[
            pltpu.VMEM((group * padded, width), F32),
            pltpu.VMEM((group * padded, width), F32),
            pltpu.VMEM((width, width), BF16),
            pltpu.VMEM((width, hidden), BF16),
            pltpu.VMEM((hidden, width), BF16),
            pltpu.VMEM((width, hidden), F32),
            pltpu.VMEM((width, hidden), F32),
            pltpu.VMEM((width, width), F32),
            pltpu.VMEM((8, width), F32),
            pltpu.VMEM((8, hidden), F32),
        ],
        compiler_params=PARAMS,
        cost_estimate=pl.CostEstimate(flops=3 * 10**10, bytes_accessed=5 * 10**7, transcendentals=0),
        name="feed",
    )(facts, images, cotangent, context, vectors, up_bias, *weights)


def attend_back_kernel(length, group, first, last, x_ref, mixed_ref, probs_ref, context_ref, dcontext_ref,
                       spread_ref, *refs):
    if first:
        (dmixed_ref, qkv_out, sums_out), refs = refs[:3], refs[3:]
    else:
        (qkv_in, sums_in, dmixed_ref, qkv_out, sums_out), refs = refs[:5], refs[5:]
    if last:
        pack_ref, refs = refs[0], refs[1:]
    rows, qpad, opad = refs
    padded = rows.shape[0] // group
    width = rows.shape[1]

    @pl.when(pl.program_id(0) == 0)
    def _():
        rows[...] = jnp.zeros_like(rows)
        qpad[...] = jnp.zeros_like(qpad)
        opad[...] = jnp.zeros_like(opad)
        qkv_out[...] = jnp.zeros_like(qkv_out) if first else qkv_in[...]
        sums_out[...] = jnp.zeros_like(sums_out) if first else sums_in[...]

    low, high = pair_masks(BF16)
    lane = lax.broadcasted_iota(jnp.int32, (1, PAIR), 1)
    keys_ts = []
    for g in range(group):
        rows[g * padded : g * padded + length, :] = x_ref[g].astype(F32)
        span = slice(g * padded, (g + 1) * padded)
        qpad[g, :padded, :] = mixed_ref[span, :width]
        dcontext = dcontext_ref[span, :]
        opad[g, :padded, :width] = dcontext
        delta = nn((dcontext.astype(F32) * context_ref[span, :].astype(F32)).astype(BF16), spread_ref[...])
        coarse = delta.astype(BF16).astype(F32)
        opad[g, :padded, width:] = jnp.where(lane < 8, coarse, delta - coarse).astype(BF16)
        keys_ts.append(mixed_ref[span, width : 2 * width].T)

    def dprobs_of(g, h):
        span = slice(g * padded, (g + 1) * padded)
        at = h // 2 * PAIR
        mask = low if h % 2 == 0 else high
        pick = jnp.where((lane == h) | (lane == h + 8), -1.0, 0.0).astype(BF16)
        value = mixed_ref[span, 2 * width + at : 2 * width + at + PAIR] * mask
        value = jnp.concatenate([value, jnp.broadcast_to(pick, value.shape)], axis=1)
        douter = jnp.concatenate([opad[g, :, at : at + PAIR], opad[g, :, width:]], axis=1)
        return nt(value, douter)

    def finish(g, h, dscores):
        at = h // 2 * PAIR
        mask = low if h % 2 == 0 else high
        return (
            nn(probs_ref[g, h], opad[g, :, at : at + PAIR] * mask),
            nn(dscores, qpad[g, :, at : at + PAIR] * mask),
            nn(keys_ts[g][h * HEAD : (h + 1) * HEAD], dscores),
        )

    jobs = [(g, h) for g in range(group) for h in range(HEADS)]
    dprobs = {job: dprobs_of(*job) for job in jobs[:AHEAD3]}
    done, outs = {}, {}
    for i, job in enumerate(jobs):
        if i + AHEAD3 < len(jobs):
            dprobs[jobs[i + AHEAD3]] = dprobs_of(*jobs[i + AHEAD3])
        done[job] = (probs_ref[job[0], job[1]].astype(F32) * dprobs.pop(job)).astype(BF16)
        if i >= LAG3:
            outs[jobs[i - LAG3]] = finish(*jobs[i - LAG3], done.pop(jobs[i - LAG3]))
    for job in jobs[len(jobs) - LAG3 :]:
        outs[job] = finish(*job, done.pop(job))
    for g in range(group):
        span = slice(g * padded, (g + 1) * padded)
        for pair in range(HEADS // 2):
            at = pair * PAIR
            one, two = outs[g, 2 * pair], outs[g, 2 * pair + 1]
            dmixed_ref[span, width + at : width + at + PAIR] = ((one[1] + two[1]) * 0.125).astype(BF16)
            dmixed_ref[span, 2 * width + at : 2 * width + at + PAIR] = (one[0] + two[0]).astype(BF16)
        dquery_t = jnp.concatenate([outs[g, h][2] for h in range(HEADS)], axis=0)
        dmixed_ref[span, :width] = (dquery_t * 0.125).astype(BF16).T[:padded]
    hat, _ = normalize(rows[...])
    dmixed = dmixed_ref[...]
    sums_out[0:1, :] += column_sum(dmixed.astype(F32))
    qkv_out[...] += tn(hat.astype(BF16), dmixed)

    if last:
        @pl.when(pl.program_id(0) == pl.num_programs(0) - 1)
        def _():
            half, third = width // 2, width // 6
            part = 7 * PAIR
            rest = 3 * width - part
            for k in range(2):
                pack_ref[k, :half, :part] = qkv_out[k * half : (k + 1) * half, :part].astype(BF16)
                for j in range(3):
                    strip = slice(k * half + j * third, k * half + (j + 1) * third)
                    pack_ref[k, half:, j * rest : (j + 1) * rest] = qkv_out[strip, part:].astype(BF16)
                totals = jnp.concatenate(
                    [sums_out[0:1, j * PAIR : (j + 1) * PAIR] for j in range(3 * width // PAIR)]
                    + [jnp.zeros((third - 3 * width // PAIR, PAIR), F32)],
                    axis=0,
                )
                pack_ref[k, half:, 3 * rest :] = totals.astype(BF16)


def attend_back(images, mixed, probs, context, dcontext, carried, start, stop, group):
    blocks, length, width = images.shape
    padded = up_to(length, 16)
    lanes = up_to(length, 128)
    first, last = carried is None, stop == blocks
    base = start // group
    row = lambda cols: pl.BlockSpec((group * padded, cols), lambda i: (base + i, 0))
    head_of = lax.broadcasted_iota(jnp.int32, (width, PAIR), 0) // HEAD
    column = lax.broadcasted_iota(jnp.int32, (width, PAIR), 1)
    spread = ((column == head_of) | (column == head_of + 8)).astype(BF16)
    totals = [
        jax.ShapeDtypeStruct((width, 3 * width), F32),
        jax.ShapeDtypeStruct((8, 3 * width), F32),
    ]
    pack = jax.ShapeDtypeStruct((2, width // 2 + width // 6, 7 * PAIR), BF16)
    return pl.pallas_call(
        functools.partial(attend_back_kernel, length, group, first, last),
        grid=((stop - start) // group,),
        in_specs=[
            pl.BlockSpec((group, length, width), lambda i: (base + i, 0, 0)),
            row(3 * width),
            pl.BlockSpec((group, HEADS, padded, lanes), lambda i: (base + i, 0, 0, 0)),
            row(width),
            row(width),
            once((width, PAIR)),
        ]
        + ([] if first else [once(total.shape) for total in totals]),
        out_specs=[pl.BlockSpec((group * padded, 3 * width), lambda i: (i, 0))]
        + [once(total.shape) for total in totals]
        + ([once(pack.shape)] if last else []),
        out_shape=[jax.ShapeDtypeStruct(((stop - start) * padded, 3 * width), BF16)]
        + totals
        + ([pack] if last else []),
        scratch_shapes=[
            pltpu.VMEM((group * padded, width), F32),
            pltpu.VMEM((group, lanes, width), BF16),
            pltpu.VMEM((group, lanes, width + PAIR), BF16),
        ],
        compiler_params=PARAMS,
        cost_estimate=pl.CostEstimate(
            flops=10**9 * (stop - start), bytes_accessed=2 * 10**6 * (stop - start), transcendentals=0
        ),
        name="attend_back",
    )(images, mixed, probs, context, dcontext, spread, *(() if first else carried))


def outputs_kernel(length, group, start, facts, x_ref, resid_ref, active_ref, dresid_ref, dmixed_ref, vec_ref,
                   down_mine, down_other, qkv_mine, qkv_other, out_ref, dx_ref, rows, down, qkv):
    padded = rows.shape[0] // group
    step = pl.program_id(0)

    @pl.when(step == 0)
    def _():
        rows[...] = jnp.zeros_like(rows)
        join_halves(down, down_mine, down_other, facts[1])
        join_halves(qkv, qkv_mine, qkv_other, facts[1])

    for g in range(group):
        rows[g * padded : g * padded + length, :] = x_ref[g].astype(F32)
    result = resid_ref[...] + nn(active_ref[...], down[...]) + vec_ref[7:8, :]
    dnormed = nt(dmixed_ref[...], qkv[...])
    hat, inv = normalize(rows[...])
    dx = dresid_ref[...] + normalize_back(hat, inv, dnormed * vec_ref[0:1, :])
    for g in range(group):
        live = jnp.where(start + step * group + g < facts[0], 1.0, 0.0)
        out_ref[g] = (result[g * padded : g * padded + length] * live).astype(BF16)
        dx_ref[g] = dx[g * padded : g * padded + length]


def outputs(facts, images, resid, active, dresid, dmixed, vectors, weights, start, stop, group):
    blocks, length, width = images.shape
    padded = up_to(length, 16)
    base = start // group
    hidden = active.shape[1]
    row = lambda cols: pl.BlockSpec((group * padded, cols), lambda i: (base + i, 0))
    image = pl.BlockSpec((group, length, width), lambda i: (i, 0, 0))
    return pl.pallas_call(
        functools.partial(outputs_kernel, length, group, start),
        grid=((stop - start) // group,),
        in_specs=[
            SCALARS,
            pl.BlockSpec((group, length, width), lambda i: (base + i, 0, 0)),
            row(width),
            row(hidden),
            row(width),
            pl.BlockSpec((group * padded, 3 * width), lambda i: (i, 0)),
            once(vectors.shape),
        ]
        + [once(weight.shape) for weight in weights],
        out_specs=[image, image],
        out_shape=[
            jax.ShapeDtypeStruct((stop - start, length, width), BF16),
            jax.ShapeDtypeStruct((stop - start, length, width), F32),
        ],
        scratch_shapes=[
            pltpu.VMEM((group * padded, width), F32),
            pltpu.VMEM((hidden, width), BF16),
            pltpu.VMEM((width, 3 * width), BF16),
        ],
        compiler_params=PARAMS,
        cost_estimate=pl.CostEstimate(
            flops=10**9 * (stop - start), bytes_accessed=2 * 10**6 * (stop - start), transcendentals=0
        ),
        name="outputs",
    )(facts, images, resid, active, dresid, dmixed, vectors, *weights)


def unpack_feed_kernel(factor, facts, pack_ref, up_ref, down_ref, proj_ref, vec_ref, up_bias_ref):
    half, hidden = up_ref.shape
    width = proj_ref.shape[1]
    part, third, own = hidden // 4 * 3, width // 6, hidden // 2
    extra, tall = hidden - part, half + third
    split = width - tall
    last = part + own + width
    whole = pack_ref[...].astype(F32) * factor
    up_ref[:, :part] = whole[:half, :part]
    for j in range(3):
        up_ref[j * third : (j + 1) * third, part:] = whole[half:, j * extra : (j + 1) * extra]
    down_ref[:, :tall] = whole[:, part : part + own].T
    for j in range(2):
        down_ref[j * width : (j + 1) * width, tall:] = whole[j * split : (j + 1) * split, part + own : last].T
    proj_ref[...] = whole[:half, last:]
    totals = whole[half : half + 8, last:]
    first = facts[1] == 0
    vec_ref[...] = jnp.where(first, totals[:, :half], totals[:, half:])
    pieces = [totals[4 + j : 5 + j, :] for j in range(hidden // width)]
    near, far = jnp.concatenate(pieces[:2], axis=1), jnp.concatenate(pieces[2:], axis=1)
    up_bias_ref[...] = jnp.where(first, near, far)


def unpack_feed(facts, pack, factor, half, hidden):
    width = 2 * half
    vmem = pl.BlockSpec(memory_space=pltpu.VMEM)
    return pl.pallas_call(
        functools.partial(unpack_feed_kernel, factor),
        in_specs=[SCALARS, vmem],
        out_specs=[vmem] * 5,
        out_shape=[
            jax.ShapeDtypeStruct((half, hidden), F32),
            jax.ShapeDtypeStruct((hidden // 2, width), F32),
            jax.ShapeDtypeStruct((half, width), F32),
            jax.ShapeDtypeStruct((8, half), F32),
            jax.ShapeDtypeStruct((1, hidden // 2), F32),
        ],
        compiler_params=PARAMS,
        name="unpack_feed",
    )(facts, pack)


def unpack_attend_kernel(factor, facts, pack_ref, weight_ref, columns_ref, qkv_ref, vec_ref):
    half, wide = qkv_ref.shape
    width = wide // 3
    third, part = width // 6, 7 * PAIR
    rest = wide - part
    whole = pack_ref[...].astype(F32) * factor
    lower = [whole[half:, j * rest : (j + 1) * rest] for j in range(3)]
    product = jnp.concatenate([whole[:half, :part], jnp.concatenate(lower, axis=0)], axis=1)
    totals = jnp.concatenate(
        [whole[half + j : half + j + 1, 3 * rest :] for j in range(wide // PAIR)], axis=1
    )
    qkv_ref[...] = product * columns_ref[:, 0:1] + totals * columns_ref[:, 1:2]
    weight = weight_ref[...].astype(F32)
    ones = jnp.ones((8, wide), F32)
    dot = functools.partial(
        lax.dot_general,
        dimension_numbers=(((1,), (1,)), ((), ())),
        precision=lax.Precision.HIGHEST,
        preferred_element_type=F32,
    )
    gain = dot(ones, weight * product)
    shift = dot(ones, weight * totals)
    first = facts[1] == 0
    query = jnp.where(first, totals[:, :half], totals[:, half:width])
    value = jnp.where(first, totals[:, 2 * width : 2 * width + half], totals[:, 2 * width + half :])
    vec_ref[...] = jnp.concatenate([gain[0:1], shift[0:1], query, value, jnp.zeros((4, half), F32)], axis=0)


def unpack_attend(facts, pack, weight, columns, factor):
    vmem = pl.BlockSpec(memory_space=pltpu.VMEM)
    half, wide = weight.shape
    return pl.pallas_call(
        functools.partial(unpack_attend_kernel, factor),
        in_specs=[SCALARS, vmem, vmem, vmem],
        out_specs=[vmem] * 2,
        out_shape=[
            jax.ShapeDtypeStruct((half, wide), F32),
            jax.ShapeDtypeStruct((8, half), F32),
        ],
        compiler_params=PARAMS,
        name="unpack_attend",
    )(facts, pack, weight, columns)


def swap(values):
    return lax.ppermute(values, "shard", [(0, 1), (1, 0)])


def partners(devices, stride, size, flip):
    pairs = []
    for position in range(devices):
        digit = position // stride % size
        pairs.append((position, position + ((digit ^ flip) - digit) * stride))
    return pairs


def tree_sum(terms):
    terms = [term.astype(F32) for term in terms]
    while len(terms) > 1:
        terms = [terms[k] + terms[k + 1] for k in range(0, len(terms), 2)]
    return terms[0].astype(BF16)


class Exchange:
    def __init__(self, pack, devices, direct_last):
        self.value = pack
        self.devices = devices
        self.sizes = []
        left = devices
        while left > 1:
            self.sizes.append(4 if left % 4 == 0 else 2)
            left //= self.sizes[-1]
        self.direct_last = direct_last

    def phases(self):
        me = lax.axis_index("shard")
        pack = self.value
        keep = lax.dynamic_index_in_dim(pack, me, 0, keepdims=False)
        got = yield [(lax.dynamic_index_in_dim(pack, 1 - me, 0, keepdims=False), None)]
        value = tree_sum([keep, got[0]])
        index = lax.axis_index("dp")
        stride = 1
        kept = []
        for order, size in enumerate(self.sizes):
            digit = index // stride % size
            pairs = [partners(self.devices, stride, size, flip) for flip in range(1, size)]
            if self.direct_last and order == len(self.sizes) - 1:
                got = yield [(value, pair) for pair in pairs]
                value = tree_sum([value] + got)
            else:
                rows, columns = value.shape
                chunks = value.reshape(size, rows // size, columns)
                mine = lax.dynamic_index_in_dim(chunks, digit, 0, keepdims=False)
                got = yield [
                    (lax.dynamic_index_in_dim(chunks, digit ^ flip, 0, keepdims=False), pairs[flip - 1])
                    for flip in range(1, size)
                ]
                value = tree_sum([mine] + got)
                kept.append((size, digit, pairs))
            stride *= size
        for size, digit, pairs in reversed(kept):
            got = yield [(value, pair) for pair in pairs]
            rows, columns = value.shape
            whole = jnp.zeros((size, rows, columns), BF16)
            for flip, piece in enumerate([value] + got):
                whole = lax.dynamic_update_index_in_dim(whole, piece, digit ^ flip, 0)
            value = whole.reshape(size * rows, columns)
        self.value = value


def send(items):
    return [swap(value) if pairs is None else lax.ppermute(value, "dp", pairs) for value, pairs in items]


def on_device(
    images,
    counts,
    cotangent,
    attn_gain,
    attn_shift,
    qkv_weight,
    query_bias,
    value_bias,
    proj_weight,
    proj_bias,
    mlp_gain,
    mlp_shift,
    up_weight,
    up_bias,
    down_weight,
    down_bias,
):
    blocks, length, width = images.shape
    half = attn_gain.shape[0]
    hidden = 2 * up_bias.shape[0]
    devices = lax.axis_size("dp")
    me = lax.axis_index("shard")
    facts = jnp.stack([counts[0], me.astype(jnp.int32)])
    small = jnp.concatenate(
        [attn_gain, attn_shift, query_bias, value_bias, proj_bias, mlp_gain, mlp_shift, down_bias, up_bias]
    )
    small_other = swap(small)
    qkv_other = swap(qkv_weight)
    pair = jnp.where(me == 0, jnp.stack([small, small_other]), jnp.stack([small_other, small])).astype(F32)
    vectors = pair[:, : 8 * half].reshape(2, 8, half).transpose(1, 0, 2).reshape(8, width)
    up_bias_row = pair[:, 8 * half :].reshape(1, hidden)
    proj_other, up_other, down_other = swap(proj_weight), swap(up_weight), swap(down_weight)

    mixed, probs, context = attend(facts, images, vectors, qkv_weight, qkv_other, 2)
    resid, active, dresid, dcontext, pack = feed(
        facts,
        images,
        cotangent,
        context,
        vectors,
        up_bias_row,
        (proj_weight, proj_other, up_weight, up_other, down_weight, down_other),
        4,
    )

    feed_sum = Exchange(pack, devices, False)
    transfer = feed_sum.phases()
    items = next(transfer)
    cuts = [0, 2, 8, 12, blocks]
    carried = None
    dmixed = []
    finished = False
    for start, stop in zip(cuts[:-1], cuts[1:]):
        got = None if finished else send(items)
        result = attend_back(images, mixed, probs, context, dcontext, carried, start, stop, 2)
        if got is not None:
            got, result = lax.optimization_barrier((got, result))
        carried = result[1:3]
        dmixed.append(result[0])
        if not finished:
            try:
                items = transfer.send(got)
            except StopIteration:
                finished = True
        if stop < blocks and not finished:
            items_values = [value for value, _ in items]
            items_values, carried = lax.optimization_barrier((items_values, carried))
            items = [(value, pairs) for value, (_, pairs) in zip(items_values, items)]
    attend_pack = result[3]
    while not finished:
        try:
            items = transfer.send(send(items))
        except StopIteration:
            finished = True

    attend_sum = Exchange(attend_pack, devices, True)
    transfer = attend_sum.phases()
    items = next(transfer)
    finished = False
    done = []
    for k, (start, stop) in enumerate(zip(cuts[:-1], cuts[1:])):
        done.append(
            outputs(
                facts, images, resid, active, dresid, dmixed[k], vectors,
                (down_weight, down_other, qkv_weight, qkv_other), start, stop, 2,
            )
        )
    while not finished:
        try:
            items = transfer.send(send(items))
        except StopIteration:
            finished = True
    layer_out = jnp.concatenate([piece[0] for piece in done], axis=0)
    images_grad = jnp.concatenate([piece[1] for piece in done], axis=0)

    factor = 1.0 / math.sqrt(blocks * length * devices * lax.axis_size("shard"))
    up_g, down_g, proj_g, feed_vec, up_bias_g = unpack_feed(facts, feed_sum.value, factor, half, hidden)
    columns = jnp.stack([attn_gain, attn_shift], axis=1).astype(F32)
    qkv_g, attend_vec = unpack_attend(facts, attend_sum.value, qkv_weight, columns, factor)
    return (
        layer_out,
        images_grad,
        attend_vec[0],
        attend_vec[1],
        qkv_g,
        attend_vec[2],
        attend_vec[3],
        proj_g,
        feed_vec[0],
        feed_vec[1],
        feed_vec[2],
        up_g,
        up_bias_g[0],
        down_g,
        feed_vec[3],
    )


def solution(mesh):
    placed = (
        P(("dp", "shard"), None, None),
        P(("dp", "shard")),
        P(("dp", "shard"), None, None),
        P("shard"),
        P("shard"),
        P("shard", None),
        P("shard"),
        P("shard"),
        P("shard", None),
        P("shard"),
        P("shard"),
        P("shard"),
        P("shard", None),
        P("shard"),
        P("shard", None),
        P("shard"),
    )
    return jax.shard_map(
        on_device,
        mesh=mesh,
        in_specs=placed,
        out_specs=(
            P(("dp", "shard"), None, None),
            P(("dp", "shard"), None, None),
            P("shard"),
            P("shard"),
            P("shard", None),
            P("shard"),
            P("shard"),
            P("shard", None),
            P("shard"),
            P("shard"),
            P("shard"),
            P("shard", None),
            P("shard"),
            P("shard", None),
            P("shard"),
        ),
        check_vma=False,
    )
```

```python
import functools
import math

import jax
import jax.numpy as jnp
from jax import lax
from jax.experimental import pallas as pl
from jax.experimental.pallas import tpu as pltpu
from jax.sharding import PartitionSpec as P

HEADS = 6
HEAD = 64
PAIR = 2 * HEAD
EPS = 1e-06
AHEAD3 = 2
LAG3 = 1
AHEAD = 2
LAG = 1
F32 = jnp.float32
BF16 = jnp.bfloat16
INV_SQRT_2PI = 1.0 / math.sqrt(2.0 * math.pi)


def up_to(size, step):
    return -(-size // step) * step


def nn(a, b):
    return lax.dot_general(a, b, (((1,), (0,)), ((), ())), preferred_element_type=F32)


def nt(a, b):
    return lax.dot_general(a, b, (((1,), (1,)), ((), ())), preferred_element_type=F32)


def tn(a, b):
    return lax.dot_general(a, b, (((0,), (0,)), ((), ())), preferred_element_type=F32)


def normalize(rows):
    center = jnp.mean(rows, axis=-1, keepdims=True)
    centered = rows - center
    inv = lax.rsqrt(jnp.mean(centered * centered, axis=-1, keepdims=True) + EPS)
    return centered * inv, inv


def normalize_back(hat, inv, dhat):
    first = jnp.mean(dhat, axis=-1, keepdims=True)
    second = jnp.mean(dhat * hat, axis=-1, keepdims=True)
    return inv * (dhat - first - hat * second)


def column_sum(rows):
    return jnp.sum(rows, axis=0, keepdims=True)


def pair_masks(dtype):
    lane = lax.broadcasted_iota(jnp.int32, (1, PAIR), 1)
    low = jnp.where(lane < HEAD, 1.0, 0.0)
    return low.astype(dtype), (1.0 - low).astype(dtype)


def gelu_parts(hidden):
    cdf = 0.5 + 0.5 * lax.erf(hidden * math.sqrt(0.5))
    return hidden * cdf, cdf + hidden * jnp.exp(hidden * hidden * -0.5) * INV_SQRT_2PI


def join_halves(whole, mine, other, me):
    half = mine.shape[0]
    whole[pl.ds(pl.multiple_of(me * half, 16), half), :] = mine[...]
    whole[pl.ds(pl.multiple_of((1 - me) * half, 16), half), :] = other[...]


def once(shape):
    return pl.BlockSpec(shape, lambda i: (0,) * len(shape), pipeline_mode=pl.Buffered(1))


SCALARS = pl.BlockSpec(memory_space=pltpu.SMEM)
PARAMS = pltpu.CompilerParams(vmem_limit_bytes=56 * 2**20)


VMEM_WHOLE = pl.BlockSpec(memory_space=pltpu.VMEM)


def pack_small_kernel(*refs):
    out = refs[-1]
    half = out.shape[1]
    out[...] = jnp.zeros_like(out)
    for k, ref in enumerate(refs[:8]):
        out[k : k + 1, :] = ref[...].astype(F32).reshape(1, half)
    long = refs[8][...].astype(F32)
    for k in range(long.shape[0] // half):
        out[8 + k : 9 + k, :] = long[k * half : (k + 1) * half].reshape(1, half)


def pack_small(vectors):
    half = vectors[0].shape[0]
    return pl.pallas_call(
        pack_small_kernel,
        in_specs=[VMEM_WHOLE] * 9,
        out_specs=VMEM_WHOLE,
        out_shape=jax.ShapeDtypeStruct((16, half), F32),
        name="pack_small",
    )(*vectors)


def join_small_kernel(facts, mine_ref, other_ref, vec_ref, up_bias_ref):
    first = facts[1] == 0
    mine, other = mine_ref[...], other_ref[...]
    near, far = jnp.where(first, mine, other), jnp.where(first, other, mine)
    vec_ref[...] = jnp.concatenate([near[:8], far[:8]], axis=1)
    count = up_bias_ref.shape[1] // mine.shape[1] // 2
    rows = [near[8 + k : 9 + k] for k in range(count)] + [far[8 + k : 9 + k] for k in range(count)]
    up_bias_ref[...] = jnp.concatenate(rows, axis=1)


def join_small(facts, mine, other, hidden):
    half = mine.shape[1]
    return pl.pallas_call(
        join_small_kernel,
        in_specs=[SCALARS, VMEM_WHOLE, VMEM_WHOLE],
        out_specs=[VMEM_WHOLE] * 2,
        out_shape=[
            jax.ShapeDtypeStruct((8, 2 * half), F32),
            jax.ShapeDtypeStruct((1, hidden), F32),
        ],
        name="join_small",
    )(facts, mine, other)


def attend_kernel(length, group, facts, x_ref, vec_ref, mine_ref, other_ref,
                  mixed_ref, probs_ref, context_ref, rows, qpad, weight):
    padded = rows.shape[0] // group
    width = rows.shape[1]

    @pl.when(pl.program_id(0) == 0)
    def _():
        rows[...] = jnp.zeros_like(rows)
        qpad[...] = jnp.zeros_like(qpad)
        join_halves(weight, mine_ref, other_ref, facts[1])

    for g in range(group):
        rows[g * padded : g * padded + length, :] = x_ref[g].astype(F32)
    hat, _ = normalize(rows[...])
    normed = (hat * vec_ref[0:1, :] + vec_ref[1:2, :]).astype(BF16)
    bias = jnp.concatenate([vec_ref[2:3, :], jnp.zeros((1, width), F32), vec_ref[3:4, :]], axis=1)
    mixed = (nn(normed, weight[...]) + bias).astype(BF16)
    mixed_ref[...] = mixed
    low, high = pair_masks(BF16)
    cut = length // 8 * 8
    live_key = lax.broadcasted_iota(jnp.int32, (padded - cut, 1), 0) < length - cut

    def scores_of(g, h):
        at = h // 2 * PAIR
        key = mixed[g * padded : (g + 1) * padded, width + at : width + at + PAIR] * (low if h % 2 == 0 else high)
        return nt(key, qpad[g, :, at : at + PAIR]) * 0.125

    def probs_of(g, h, scores):
        top = scores[:cut]
        rest = jnp.where(live_key, scores[cut:], -jnp.inf)
        peak = jnp.maximum(jnp.max(top, axis=0, keepdims=True), jnp.max(rest, axis=0, keepdims=True))
        top = jnp.exp(top - peak)
        rest = jnp.exp(rest - peak)
        scale = 1.0 / (column_sum(top) + column_sum(rest))
        probs = jnp.concatenate([top * scale, rest * scale], axis=0).astype(BF16)
        probs_ref[g, h] = probs
        return probs

    for g in range(group):
        qpad[g, :padded, :] = mixed[g * padded : (g + 1) * padded, :width]
    values_t = [mixed[g * padded : (g + 1) * padded, 2 * width :].T for g in range(group)]
    jobs = [(g, h) for g in range(group) for h in range(HEADS)]
    scores = {job: scores_of(*job) for job in jobs[:AHEAD]}
    outs, done = {}, {}
    for i, (g, h) in enumerate(jobs):
        if i + AHEAD < len(jobs):
            scores[jobs[i + AHEAD]] = scores_of(*jobs[i + AHEAD])
        done[g, h] = probs_of(g, h, scores.pop((g, h)))
        if i >= LAG:
            pg, ph = jobs[i - LAG]
            outs[pg, ph] = nn(values_t[pg][ph * HEAD : (ph + 1) * HEAD], done.pop((pg, ph)))
    for pg, ph in jobs[len(jobs) - LAG :]:
        outs[pg, ph] = nn(values_t[pg][ph * HEAD : (ph + 1) * HEAD], done.pop((pg, ph)))
    for g in range(group):
        context_t = jnp.concatenate([outs[g, h] for h in range(HEADS)], axis=0).astype(BF16)
        context_ref[g * padded : (g + 1) * padded, :] = context_t.T[:padded]


def attend(facts, images, vectors, mine, other, group):
    blocks, length, width = images.shape
    padded = up_to(length, 16)
    lanes = up_to(length, 128)
    return pl.pallas_call(
        functools.partial(attend_kernel, length, group),
        grid=(blocks // group,),
        in_specs=[
            SCALARS,
            pl.BlockSpec((group, length, width), lambda i: (i, 0, 0)),
            once(vectors.shape),
            once(mine.shape),
            once(other.shape),
        ],
        out_specs=[
            pl.BlockSpec((group * padded, 3 * width), lambda i: (i, 0)),
            pl.BlockSpec((group, HEADS, padded, lanes), lambda i: (i, 0, 0, 0)),
            pl.BlockSpec((group * padded, width), lambda i: (i, 0)),
        ],
        out_shape=[
            jax.ShapeDtypeStruct((blocks * padded, 3 * width), BF16),
            jax.ShapeDtypeStruct((blocks, HEADS, padded, lanes), BF16),
            jax.ShapeDtypeStruct((blocks * padded, width), BF16),
        ],
        scratch_shapes=[
            pltpu.VMEM((group * padded, width), F32),
            pltpu.VMEM((group, lanes, width), BF16),
            pltpu.VMEM((width, 3 * width), BF16),
        ],
        compiler_params=PARAMS,
        cost_estimate=pl.CostEstimate(flops=10**10, bytes_accessed=3 * 10**7, transcendentals=0),
        name="attend",
    )(facts, images, vectors, mine, other)


def feed_kernel(length, group, facts, x_ref, cot_ref, context_ref, vec_ref, up_bias_ref,
                proj_mine, proj_other, up_mine, up_other, down_mine, down_other,
                resid_ref, active_ref, dresid_ref, dcontext_ref, pack_ref,
                rows, cots, proj, up, down, up_g, down_g, proj_g, sums, up_sum):
    padded = rows.shape[0] // group
    width = rows.shape[1]
    hidden_size = up.shape[1]
    step = pl.program_id(0)

    @pl.when(step == 0)
    def _():
        for ref in (rows, cots, up_g, down_g, proj_g, sums, up_sum):
            ref[...] = jnp.zeros_like(ref)
        join_halves(proj, proj_mine, proj_other, facts[1])
        join_halves(up, up_mine, up_other, facts[1])
        join_halves(down, down_mine, down_other, facts[1])

    for g in range(group):
        live = jnp.where(step * group + g < facts[0], 1.0, 0.0)
        rows[g * padded : g * padded + length, :] = x_ref[g].astype(F32)
        cots[g * padded : g * padded + length, :] = cot_ref[g].astype(F32) * live
    context = context_ref[...]
    resid = rows[...] + nn(context, proj[...]) + vec_ref[4:5, :]
    resid_ref[...] = resid
    hat, inv = normalize(resid)
    gain = vec_ref[5:6, :]
    normed = (hat * gain + vec_ref[6:7, :]).astype(BF16)
    hidden = nn(normed, up[...]) + up_bias_ref[...]
    active, slope = gelu_parts(hidden)
    active = active.astype(BF16)
    active_ref[...] = active
    dout = cots[...]
    dout_low = dout.astype(BF16)
    dhidden = nt(dout_low, down[...]) * slope
    up_sum[0:1, :] += column_sum(dhidden)
    dhidden = dhidden.astype(BF16)
    dnormed = nt(dhidden, up[...])
    dresid = dout + normalize_back(hat, inv, dnormed * gain)
    dresid_ref[...] = dresid
    dresid_low = dresid.astype(BF16)
    dcontext_ref[...] = nt(dresid_low, proj[...]).astype(BF16)
    sums[0:1, :] += column_sum(dresid)
    sums[1:2, :] += column_sum(dnormed * hat)
    sums[2:3, :] += column_sum(dnormed)
    sums[3:4, :] += column_sum(dout)
    up_g[...] += tn(normed, dhidden)
    down_g[...] += tn(dout_low, active)
    proj_g[...] += tn(context, dresid_low)

    @pl.when(step == pl.num_programs(0) - 1)
    def _():
        half, part = width // 2, hidden_size // 4 * 3
        extra, third = hidden_size - part, width // 6
        for k in range(2):
            mine = slice(k * half, (k + 1) * half)
            pack_ref[k, :half, :part] = up_g[mine, :part].astype(BF16)
            for j in range(3):
                strip = slice(k * half + j * third, k * half + (j + 1) * third)
                pack_ref[k, half:, j * extra : (j + 1) * extra] = up_g[strip, part:].astype(BF16)
            own = hidden_size // 2
            cols = slice(k * own, (k + 1) * own)
            tall = half + third
            pack_ref[k, :, part : part + own] = down_g[:tall, cols].astype(BF16)
            split = width - tall
            for j in range(2):
                pack_ref[k, j * split : (j + 1) * split, part + own : part + own + width] = down_g[
                    tall:, k * own + j * width : k * own + (j + 1) * width
                ].astype(BF16)
            last = part + own + width
            pack_ref[k, :half, last:] = proj_g[mine, :].astype(BF16)
            totals = jnp.concatenate(
                [sums[0:4, :]]
                + [up_sum[0:1, j * width : (j + 1) * width] for j in range(hidden_size // width)]
                + [jnp.zeros((third - 4 - hidden_size // width, width), F32)],
                axis=0,
            )
            pack_ref[k, half:, last:] = totals.astype(BF16)


def feed(facts, images, cotangent, context, vectors, up_bias, weights, group):
    blocks, length, width = images.shape
    padded = up_to(length, 16)
    hidden = up_bias.shape[1]
    row = lambda cols: pl.BlockSpec((group * padded, cols), lambda i: (i, 0))
    image = pl.BlockSpec((group, length, width), lambda i: (i, 0, 0))
    pack = (2, width // 2 + width // 6, hidden // 4 * 3 + hidden // 2 + 2 * width)
    return pl.pallas_call(
        functools.partial(feed_kernel, length, group),
        grid=(blocks // group,),
        in_specs=[SCALARS, image, image, row(width), once(vectors.shape), once(up_bias.shape)]
        + [once(weight.shape) for weight in weights],
        out_specs=[row(width), row(hidden), row(width), row(width), once(pack)],
        out_shape=[
            jax.ShapeDtypeStruct((blocks * padded, width), F32),
            jax.ShapeDtypeStruct((blocks * padded, hidden), BF16),
            jax.ShapeDtypeStruct((blocks * padded, width), F32),
            jax.ShapeDtypeStruct((blocks * padded, width), BF16),
            jax.ShapeDtypeStruct(pack, BF16),
        ],
        scratch_shapes=[
            pltpu.VMEM((group * padded, width), F32),
            pltpu.VMEM((group * padded, width), F32),
            pltpu.VMEM((width, width), BF16),
            pltpu.VMEM((width, hidden), BF16),
            pltpu.VMEM((hidden, width), BF16),
            pltpu.VMEM((width, hidden), F32),
            pltpu.VMEM((width, hidden), F32),
            pltpu.VMEM((width, width), F32),
            pltpu.VMEM((8, width), F32),
            pltpu.VMEM((8, hidden), F32),
        ],
        compiler_params=PARAMS,
        cost_estimate=pl.CostEstimate(flops=3 * 10**10, bytes_accessed=5 * 10**7, transcendentals=0),
        name="feed",
    )(facts, images, cotangent, context, vectors, up_bias, *weights)


def attend_back_kernel(length, group, first, last, x_ref, mixed_ref, probs_ref, context_ref, dcontext_ref,
                       spread_ref, *refs):
    if first:
        (dmixed_ref, qkv_out, sums_out), refs = refs[:3], refs[3:]
    else:
        (qkv_in, sums_in, dmixed_ref, qkv_out, sums_out), refs = refs[:5], refs[5:]
    if last:
        pack_ref, refs = refs[0], refs[1:]
    rows, qpad, opad = refs
    padded = rows.shape[0] // group
    width = rows.shape[1]

    @pl.when(pl.program_id(0) == 0)
    def _():
        rows[...] = jnp.zeros_like(rows)
        qpad[...] = jnp.zeros_like(qpad)
        opad[...] = jnp.zeros_like(opad)
        qkv_out[...] = jnp.zeros_like(qkv_out) if first else qkv_in[...]
        sums_out[...] = jnp.zeros_like(sums_out) if first else sums_in[...]

    low, high = pair_masks(BF16)
    lane = lax.broadcasted_iota(jnp.int32, (1, PAIR), 1)
    keys_ts = []
    for g in range(group):
        rows[g * padded : g * padded + length, :] = x_ref[g].astype(F32)
        span = slice(g * padded, (g + 1) * padded)
        qpad[g, :padded, :] = mixed_ref[span, :width]
        dcontext = dcontext_ref[span, :]
        opad[g, :padded, :width] = dcontext
        delta = nn((dcontext.astype(F32) * context_ref[span, :].astype(F32)).astype(BF16), spread_ref[...])
        coarse = delta.astype(BF16).astype(F32)
        opad[g, :padded, width:] = jnp.where(lane < 8, coarse, delta - coarse).astype(BF16)
        keys_ts.append(mixed_ref[span, width : 2 * width].T)

    def dprobs_of(g, h):
        span = slice(g * padded, (g + 1) * padded)
        at = h // 2 * PAIR
        mask = low if h % 2 == 0 else high
        pick = jnp.where((lane == h) | (lane == h + 8), -1.0, 0.0).astype(BF16)
        value = mixed_ref[span, 2 * width + at : 2 * width + at + PAIR] * mask
        value = jnp.concatenate([value, jnp.broadcast_to(pick, value.shape)], axis=1)
        douter = jnp.concatenate([opad[g, :, at : at + PAIR], opad[g, :, width:]], axis=1)
        return nt(value, douter)

    def finish(g, h, dscores):
        at = h // 2 * PAIR
        mask = low if h % 2 == 0 else high
        return (
            nn(probs_ref[g, h], opad[g, :, at : at + PAIR] * mask),
            nn(dscores, qpad[g, :, at : at + PAIR] * mask),
            nn(keys_ts[g][h * HEAD : (h + 1) * HEAD], dscores),
        )

    jobs = [(g, h) for g in range(group) for h in range(HEADS)]
    dprobs = {job: dprobs_of(*job) for job in jobs[:AHEAD3]}
    done, outs = {}, {}
    for i, job in enumerate(jobs):
        if i + AHEAD3 < len(jobs):
            dprobs[jobs[i + AHEAD3]] = dprobs_of(*jobs[i + AHEAD3])
        done[job] = (probs_ref[job[0], job[1]].astype(F32) * dprobs.pop(job)).astype(BF16)
        if i >= LAG3:
            outs[jobs[i - LAG3]] = finish(*jobs[i - LAG3], done.pop(jobs[i - LAG3]))
    for job in jobs[len(jobs) - LAG3 :]:
        outs[job] = finish(*job, done.pop(job))
    for g in range(group):
        span = slice(g * padded, (g + 1) * padded)
        for pair in range(HEADS // 2):
            at = pair * PAIR
            one, two = outs[g, 2 * pair], outs[g, 2 * pair + 1]
            dmixed_ref[span, width + at : width + at + PAIR] = ((one[1] + two[1]) * 0.125).astype(BF16)
            dmixed_ref[span, 2 * width + at : 2 * width + at + PAIR] = (one[0] + two[0]).astype(BF16)
        dquery_t = jnp.concatenate([outs[g, h][2] for h in range(HEADS)], axis=0)
        dmixed_ref[span, :width] = (dquery_t * 0.125).astype(BF16).T[:padded]
    hat, _ = normalize(rows[...])
    dmixed = dmixed_ref[...]
    sums_out[0:1, :] += column_sum(dmixed.astype(F32))
    qkv_out[...] += tn(hat.astype(BF16), dmixed)

    if last:
        @pl.when(pl.program_id(0) == pl.num_programs(0) - 1)
        def _():
            half, third = width // 2, width // 6
            part = 7 * PAIR
            rest = 3 * width - part
            for k in range(2):
                pack_ref[k, :half, :part] = qkv_out[k * half : (k + 1) * half, :part].astype(BF16)
                for j in range(3):
                    strip = slice(k * half + j * third, k * half + (j + 1) * third)
                    pack_ref[k, half:, j * rest : (j + 1) * rest] = qkv_out[strip, part:].astype(BF16)
                totals = jnp.concatenate(
                    [sums_out[0:1, j * PAIR : (j + 1) * PAIR] for j in range(3 * width // PAIR)]
                    + [jnp.zeros((third - 3 * width // PAIR, PAIR), F32)],
                    axis=0,
                )
                pack_ref[k, half:, 3 * rest :] = totals.astype(BF16)


def head_columns(width):
    head_of = lax.broadcasted_iota(jnp.int32, (width, PAIR), 0) // HEAD
    column = lax.broadcasted_iota(jnp.int32, (width, PAIR), 1)
    return ((column == head_of) | (column == head_of + 8)).astype(BF16)


def attend_back(images, mixed, probs, context, dcontext, spread, carried, start, stop, group):
    blocks, length, width = images.shape
    padded = up_to(length, 16)
    lanes = up_to(length, 128)
    first, last = carried is None, stop == blocks
    base = start // group
    row = lambda cols: pl.BlockSpec((group * padded, cols), lambda i: (base + i, 0))
    totals = [
        jax.ShapeDtypeStruct((width, 3 * width), F32),
        jax.ShapeDtypeStruct((8, 3 * width), F32),
    ]
    pack = jax.ShapeDtypeStruct((2, width // 2 + width // 6, 7 * PAIR), BF16)
    return pl.pallas_call(
        functools.partial(attend_back_kernel, length, group, first, last),
        grid=((stop - start) // group,),
        in_specs=[
            pl.BlockSpec((group, length, width), lambda i: (base + i, 0, 0)),
            row(3 * width),
            pl.BlockSpec((group, HEADS, padded, lanes), lambda i: (base + i, 0, 0, 0)),
            row(width),
            row(width),
            once((width, PAIR)),
        ]
        + ([] if first else [once(total.shape) for total in totals]),
        out_specs=[pl.BlockSpec((group * padded, 3 * width), lambda i: (i, 0))]
        + [once(total.shape) for total in totals]
        + ([once(pack.shape)] if last else []),
        out_shape=[jax.ShapeDtypeStruct(((stop - start) * padded, 3 * width), BF16)]
        + totals
        + ([pack] if last else []),
        scratch_shapes=[
            pltpu.VMEM((group * padded, width), F32),
            pltpu.VMEM((group, lanes, width), BF16),
            pltpu.VMEM((group, lanes, width + PAIR), BF16),
        ],
        compiler_params=PARAMS,
        cost_estimate=pl.CostEstimate(
            flops=10**9 * (stop - start), bytes_accessed=2 * 10**6 * (stop - start), transcendentals=0
        ),
        name="attend_back",
    )(images, mixed, probs, context, dcontext, spread, *(() if first else carried))


def layer_out_kernel(length, group, facts, resid_ref, active_ref, vec_ref, down_mine, down_other, out_ref, down):
    padded = resid_ref.shape[0] // group
    step = pl.program_id(0)

    @pl.when(step == 0)
    def _():
        join_halves(down, down_mine, down_other, facts[1])

    result = resid_ref[...] + nn(active_ref[...], down[...]) + vec_ref[7:8, :]
    for g in range(group):
        live = jnp.where(step * group + g < facts[0], 1.0, 0.0)
        out_ref[g] = (result[g * padded : g * padded + length] * live).astype(BF16)


def layer_output(facts, images, resid, active, vectors, mine, other, group):
    blocks, length, width = images.shape
    padded = up_to(length, 16)
    hidden = active.shape[1]
    row = lambda cols: pl.BlockSpec((group * padded, cols), lambda i: (i, 0))
    return pl.pallas_call(
        functools.partial(layer_out_kernel, length, group),
        grid=(blocks // group,),
        in_specs=[SCALARS, row(width), row(hidden), once(vectors.shape), once(mine.shape), once(other.shape)],
        out_specs=pl.BlockSpec((group, length, width), lambda i: (i, 0, 0)),
        out_shape=jax.ShapeDtypeStruct((blocks, length, width), BF16),
        scratch_shapes=[pltpu.VMEM((hidden, width), BF16)],
        compiler_params=PARAMS,
        cost_estimate=pl.CostEstimate(flops=10**10, bytes_accessed=2 * 10**7, transcendentals=0),
        name="layer_output",
    )(facts, resid, active, vectors, mine, other)


def input_grad_kernel(length, group, facts, x_ref, dresid_ref, dmixed_ref, vec_ref, qkv_mine, qkv_other,
                      dx_ref, rows, qkv):
    padded = rows.shape[0] // group

    @pl.when(pl.program_id(0) == 0)
    def _():
        rows[...] = jnp.zeros_like(rows)
        join_halves(qkv, qkv_mine, qkv_other, facts[1])

    for g in range(group):
        rows[g * padded : g * padded + length, :] = x_ref[g].astype(F32)
    dnormed = nt(dmixed_ref[...], qkv[...])
    hat, inv = normalize(rows[...])
    dx = dresid_ref[...] + normalize_back(hat, inv, dnormed * vec_ref[0:1, :])
    for g in range(group):
        dx_ref[g] = dx[g * padded : g * padded + length]


def input_grad(facts, images, dresid, dmixed, vectors, mine, other, start, group):
    _, length, width = images.shape
    padded = up_to(length, 16)
    count = dmixed.shape[0] // padded
    base = start // group
    return pl.pallas_call(
        functools.partial(input_grad_kernel, length, group),
        grid=(count // group,),
        in_specs=[
            SCALARS,
            pl.BlockSpec((group, length, width), lambda i: (base + i, 0, 0)),
            pl.BlockSpec((group * padded, width), lambda i: (base + i, 0)),
            pl.BlockSpec((group * padded, 3 * width), lambda i: (i, 0)),
            once(vectors.shape),
            once(mine.shape),
            once(other.shape),
        ],
        out_specs=pl.BlockSpec((group, length, width), lambda i: (i, 0, 0)),
        out_shape=jax.ShapeDtypeStruct((count, length, width), F32),
        scratch_shapes=[
            pltpu.VMEM((group * padded, width), F32),
            pltpu.VMEM((width, 3 * width), BF16),
        ],
        compiler_params=PARAMS,
        cost_estimate=pl.CostEstimate(flops=10**9 * count, bytes_accessed=2 * 10**6 * count, transcendentals=0),
        name="input_grad",
    )(facts, images, dresid, dmixed, vectors, mine, other)


def unpack_feed_kernel(factor, facts, pack_ref, up_ref, down_ref, proj_ref, up_bias_ref, *vec_refs):
    half, hidden = up_ref.shape
    width = proj_ref.shape[1]
    part, third, own = hidden // 4 * 3, width // 6, hidden // 2
    extra, tall = hidden - part, half + third
    split = width - tall
    last = part + own + width
    whole = pack_ref[...].astype(F32) * factor
    up_ref[:, :part] = whole[:half, :part]
    for j in range(3):
        up_ref[j * third : (j + 1) * third, part:] = whole[half:, j * extra : (j + 1) * extra]
    down_ref[:, :tall] = whole[:, part : part + own].T
    for j in range(2):
        down_ref[j * width : (j + 1) * width, tall:] = whole[j * split : (j + 1) * split, part + own : last].T
    proj_ref[...] = whole[:half, last:]
    totals = whole[half : half + 8, last:]
    first = facts[1] == 0
    own_totals = jnp.where(first, totals[:, :half], totals[:, half:])
    for k, ref in enumerate(vec_refs):
        ref[...] = own_totals[k : k + 1, :].reshape(half)
    pieces = [totals[4 + j : 5 + j, :] for j in range(hidden // width)]
    near, far = jnp.concatenate(pieces[:2], axis=1), jnp.concatenate(pieces[2:], axis=1)
    up_bias_ref[...] = jnp.where(first, near, far).reshape(own)


def unpack_feed(facts, pack, factor, half, hidden):
    width = 2 * half
    return pl.pallas_call(
        functools.partial(unpack_feed_kernel, factor),
        in_specs=[SCALARS, VMEM_WHOLE],
        out_specs=[VMEM_WHOLE] * 8,
        out_shape=[
            jax.ShapeDtypeStruct((half, hidden), F32),
            jax.ShapeDtypeStruct((hidden // 2, width), F32),
            jax.ShapeDtypeStruct((half, width), F32),
            jax.ShapeDtypeStruct((hidden // 2,), F32),
        ]
        + [jax.ShapeDtypeStruct((half,), F32)] * 4,
        compiler_params=PARAMS,
        name="unpack_feed",
    )(facts, pack)


def unpack_attend_kernel(factor, facts, pack_ref, weight_ref, small_ref, qkv_ref, *vec_refs):
    half, wide = qkv_ref.shape
    width = wide // 3
    third, part = width // 6, 7 * PAIR
    rest = wide - part
    whole = pack_ref[...].astype(F32) * factor
    lower = [whole[half:, j * rest : (j + 1) * rest] for j in range(3)]
    product = jnp.concatenate([whole[:half, :part], jnp.concatenate(lower, axis=0)], axis=1)
    totals = jnp.concatenate(
        [whole[half + j : half + j + 1, 3 * rest :] for j in range(wide // PAIR)], axis=1
    )
    columns = small_ref[:8, :].T
    qkv_ref[...] = product * columns[:, 0:1] + totals * columns[:, 1:2]
    weight = weight_ref[...].astype(F32)
    ones = jnp.ones((8, wide), F32)
    dot = functools.partial(
        lax.dot_general,
        dimension_numbers=(((1,), (1,)), ((), ())),
        precision=lax.Precision.HIGHEST,
        preferred_element_type=F32,
    )
    gain = dot(ones, weight * product)
    shift = dot(ones, weight * totals)
    first = facts[1] == 0
    query = jnp.where(first, totals[:, :half], totals[:, half:width])
    value = jnp.where(first, totals[:, 2 * width : 2 * width + half], totals[:, 2 * width + half :])
    for ref, row in zip(vec_refs, (gain[0:1], shift[0:1], query, value)):
        ref[...] = row.reshape(half)


def unpack_attend(facts, pack, weight, small, factor):
    half, wide = weight.shape
    return pl.pallas_call(
        functools.partial(unpack_attend_kernel, factor),
        in_specs=[SCALARS] + [VMEM_WHOLE] * 3,
        out_specs=[VMEM_WHOLE] * 5,
        out_shape=[jax.ShapeDtypeStruct((half, wide), F32)] + [jax.ShapeDtypeStruct((half,), F32)] * 4,
        compiler_params=PARAMS,
        name="unpack_attend",
    )(facts, pack, weight, small)


def swap(values):
    return lax.ppermute(values, "shard", [(0, 1), (1, 0)])


def partners(devices, stride, size, flip):
    pairs = []
    for position in range(devices):
        digit = position // stride % size
        pairs.append((position, position + ((digit ^ flip) - digit) * stride))
    return pairs


def tree_sum(terms):
    terms = [term.astype(F32) for term in terms]
    while len(terms) > 1:
        terms = [terms[k] + terms[k + 1] for k in range(0, len(terms), 2)]
    return terms[0].astype(BF16)


def exchange(pack, devices, direct_last):
    sizes = []
    left = devices
    while left > 1:
        sizes.append(4 if left % 4 == 0 else 2)
        left //= sizes[-1]
    me = lax.axis_index("shard")
    keep = lax.dynamic_index_in_dim(pack, me, 0, keepdims=False)
    got = yield [(lax.dynamic_index_in_dim(pack, 1 - me, 0, keepdims=False), None)]
    value = tree_sum([keep, got[0]])
    index = lax.axis_index("dp")
    stride = 1
    kept = []
    for order, size in enumerate(sizes):
        digit = index // stride % size
        pairs = [partners(devices, stride, size, flip) for flip in range(1, size)]
        if direct_last and order == len(sizes) - 1:
            got = yield [(value, pair) for pair in pairs]
            value = tree_sum([value] + got)
        else:
            rows, columns = value.shape
            chunks = value.reshape(size, rows // size, columns)
            mine = lax.dynamic_index_in_dim(chunks, digit, 0, keepdims=False)
            got = yield [
                (lax.dynamic_index_in_dim(chunks, digit ^ flip, 0, keepdims=False), pairs[flip - 1])
                for flip in range(1, size)
            ]
            value = tree_sum([mine] + got)
            kept.append((size, digit, pairs))
        stride *= size
    for size, digit, pairs in reversed(kept):
        got = yield [(value, pair) for pair in pairs]
        rows, columns = value.shape
        whole = jnp.zeros((size, rows, columns), BF16)
        for flip, piece in enumerate([value] + got):
            whole = lax.dynamic_update_index_in_dim(whole, piece, digit ^ flip, 0)
        value = whole.reshape(size * rows, columns)
    return value


def beside(steps, items, works):
    results = []
    while True:
        work, token = works.pop(0) if works else (None, None)
        if work is not None:
            values, token = lax.optimization_barrier(([value for value, _ in items], token))
            items = [(value, pairs) for value, (_, pairs) in zip(values, items)]
        got = [swap(value) if pairs is None else lax.ppermute(value, "dp", pairs) for value, pairs in items]
        if work is not None:
            got, result = lax.optimization_barrier((got, work(token)))
            results.append(result)
        try:
            items = steps.send(got)
        except StopIteration as stop:
            return stop.value, results


def on_device(
    images,
    counts,
    cotangent,
    attn_gain,
    attn_shift,
    qkv_weight,
    query_bias,
    value_bias,
    proj_weight,
    proj_bias,
    mlp_gain,
    mlp_shift,
    up_weight,
    up_bias,
    down_weight,
    down_bias,
):
    blocks, length, width = images.shape
    half = attn_gain.shape[0]
    hidden = 2 * up_bias.shape[0]
    devices = lax.axis_size("dp")
    me = lax.axis_index("shard")
    facts = jnp.stack([counts[0], me.astype(jnp.int32)])
    qkv_other = swap(qkv_weight)
    small = pack_small(
        [attn_gain, attn_shift, query_bias, value_bias, proj_bias, mlp_gain, mlp_shift, down_bias, up_bias]
    )
    vectors, up_bias_row = join_small(facts, small, swap(small), hidden)
    proj_other, up_other, down_other = swap(proj_weight), swap(up_weight), swap(down_weight)

    mixed, probs, context = attend(facts, images, vectors, qkv_weight, qkv_other, 2)
    resid, active, dresid, dcontext, pack = feed(
        facts,
        images,
        cotangent,
        context,
        vectors,
        up_bias_row,
        (proj_weight, proj_other, up_weight, up_other, down_weight, down_other),
        4,
    )

    spread = head_columns(width)
    cuts = [0, 6, 10, blocks]
    state = {"carried": None, "dmixed": []}

    def write_layer(token):
        rows = layer_output(token, images, resid, active, vectors, down_weight, down_other, 4)
        return jnp.transpose(rows, (1, 0, 2))

    def back(start, stop):
        def work(token):
            results = attend_back(
                images, mixed, probs, context, dcontext, token, state["carried"], start, stop, 2
            )
            state["carried"] = results[1:3]
            return results

        return work

    steps = exchange(pack, devices, False)
    works = [(None, None), (write_layer, facts)]
    works += [(back(start, stop), spread) for start, stop in zip(cuts[:-1], cuts[1:])]
    feed_total, results = beside(steps, next(steps), works)
    layer_out = jnp.transpose(results[0], (1, 0, 2))
    attend_pack = results[-1][3]
    dmixed = [result[0] for result in results[1:]]

    factor = 1.0 / math.sqrt(blocks * length * devices * lax.axis_size("shard"))

    def spread_feed(token):
        return unpack_feed(token, feed_total, factor, half, hidden)

    def first_grads(token):
        return [
            input_grad(token, images, dresid, dmixed[k], vectors, qkv_weight, qkv_other, cuts[k], 2) for k in (0, 1)
        ]

    def last_grads(token):
        return input_grad(token, images, dresid, dmixed[2], vectors, qkv_weight, qkv_other, cuts[2], 2)

    steps = exchange(attend_pack, devices, True)
    works = [(spread_feed, facts), (first_grads, facts), (last_grads, facts)]
    attend_total, results = beside(steps, next(steps), works)
    up_g, down_g, proj_g, up_bias_g, proj_bias_g, mlp_gain_g, mlp_shift_g, down_bias_g = results[0]
    images_grad = jnp.concatenate(list(results[1]) + [results[2]], axis=0)
    qkv_g, attn_gain_g, attn_shift_g, query_bias_g, value_bias_g = unpack_attend(
        facts, attend_total, qkv_weight, small, factor
    )
    return (
        layer_out,
        images_grad,
        attn_gain_g,
        attn_shift_g,
        qkv_g,
        query_bias_g,
        value_bias_g,
        proj_g,
        proj_bias_g,
        mlp_gain_g,
        mlp_shift_g,
        up_g,
        up_bias_g,
        down_g,
        down_bias_g,
    )


def solution(mesh):
    placed = (
        P(("dp", "shard"), None, None),
        P(("dp", "shard")),
        P(("dp", "shard"), None, None),
        P("shard"),
        P("shard"),
        P("shard", None),
        P("shard"),
        P("shard"),
        P("shard", None),
        P("shard"),
        P("shard"),
        P("shard"),
        P("shard", None),
        P("shard"),
        P("shard", None),
        P("shard"),
    )
    return jax.shard_map(
        on_device,
        mesh=mesh,
        in_specs=placed,
        out_specs=(
            P(("dp", "shard"), None, None),
            P(("dp", "shard"), None, None),
            P("shard"),
            P("shard"),
            P("shard", None),
            P("shard"),
            P("shard"),
            P("shard", None),
            P("shard"),
            P("shard"),
            P("shard"),
            P("shard", None),
            P("shard"),
            P("shard", None),
            P("shard"),
        ),
        check_vma=False,
    )
```

```python
import functools
import math

import jax
import jax.numpy as jnp
from jax import lax
from jax.experimental import pallas as pl
from jax.experimental.pallas import tpu as pltpu
from jax.sharding import PartitionSpec as P

HEADS = 6
HEAD = 64
PAIR = 2 * HEAD
EPS = 1e-06
CHUNK = 256
DEPTH = 256
AHEAD3 = 3
LAG3 = 2
AHEAD = 3
LAG = 2
F32 = jnp.float32
BF16 = jnp.bfloat16
INV_SQRT_2PI = 1.0 / math.sqrt(2.0 * math.pi)


def up_to(size, step):
    return -(-size // step) * step


def nn(a, b):
    return lax.dot_general(a, b, (((1,), (0,)), ((), ())), preferred_element_type=F32)


def nt(a, b):
    return lax.dot_general(a, b, (((1,), (1,)), ((), ())), preferred_element_type=F32)


def tn(a, b):
    return lax.dot_general(a, b, (((0,), (0,)), ((), ())), preferred_element_type=F32)


def normalize(rows):
    center = jnp.mean(rows, axis=-1, keepdims=True)
    centered = rows - center
    inv = lax.rsqrt(jnp.mean(centered * centered, axis=-1, keepdims=True) + EPS)
    return centered * inv, inv


def normalize_back(hat, inv, dhat):
    first = jnp.mean(dhat, axis=-1, keepdims=True)
    second = jnp.mean(dhat * hat, axis=-1, keepdims=True)
    return inv * (dhat - first - hat * second)


def column_sum(rows):
    return jnp.sum(rows, axis=0, keepdims=True)


def pair_masks(dtype):
    lane = lax.broadcasted_iota(jnp.int32, (1, PAIR), 1)
    low = jnp.where(lane < HEAD, 1.0, 0.0)
    return low.astype(dtype), (1.0 - low).astype(dtype)


def gelu_parts(hidden):
    cdf = 0.5 + 0.5 * lax.erf(hidden * math.sqrt(0.5))
    return hidden * cdf, cdf + hidden * jnp.exp(hidden * hidden * -0.5) * INV_SQRT_2PI


def join_halves(whole, mine, other, me):
    half = mine.shape[0]
    whole[pl.ds(pl.multiple_of(me * half, 16), half), :] = mine[...]
    whole[pl.ds(pl.multiple_of((1 - me) * half, 16), half), :] = other[...]


def keep_rest(left, values, full):
    rest = values[0].shape[0] - full
    if rest:
        at = pl.ds(pl.multiple_of(pl.program_id(0) * rest, 16), rest)
        for ref, value in zip(left, values):
            ref[at, :] = value[full:]


def rest_space(blocks, rows, group, widths):
    rest = rows % DEPTH * (blocks // group)
    return [pltpu.VMEM((rest, width), BF16) for width in widths] if rest else []


def once(shape):
    return pl.BlockSpec(shape, lambda i: (0,) * len(shape), pipeline_mode=pl.Buffered(1))


SCALARS = pl.BlockSpec(memory_space=pltpu.SMEM)
PARAMS = pltpu.CompilerParams(vmem_limit_bytes=56 * 2**20)


VMEM_WHOLE = pl.BlockSpec(memory_space=pltpu.VMEM)


def pack_small_kernel(*refs):
    out = refs[-1]
    half = out.shape[1]
    out[...] = jnp.zeros_like(out)
    for k, ref in enumerate(refs[:8]):
        out[k : k + 1, :] = ref[...].astype(F32).reshape(1, half)
    long = refs[8][...].astype(F32)
    for k in range(long.shape[0] // half):
        out[8 + k : 9 + k, :] = long[k * half : (k + 1) * half].reshape(1, half)


def pack_small(vectors):
    half = vectors[0].shape[0]
    return pl.pallas_call(
        pack_small_kernel,
        in_specs=[VMEM_WHOLE] * 9,
        out_specs=VMEM_WHOLE,
        out_shape=jax.ShapeDtypeStruct((16, half), F32),
        name="pack_small",
    )(*vectors)


def join_small_kernel(facts, mine_ref, other_ref, vec_ref, up_bias_ref):
    first = facts[1] == 0
    mine, other = mine_ref[...], other_ref[...]
    near, far = jnp.where(first, mine, other), jnp.where(first, other, mine)
    vec_ref[...] = jnp.concatenate([near[:8], far[:8]], axis=1)
    count = up_bias_ref.shape[1] // mine.shape[1] // 2
    rows = [near[8 + k : 9 + k] for k in range(count)] + [far[8 + k : 9 + k] for k in range(count)]
    up_bias_ref[...] = jnp.concatenate(rows, axis=1)


def join_small(facts, mine, other, hidden):
    half = mine.shape[1]
    return pl.pallas_call(
        join_small_kernel,
        in_specs=[SCALARS, VMEM_WHOLE, VMEM_WHOLE],
        out_specs=[VMEM_WHOLE] * 2,
        out_shape=[
            jax.ShapeDtypeStruct((8, 2 * half), F32),
            jax.ShapeDtypeStruct((1, hidden), F32),
        ],
        name="join_small",
    )(facts, mine, other)


def attend_kernel(length, group, facts, x_ref, vec_ref, mine_ref, other_ref,
                  mixed_ref, probs_ref, context_ref, rows, qpad, weight):
    padded = rows.shape[0] // group
    width = rows.shape[1]

    @pl.when(pl.program_id(0) == 0)
    def _():
        rows[...] = jnp.zeros_like(rows)
        qpad[...] = jnp.zeros_like(qpad)
        join_halves(weight, mine_ref, other_ref, facts[1])

    for g in range(group):
        rows[g * padded : g * padded + length, :] = x_ref[g].astype(F32)
    hat, _ = normalize(rows[...])
    normed = (hat * vec_ref[0:1, :] + vec_ref[1:2, :]).astype(BF16)
    bias = jnp.concatenate([vec_ref[2:3, :], jnp.zeros((1, width), F32), vec_ref[3:4, :]], axis=1)
    mixed = (nn(normed, weight[...]) + bias).astype(BF16)
    mixed_ref[...] = mixed
    low, high = pair_masks(BF16)
    cut = length // 8 * 8
    live_key = lax.broadcasted_iota(jnp.int32, (padded - cut, 1), 0) < length - cut

    def scores_of(g, h):
        at = h // 2 * PAIR
        key = mixed[g * padded : (g + 1) * padded, width + at : width + at + PAIR] * (low if h % 2 == 0 else high)
        return nt(key, qpad[g, :, at : at + PAIR]) * 0.125

    def probs_of(g, h, scores):
        top = scores[:cut]
        rest = jnp.where(live_key, scores[cut:], -jnp.inf)
        peak = jnp.maximum(jnp.max(top, axis=0, keepdims=True), jnp.max(rest, axis=0, keepdims=True))
        top = jnp.exp(top - peak)
        rest = jnp.exp(rest - peak)
        scale = 1.0 / (column_sum(top) + column_sum(rest))
        probs = jnp.concatenate([top * scale, rest * scale], axis=0).astype(BF16)
        probs_ref[g, h] = probs
        return probs

    for g in range(group):
        qpad[g, :padded, :] = mixed[g * padded : (g + 1) * padded, :width]
    values_t = [mixed[g * padded : (g + 1) * padded, 2 * width :].T for g in range(group)]
    jobs = [(g, h) for g in range(group) for h in range(HEADS)]
    scores = {job: scores_of(*job) for job in jobs[:AHEAD]}
    outs, done = {}, {}
    for i, (g, h) in enumerate(jobs):
        if i + AHEAD < len(jobs):
            scores[jobs[i + AHEAD]] = scores_of(*jobs[i + AHEAD])
        done[g, h] = probs_of(g, h, scores.pop((g, h)))
        if i >= LAG:
            pg, ph = jobs[i - LAG]
            outs[pg, ph] = nn(values_t[pg][ph * HEAD : (ph + 1) * HEAD], done.pop((pg, ph)))
    for pg, ph in jobs[len(jobs) - LAG :]:
        outs[pg, ph] = nn(values_t[pg][ph * HEAD : (ph + 1) * HEAD], done.pop((pg, ph)))
    for g in range(group):
        context_t = jnp.concatenate([outs[g, h] for h in range(HEADS)], axis=0).astype(BF16)
        context_ref[g * padded : (g + 1) * padded, :] = context_t.T[:padded]


def attend(facts, images, vectors, mine, other, group):
    blocks, length, width = images.shape
    padded = up_to(length, 16)
    lanes = up_to(length, 128)
    return pl.pallas_call(
        functools.partial(attend_kernel, length, group),
        grid=(blocks // group,),
        in_specs=[
            SCALARS,
            pl.BlockSpec((group, length, width), lambda i: (i, 0, 0)),
            once(vectors.shape),
            once(mine.shape),
            once(other.shape),
        ],
        out_specs=[
            pl.BlockSpec((group * padded, 3 * width), lambda i: (i, 0)),
            pl.BlockSpec((group, HEADS, padded, lanes), lambda i: (i, 0, 0, 0)),
            pl.BlockSpec((group * padded, width), lambda i: (i, 0)),
        ],
        out_shape=[
            jax.ShapeDtypeStruct((blocks * padded, 3 * width), BF16),
            jax.ShapeDtypeStruct((blocks, HEADS, padded, lanes), BF16),
            jax.ShapeDtypeStruct((blocks * padded, width), BF16),
        ],
        scratch_shapes=[
            pltpu.VMEM((group * padded, width), F32),
            pltpu.VMEM((group, lanes, width), BF16),
            pltpu.VMEM((width, 3 * width), BF16),
        ],
        compiler_params=PARAMS,
        cost_estimate=pl.CostEstimate(flops=10**10, bytes_accessed=3 * 10**7, transcendentals=0),
        name="attend",
    )(facts, images, vectors, mine, other)


def feed_kernel(length, group, facts, x_ref, cot_ref, context_ref, vec_ref, up_bias_ref,
                proj_mine, proj_other, up_mine, up_other, down_mine, down_other,
                resid_ref, active_ref, dresid_ref, dcontext_ref, keep_ref, send_ref,
                rows, cots, proj, up, down, up_g, down_g, proj_g, sums, up_sum, *left):
    padded = rows.shape[0] // group
    width = rows.shape[1]
    hidden_size = up.shape[1]
    step = pl.program_id(0)

    @pl.when(step == 0)
    def _():
        for ref in (rows, cots, up_g, down_g, proj_g, sums, up_sum):
            ref[...] = jnp.zeros_like(ref)
        join_halves(proj, proj_mine, proj_other, facts[1])
        join_halves(up, up_mine, up_other, facts[1])
        join_halves(down, down_mine, down_other, facts[1])

    for g in range(group):
        live = jnp.where(step * group + g < facts[0], 1.0, 0.0)
        rows[g * padded : g * padded + length, :] = x_ref[g].astype(F32)
        cots[g * padded : g * padded + length, :] = cot_ref[g].astype(F32) * live
    context = context_ref[...]
    resid = rows[...] + nn(context, proj[...]) + vec_ref[4:5, :]
    resid_ref[...] = resid
    hat, inv = normalize(resid)
    gain = vec_ref[5:6, :]
    normed = (hat * gain + vec_ref[6:7, :]).astype(BF16)
    dout = cots[...]
    dout_low = dout.astype(BF16)
    actives, dhiddens = [], []
    for at in range(0, hidden_size, CHUNK):
        cols = slice(at, at + CHUNK)
        hidden = nn(normed, up[:, cols]) + up_bias_ref[:, cols]
        active, slope = gelu_parts(hidden)
        actives.append(active.astype(BF16))
        active_ref[:, cols] = actives[-1]
        dhidden = nt(dout_low, down[cols, :]) * slope
        up_sum[0:1, cols] += column_sum(dhidden)
        dhiddens.append(dhidden.astype(BF16))
    active = jnp.concatenate(actives, axis=1)
    dhidden = jnp.concatenate(dhiddens, axis=1)
    dnormed = nt(dhidden, up[...])
    dresid = dout + normalize_back(hat, inv, dnormed * gain)
    dresid_ref[...] = dresid
    dresid_low = dresid.astype(BF16)
    dcontext_ref[...] = nt(dresid_low, proj[...]).astype(BF16)
    sums[0:1, :] += column_sum(dresid)
    sums[1:2, :] += column_sum(dnormed * hat)
    sums[2:3, :] += column_sum(dnormed)
    sums[3:4, :] += column_sum(dout)
    full = normed.shape[0] // DEPTH * DEPTH
    up_g[...] += tn(normed[:full], dhidden[:full])
    down_g[...] += tn(dout_low[:full], active[:full])
    proj_g[...] += tn(context[:full], dresid_low[:full])
    keep_rest(left, (normed, dhidden, dout_low, active, context, dresid_low), full)

    @pl.when(step == pl.num_programs(0) - 1)
    def _():
        if left:
            up_g[...] += tn(left[0][...], left[1][...])
            down_g[...] += tn(left[2][...], left[3][...])
            proj_g[...] += tn(left[4][...], left[5][...])
        half, part = width // 2, hidden_size // 4 * 3
        extra, third, own = hidden_size - part, width // 6, hidden_size // 2
        tall, last = half + third, part + own + width
        split = width - tall

        def put(k, ref):
            mine = slice(k * half, (k + 1) * half)
            ref[:half, :part] = up_g[mine, :part].astype(BF16)
            for j in range(3):
                strip = slice(k * half + j * third, k * half + (j + 1) * third)
                ref[half:, j * extra : (j + 1) * extra] = up_g[strip, part:].astype(BF16)
            ref[:, part : part + own] = down_g[:tall, k * own : (k + 1) * own].astype(BF16)
            for j in range(2):
                cols = slice(k * own + j * width, k * own + (j + 1) * width)
                ref[j * split : (j + 1) * split, part + own : last] = down_g[tall:, cols].astype(BF16)
            ref[:half, last:] = proj_g[mine, :].astype(BF16)
            totals = jnp.concatenate(
                [sums[0:4, :]]
                + [up_sum[0:1, j * width : (j + 1) * width] for j in range(hidden_size // width)]
                + [jnp.zeros((third - 4 - hidden_size // width, width), F32)],
                axis=0,
            )
            ref[half:, last:] = totals.astype(BF16)

        for k in range(2):
            @pl.when(facts[1] == k)
            def _(k=k):
                put(k, keep_ref)
                put(1 - k, send_ref)


def feed(facts, images, cotangent, context, vectors, up_bias, weights, group):
    blocks, length, width = images.shape
    padded = up_to(length, 16)
    hidden = up_bias.shape[1]
    row = lambda cols: pl.BlockSpec((group * padded, cols), lambda i: (i, 0))
    image = pl.BlockSpec((group, length, width), lambda i: (i, 0, 0))
    pack = (width // 2 + width // 6, hidden // 4 * 3 + hidden // 2 + 2 * width)
    return pl.pallas_call(
        functools.partial(feed_kernel, length, group),
        grid=(blocks // group,),
        in_specs=[SCALARS, image, image, row(width), once(vectors.shape), once(up_bias.shape)]
        + [once(weight.shape) for weight in weights],
        out_specs=[row(width), row(hidden), row(width), row(width), once(pack), once(pack)],
        out_shape=[
            jax.ShapeDtypeStruct((blocks * padded, width), F32),
            jax.ShapeDtypeStruct((blocks * padded, hidden), BF16),
            jax.ShapeDtypeStruct((blocks * padded, width), F32),
            jax.ShapeDtypeStruct((blocks * padded, width), BF16),
            jax.ShapeDtypeStruct(pack, BF16),
            jax.ShapeDtypeStruct(pack, BF16),
        ],
        scratch_shapes=[
            pltpu.VMEM((group * padded, width), F32),
            pltpu.VMEM((group * padded, width), F32),
            pltpu.VMEM((width, width), BF16),
            pltpu.VMEM((width, hidden), BF16),
            pltpu.VMEM((hidden, width), BF16),
            pltpu.VMEM((width, hidden), F32),
            pltpu.VMEM((width, hidden), F32),
            pltpu.VMEM((width, width), F32),
            pltpu.VMEM((8, width), F32),
            pltpu.VMEM((8, hidden), F32),
        ]
        + rest_space(blocks, group * padded, group, (width, hidden, width, hidden, width, width)),
        compiler_params=PARAMS,
        cost_estimate=pl.CostEstimate(flops=3 * 10**10, bytes_accessed=5 * 10**7, transcendentals=0),
        name="feed",
    )(facts, images, cotangent, context, vectors, up_bias, *weights)


def attend_back_kernel(length, group, facts, x_ref, mixed_ref, probs_ref, context_ref, dcontext_ref,
                       dmixed_ref, keep_ref, send_ref, rows, qpad, opad, spread, qkv_g, sums, *left):
    padded = rows.shape[0] // group
    width = rows.shape[1]

    @pl.when(pl.program_id(0) == 0)
    def _():
        for ref in (rows, qpad, opad, qkv_g, sums):
            ref[...] = jnp.zeros_like(ref)
        head_of = lax.broadcasted_iota(jnp.int32, spread.shape, 0) // HEAD
        column = lax.broadcasted_iota(jnp.int32, spread.shape, 1)
        spread[...] = jnp.where((column == head_of) | (column == head_of + 8), 1.0, 0.0).astype(BF16)

    low, high = pair_masks(BF16)
    lane = lax.broadcasted_iota(jnp.int32, (1, PAIR), 1)
    keys_ts = []
    for g in range(group):
        rows[g * padded : g * padded + length, :] = x_ref[g].astype(F32)
        span = slice(g * padded, (g + 1) * padded)
        qpad[g, :padded, :] = mixed_ref[span, :width]
        dcontext = dcontext_ref[span, :]
        opad[g, :padded, :width] = dcontext
        delta = nn((dcontext.astype(F32) * context_ref[span, :].astype(F32)).astype(BF16), spread[...])
        coarse = delta.astype(BF16).astype(F32)
        opad[g, :padded, width:] = jnp.where(lane < 8, coarse, delta - coarse).astype(BF16)
        keys_ts.append(mixed_ref[span, width : 2 * width].T)

    def dprobs_of(g, h):
        span = slice(g * padded, (g + 1) * padded)
        at = h // 2 * PAIR
        mask = low if h % 2 == 0 else high
        pick = jnp.where((lane == h) | (lane == h + 8), -1.0, 0.0).astype(BF16)
        value = mixed_ref[span, 2 * width + at : 2 * width + at + PAIR] * mask
        value = jnp.concatenate([value, jnp.broadcast_to(pick, value.shape)], axis=1)
        douter = jnp.concatenate([opad[g, :, at : at + PAIR], opad[g, :, width:]], axis=1)
        return nt(value, douter)

    def finish(g, h, dscores):
        at = h // 2 * PAIR
        mask = low if h % 2 == 0 else high
        return (
            nn(probs_ref[g, h], opad[g, :, at : at + PAIR] * mask),
            nn(dscores, qpad[g, :, at : at + PAIR] * mask),
            nn(keys_ts[g][h * HEAD : (h + 1) * HEAD], dscores),
        )

    jobs = [(g, h) for g in range(group) for h in range(HEADS)]
    dprobs = {job: dprobs_of(*job) for job in jobs[:AHEAD3]}
    done, outs = {}, {}
    for i, job in enumerate(jobs):
        if i + AHEAD3 < len(jobs):
            dprobs[jobs[i + AHEAD3]] = dprobs_of(*jobs[i + AHEAD3])
        done[job] = (probs_ref[job[0], job[1]].astype(F32) * dprobs.pop(job)).astype(BF16)
        if i >= LAG3:
            outs[jobs[i - LAG3]] = finish(*jobs[i - LAG3], done.pop(jobs[i - LAG3]))
    for job in jobs[len(jobs) - LAG3 :]:
        outs[job] = finish(*job, done.pop(job))
    for g in range(group):
        span = slice(g * padded, (g + 1) * padded)
        for pair in range(HEADS // 2):
            at = pair * PAIR
            one, two = outs[g, 2 * pair], outs[g, 2 * pair + 1]
            dmixed_ref[span, width + at : width + at + PAIR] = ((one[1] + two[1]) * 0.125).astype(BF16)
            dmixed_ref[span, 2 * width + at : 2 * width + at + PAIR] = (one[0] + two[0]).astype(BF16)
        dquery_t = jnp.concatenate([outs[g, h][2] for h in range(HEADS)], axis=0)
        dmixed_ref[span, :width] = (dquery_t * 0.125).astype(BF16).T[:padded]
    hat, _ = normalize(rows[...])
    dmixed = dmixed_ref[...]
    sums[0:1, :] += column_sum(dmixed.astype(F32))
    hat = hat.astype(BF16)
    full = hat.shape[0] // DEPTH * DEPTH
    qkv_g[...] += tn(hat[:full], dmixed[:full])
    keep_rest(left, (hat, dmixed), full)

    @pl.when(pl.program_id(0) == pl.num_programs(0) - 1)
    def _():
        if left:
            qkv_g[...] += tn(left[0][...], left[1][...])
        half, third = width // 2, width // 6
        part = 7 * PAIR
        rest = 3 * width - part

        def put(k, ref):
            ref[:half, :part] = qkv_g[k * half : (k + 1) * half, :part].astype(BF16)
            for j in range(3):
                strip = slice(k * half + j * third, k * half + (j + 1) * third)
                ref[half:, j * rest : (j + 1) * rest] = qkv_g[strip, part:].astype(BF16)
            totals = jnp.concatenate(
                [sums[0:1, j * PAIR : (j + 1) * PAIR] for j in range(3 * width // PAIR)]
                + [jnp.zeros((third - 3 * width // PAIR, PAIR), F32)],
                axis=0,
            )
            ref[half:, 3 * rest :] = totals.astype(BF16)

        for k in range(2):
            @pl.when(facts[1] == k)
            def _(k=k):
                put(k, keep_ref)
                put(1 - k, send_ref)


def attend_back(facts, images, mixed, probs, context, dcontext, group):
    blocks, length, width = images.shape
    padded = up_to(length, 16)
    lanes = up_to(length, 128)
    row = lambda cols: pl.BlockSpec((group * padded, cols), lambda i: (i, 0))
    pack = (width // 2 + width // 6, 7 * PAIR)
    return pl.pallas_call(
        functools.partial(attend_back_kernel, length, group),
        grid=(blocks // group,),
        in_specs=[
            SCALARS,
            pl.BlockSpec((group, length, width), lambda i: (i, 0, 0)),
            row(3 * width),
            pl.BlockSpec((group, HEADS, padded, lanes), lambda i: (i, 0, 0, 0)),
            row(width),
            row(width),
        ],
        out_specs=[row(3 * width), once(pack), once(pack)],
        out_shape=[
            jax.ShapeDtypeStruct((blocks * padded, 3 * width), BF16),
            jax.ShapeDtypeStruct(pack, BF16),
            jax.ShapeDtypeStruct(pack, BF16),
        ],
        scratch_shapes=[
            pltpu.VMEM((group * padded, width), F32),
            pltpu.VMEM((group, lanes, width), BF16),
            pltpu.VMEM((group, lanes, width + PAIR), BF16),
            pltpu.VMEM((width, PAIR), BF16),
            pltpu.VMEM((width, 3 * width), F32),
            pltpu.VMEM((8, 3 * width), F32),
        ]
        + rest_space(blocks, group * padded, group, (width, 3 * width)),
        compiler_params=PARAMS,
        cost_estimate=pl.CostEstimate(flops=2 * 10**10, bytes_accessed=3 * 10**7, transcendentals=0),
        name="attend_back",
    )(facts, images, mixed, probs, context, dcontext)


def layer_out_kernel(length, group, facts, resid_ref, active_ref, vec_ref, down_mine, down_other, out_ref, down):
    padded = resid_ref.shape[0] // group
    step = pl.program_id(0)

    @pl.when(step == 0)
    def _():
        join_halves(down, down_mine, down_other, facts[1])

    result = resid_ref[...] + nn(active_ref[...], down[...]) + vec_ref[7:8, :]
    for g in range(group):
        live = jnp.where(step * group + g < facts[0], 1.0, 0.0)
        out_ref[g] = (result[g * padded : g * padded + length] * live).astype(BF16)


def layer_output(facts, images, resid, active, vectors, mine, other, group):
    blocks, length, width = images.shape
    padded = up_to(length, 16)
    hidden = active.shape[1]
    row = lambda cols: pl.BlockSpec((group * padded, cols), lambda i: (i, 0))
    return pl.pallas_call(
        functools.partial(layer_out_kernel, length, group),
        grid=(blocks // group,),
        in_specs=[SCALARS, row(width), row(hidden), once(vectors.shape), once(mine.shape), once(other.shape)],
        out_specs=pl.BlockSpec((group, length, width), lambda i: (i, 0, 0)),
        out_shape=jax.ShapeDtypeStruct((blocks, length, width), BF16),
        scratch_shapes=[pltpu.VMEM((hidden, width), BF16)],
        compiler_params=PARAMS,
        cost_estimate=pl.CostEstimate(flops=10**10, bytes_accessed=2 * 10**7, transcendentals=0),
        name="layer_output",
    )(facts, resid, active, vectors, mine, other)


def input_grad_kernel(length, group, facts, x_ref, dresid_ref, dmixed_ref, vec_ref, qkv_mine, qkv_other,
                      dx_ref, rows, qkv):
    padded = rows.shape[0] // group

    @pl.when(pl.program_id(0) == 0)
    def _():
        rows[...] = jnp.zeros_like(rows)
        join_halves(qkv, qkv_mine, qkv_other, facts[1])

    for g in range(group):
        rows[g * padded : g * padded + length, :] = x_ref[g].astype(F32)
    dnormed = nt(dmixed_ref[...], qkv[...])
    hat, inv = normalize(rows[...])
    dx = dresid_ref[...] + normalize_back(hat, inv, dnormed * vec_ref[0:1, :])
    for g in range(group):
        dx_ref[g] = dx[g * padded : g * padded + length]


def input_grad(facts, images, dresid, dmixed, vectors, mine, other, start, count, group):
    _, length, width = images.shape
    padded = up_to(length, 16)
    base = start // group
    return pl.pallas_call(
        functools.partial(input_grad_kernel, length, group),
        grid=(count // group,),
        in_specs=[
            SCALARS,
            pl.BlockSpec((group, length, width), lambda i: (base + i, 0, 0)),
            pl.BlockSpec((group * padded, width), lambda i: (base + i, 0)),
            pl.BlockSpec((group * padded, 3 * width), lambda i: (base + i, 0)),
            once(vectors.shape),
            once(mine.shape),
            once(other.shape),
        ],
        out_specs=pl.BlockSpec((group, length, width), lambda i: (i, 0, 0)),
        out_shape=jax.ShapeDtypeStruct((count, length, width), F32),
        scratch_shapes=[
            pltpu.VMEM((group * padded, width), F32),
            pltpu.VMEM((width, 3 * width), BF16),
        ],
        compiler_params=PARAMS,
        cost_estimate=pl.CostEstimate(flops=10**9 * count, bytes_accessed=2 * 10**6 * count, transcendentals=0),
        name="input_grad",
    )(facts, images, dresid, dmixed, vectors, mine, other)


def unpack_feed_kernel(factor, facts, pack_ref, up_ref, down_ref, proj_ref, up_bias_ref, *vec_refs):
    half, hidden = up_ref.shape
    width = proj_ref.shape[1]
    part, third, own = hidden // 4 * 3, width // 6, hidden // 2
    extra, tall = hidden - part, half + third
    split = width - tall
    last = part + own + width
    whole = pack_ref[...].astype(F32) * factor
    up_ref[:, :part] = whole[:half, :part]
    for j in range(3):
        up_ref[j * third : (j + 1) * third, part:] = whole[half:, j * extra : (j + 1) * extra]
    down_ref[:, :tall] = whole[:, part : part + own].T
    for j in range(2):
        down_ref[j * width : (j + 1) * width, tall:] = whole[j * split : (j + 1) * split, part + own : last].T
    proj_ref[...] = whole[:half, last:]
    totals = whole[half : half + 8, last:]
    first = facts[1] == 0
    own_totals = jnp.where(first, totals[:, :half], totals[:, half:])
    for k, ref in enumerate(vec_refs):
        ref[...] = own_totals[k : k + 1, :].reshape(half)
    pieces = [totals[4 + j : 5 + j, :] for j in range(hidden // width)]
    near, far = jnp.concatenate(pieces[:2], axis=1), jnp.concatenate(pieces[2:], axis=1)
    up_bias_ref[...] = jnp.where(first, near, far).reshape(own)


def unpack_feed(facts, pack, factor, half, hidden):
    width = 2 * half
    return pl.pallas_call(
        functools.partial(unpack_feed_kernel, factor),
        in_specs=[SCALARS, VMEM_WHOLE],
        out_specs=[VMEM_WHOLE] * 8,
        out_shape=[
            jax.ShapeDtypeStruct((half, hidden), F32),
            jax.ShapeDtypeStruct((hidden // 2, width), F32),
            jax.ShapeDtypeStruct((half, width), F32),
            jax.ShapeDtypeStruct((hidden // 2,), F32),
        ]
        + [jax.ShapeDtypeStruct((half,), F32)] * 4,
        compiler_params=PARAMS,
        name="unpack_feed",
    )(facts, pack)


def unpack_attend_kernel(factor, facts, pack_ref, weight_ref, small_ref, qkv_ref, *vec_refs):
    half, wide = qkv_ref.shape
    width = wide // 3
    third, part = width // 6, 7 * PAIR
    rest = wide - part
    whole = pack_ref[...].astype(F32) * factor
    lower = [whole[half:, j * rest : (j + 1) * rest] for j in range(3)]
    product = jnp.concatenate([whole[:half, :part], jnp.concatenate(lower, axis=0)], axis=1)
    totals = jnp.concatenate(
        [whole[half + j : half + j + 1, 3 * rest :] for j in range(wide // PAIR)], axis=1
    )
    columns = small_ref[:8, :].T
    qkv_ref[...] = product * columns[:, 0:1] + totals * columns[:, 1:2]
    weight = weight_ref[...].astype(F32)
    ones = jnp.ones((8, wide), F32)
    dot = functools.partial(
        lax.dot_general,
        dimension_numbers=(((1,), (1,)), ((), ())),
        precision=lax.Precision.HIGHEST,
        preferred_element_type=F32,
    )
    gain = dot(ones, weight * product)
    shift = dot(ones, weight * totals)
    first = facts[1] == 0
    query = jnp.where(first, totals[:, :half], totals[:, half:width])
    value = jnp.where(first, totals[:, 2 * width : 2 * width + half], totals[:, 2 * width + half :])
    for ref, row in zip(vec_refs, (gain[0:1], shift[0:1], query, value)):
        ref[...] = row.reshape(half)


def unpack_attend(facts, pack, weight, small, factor):
    half, wide = weight.shape
    return pl.pallas_call(
        functools.partial(unpack_attend_kernel, factor),
        in_specs=[SCALARS] + [VMEM_WHOLE] * 3,
        out_specs=[VMEM_WHOLE] * 5,
        out_shape=[jax.ShapeDtypeStruct((half, wide), F32)] + [jax.ShapeDtypeStruct((half,), F32)] * 4,
        compiler_params=PARAMS,
        name="unpack_attend",
    )(facts, pack, weight, small)


def swap(values):
    return lax.ppermute(values, "shard", [(0, 1), (1, 0)])


def partners(devices, stride, size, flip):
    pairs = []
    for position in range(devices):
        digit = position // stride % size
        pairs.append((position, position + ((digit ^ flip) - digit) * stride))
    return pairs


def tree_sum(terms):
    terms = [term.astype(F32) for term in terms]
    while len(terms) > 1:
        terms = [terms[k] + terms[k + 1] for k in range(0, len(terms), 2)]
    return terms[0].astype(BF16)


def exchange(keep, pack, devices):
    sizes = []
    left = devices
    while left > 1:
        sizes.append(4 if left % 4 == 0 else 2)
        left //= sizes[-1]
    got = yield [(pack, None)]
    value = tree_sum([keep, got[0]])
    index = lax.axis_index("dp")
    stride = 1
    kept = []
    for order, size in enumerate(sizes):
        digit = index // stride % size
        pairs = [partners(devices, stride, size, flip) for flip in range(1, size)]
        if order == len(sizes) - 1:
            got = yield [(value, pair) for pair in pairs]
            value = tree_sum([value] + got)
        else:
            rows, columns = value.shape
            chunks = value.reshape(size, rows // size, columns)
            mine = lax.dynamic_index_in_dim(chunks, digit, 0, keepdims=False)
            got = yield [
                (lax.dynamic_index_in_dim(chunks, digit ^ flip, 0, keepdims=False), pairs[flip - 1])
                for flip in range(1, size)
            ]
            value = tree_sum([mine] + got)
            kept.append((size, digit, pairs))
        stride *= size
    for size, digit, pairs in reversed(kept):
        got = yield [(value, pair) for pair in pairs]
        rows, columns = value.shape
        whole = jnp.zeros((size, rows, columns), BF16)
        for flip, piece in enumerate([value] + got):
            whole = lax.dynamic_update_index_in_dim(whole, piece, digit ^ flip, 0)
        value = whole.reshape(size * rows, columns)
    return value


def transfer(items):
    return [swap(value) if pairs is None else lax.ppermute(value, "dp", pairs) for value, pairs in items]


def resume(steps, got):
    try:
        return steps.send(got), None
    except StopIteration as stop:
        return None, stop.value


def tie(items, token):
    values, token = lax.optimization_barrier(([value for value, _ in items], token))
    return [(value, pairs) for value, (_, pairs) in zip(values, items)], token


def phase(steps, items, work, token, under_way=()):
    items, token = tie(items, token)
    got, under_way, result = lax.optimization_barrier((transfer(items), under_way, work(token)))
    return (*resume(steps, got), result, under_way)


def finish(steps, items):
    total = None
    while items is not None:
        items, total = resume(steps, transfer(items))
    return total


def on_device(
    images,
    counts,
    cotangent,
    attn_gain,
    attn_shift,
    qkv_weight,
    query_bias,
    value_bias,
    proj_weight,
    proj_bias,
    mlp_gain,
    mlp_shift,
    up_weight,
    up_bias,
    down_weight,
    down_bias,
):
    blocks, length, width = images.shape
    half = attn_gain.shape[0]
    hidden = 2 * up_bias.shape[0]
    devices = lax.axis_size("dp")
    me = lax.axis_index("shard")
    facts = jnp.stack([counts[0], me.astype(jnp.int32)])
    qkv_other = swap(qkv_weight)
    small = pack_small(
        [attn_gain, attn_shift, query_bias, value_bias, proj_bias, mlp_gain, mlp_shift, down_bias, up_bias]
    )
    vectors, up_bias_row = join_small(facts, small, swap(small), hidden)
    proj_other, up_other, down_other = swap(proj_weight), swap(up_weight), swap(down_weight)

    mixed, probs, context = attend(facts, images, vectors, qkv_weight, qkv_other, 4)
    resid, active, dresid, dcontext, keep, pack = feed(
        facts,
        images,
        cotangent,
        context,
        vectors,
        up_bias_row,
        (proj_weight, proj_other, up_weight, up_other, down_weight, down_other),
        4,
    )

    def write_layer(token):
        rows = layer_output(token, images, resid, active, vectors, down_weight, down_other, 4)
        return jnp.transpose(rows, (1, 0, 2))

    def back(token):
        return attend_back(token, images, mixed, probs, context, dcontext, 4)

    feed_steps = exchange(keep, pack, devices)
    feed_items, _ = resume(feed_steps, transfer(next(feed_steps)))
    feed_items, _, written, _ = phase(feed_steps, feed_items, write_layer, facts)
    layer_out = jnp.transpose(written, (1, 0, 2))
    feed_items, _, (dmixed, keep, pack), _ = phase(feed_steps, feed_items, back, facts)

    factor = 1.0 / math.sqrt(blocks * length * devices * lax.axis_size("shard"))
    count = blocks // 2

    def grads(start):
        return lambda token: input_grad(
            token, images, dresid, dmixed, vectors, qkv_weight, qkv_other, start, count, 4
        )

    steps = exchange(keep, pack, devices)
    arriving = transfer(feed_items)
    items, _ = resume(steps, transfer(next(steps)))
    items, _, first_grads, arriving = phase(steps, items, grads(0), facts, arriving)
    feed_items, feed_total = resume(feed_steps, arriving)
    if feed_items is not None:
        feed_total = finish(feed_steps, feed_items)

    def late(token):
        return grads(count)(token), unpack_feed(token, feed_total, factor, half, hidden)

    items, _, (last_grads, unpacked), _ = phase(steps, items, late, facts)
    attend_total = finish(steps, items)
    up_g, down_g, proj_g, up_bias_g, proj_bias_g, mlp_gain_g, mlp_shift_g, down_bias_g = unpacked
    images_grad = jnp.concatenate([first_grads, last_grads], axis=0)
    qkv_g, attn_gain_g, attn_shift_g, query_bias_g, value_bias_g = unpack_attend(
        facts, attend_total, qkv_weight, small, factor
    )
    return (
        layer_out,
        images_grad,
        attn_gain_g,
        attn_shift_g,
        qkv_g,
        query_bias_g,
        value_bias_g,
        proj_g,
        proj_bias_g,
        mlp_gain_g,
        mlp_shift_g,
        up_g,
        up_bias_g,
        down_g,
        down_bias_g,
    )


def solution(mesh):
    placed = (
        P(("dp", "shard"), None, None),
        P(("dp", "shard")),
        P(("dp", "shard"), None, None),
        P("shard"),
        P("shard"),
        P("shard", None),
        P("shard"),
        P("shard"),
        P("shard", None),
        P("shard"),
        P("shard"),
        P("shard"),
        P("shard", None),
        P("shard"),
        P("shard", None),
        P("shard"),
    )
    return jax.shard_map(
        on_device,
        mesh=mesh,
        in_specs=placed,
        out_specs=(
            P(("dp", "shard"), None, None),
            P(("dp", "shard"), None, None),
            P("shard"),
            P("shard"),
            P("shard", None),
            P("shard"),
            P("shard"),
            P("shard", None),
            P("shard"),
            P("shard"),
            P("shard"),
            P("shard", None),
            P("shard"),
            P("shard", None),
            P("shard"),
        ),
        check_vma=False,
    )
```

```python
import functools
import math

import jax
import jax.numpy as jnp
from jax import lax
from jax.experimental import pallas as pl
from jax.experimental.pallas import tpu as pltpu
from jax.sharding import PartitionSpec as P

HEADS = 6
HEAD = 64
PAIR = 2 * HEAD
EPS = 1e-06
CHUNK = 256
DEPTH = 256
AHEAD3 = 3
LAG3 = 2
AHEAD = 3
LAG = 2
F32 = jnp.float32
BF16 = jnp.bfloat16
INV_SQRT_2PI = 1.0 / math.sqrt(2.0 * math.pi)


def up_to(size, step):
    return -(-size // step) * step


def nn(a, b):
    return lax.dot_general(a, b, (((1,), (0,)), ((), ())), preferred_element_type=F32)


def nt(a, b):
    return lax.dot_general(a, b, (((1,), (1,)), ((), ())), preferred_element_type=F32)


def tn(a, b):
    return lax.dot_general(a, b, (((0,), (0,)), ((), ())), preferred_element_type=F32)


def normalize(rows):
    center = jnp.mean(rows, axis=-1, keepdims=True)
    centered = rows - center
    inv = lax.rsqrt(jnp.mean(centered * centered, axis=-1, keepdims=True) + EPS)
    return centered * inv, inv


def normalize_back(hat, inv, dhat):
    first = jnp.mean(dhat, axis=-1, keepdims=True)
    second = jnp.mean(dhat * hat, axis=-1, keepdims=True)
    return inv * (dhat - first - hat * second)


def column_sum(rows):
    return jnp.sum(rows, axis=0, keepdims=True)


def pair_masks(dtype):
    lane = lax.broadcasted_iota(jnp.int32, (1, PAIR), 1)
    low = jnp.where(lane < HEAD, 1.0, 0.0)
    return low.astype(dtype), (1.0 - low).astype(dtype)


def gelu_parts(hidden):
    cdf = 0.5 + 0.5 * lax.erf(hidden * math.sqrt(0.5))
    return hidden * cdf, cdf + hidden * jnp.exp(hidden * hidden * -0.5) * INV_SQRT_2PI


def join_halves(whole, mine, other, me):
    half = mine.shape[0]
    whole[pl.ds(pl.multiple_of(me * half, 16), half), :] = mine[...]
    whole[pl.ds(pl.multiple_of((1 - me) * half, 16), half), :] = other[...]


def keep_rest(left, values, full):
    rest = values[0].shape[0] - full
    if rest:
        at = pl.ds(pl.multiple_of(pl.program_id(0) * rest, 16), rest)
        for ref, value in zip(left, values):
            ref[at, :] = value[full:]


def rest_space(blocks, rows, group, widths):
    rest = rows % DEPTH * (blocks // group)
    return [pltpu.VMEM((rest, width), BF16) for width in widths] if rest else []


def once(shape):
    return pl.BlockSpec(shape, lambda i: (0,) * len(shape), pipeline_mode=pl.Buffered(1))


SCALARS = pl.BlockSpec(memory_space=pltpu.SMEM)


def params(mebibytes):
    return pltpu.CompilerParams(vmem_limit_bytes=mebibytes * 2**20)


VMEM_WHOLE = pl.BlockSpec(memory_space=pltpu.VMEM)


def pack_small_kernel(*refs):
    out = refs[-1]
    half = out.shape[1]
    out[...] = jnp.zeros_like(out)
    for k, ref in enumerate(refs[:8]):
        out[k : k + 1, :] = ref[...].astype(F32).reshape(1, half)
    long = refs[8][...].astype(F32)
    for k in range(long.shape[0] // half):
        out[8 + k : 9 + k, :] = long[k * half : (k + 1) * half].reshape(1, half)


def pack_small(vectors):
    half = vectors[0].shape[0]
    return pl.pallas_call(
        pack_small_kernel,
        in_specs=[VMEM_WHOLE] * 9,
        out_specs=VMEM_WHOLE,
        out_shape=jax.ShapeDtypeStruct((16, half), F32),
        name="pack_small",
    )(*vectors)


def join_small(first, mine, other, vec_ref, up_bias_ref):
    near, far = jnp.where(first, mine, other), jnp.where(first, other, mine)
    vec_ref[...] = jnp.concatenate([near[:8], far[:8]], axis=1)
    count = up_bias_ref.shape[1] // mine.shape[1] // 2
    rows = [near[8 + k : 9 + k] for k in range(count)] + [far[8 + k : 9 + k] for k in range(count)]
    up_bias_ref[...] = jnp.concatenate(rows, axis=1)


def attend_kernel(length, group, facts, x_ref, small_mine, small_other, mine_ref, other_ref,
                  mixed_ref, probs_ref, context_ref, vec_ref, up_bias_ref, rows, qpad, weight):
    padded = rows.shape[0] // group
    width = rows.shape[1]

    @pl.when(pl.program_id(0) == 0)
    def _():
        rows[...] = jnp.zeros_like(rows)
        qpad[...] = jnp.zeros_like(qpad)
        join_halves(weight, mine_ref, other_ref, facts[1])
        join_small(facts[1] == 0, small_mine[...], small_other[...], vec_ref, up_bias_ref)

    for g in range(group):
        rows[g * padded : g * padded + length, :] = x_ref[g].astype(F32)
    hat, _ = normalize(rows[...])
    normed = (hat * vec_ref[0:1, :] + vec_ref[1:2, :]).astype(BF16)
    bias = jnp.concatenate([vec_ref[2:3, :], jnp.zeros((1, width), F32), vec_ref[3:4, :]], axis=1)
    mixed = (nn(normed, weight[...]) + bias).astype(BF16)
    mixed_ref[...] = mixed
    low, high = pair_masks(BF16)
    cut = length // 8 * 8
    live_key = lax.broadcasted_iota(jnp.int32, (padded - cut, 1), 0) < length - cut

    def scores_of(g, h):
        at = h // 2 * PAIR
        key = mixed[g * padded : (g + 1) * padded, width + at : width + at + PAIR] * (low if h % 2 == 0 else high)
        return nt(key, qpad[g, :, at : at + PAIR]) * 0.125

    def probs_of(g, h, scores):
        top = scores[:cut]
        rest = jnp.where(live_key, scores[cut:], -jnp.inf)
        peak = jnp.maximum(jnp.max(top, axis=0, keepdims=True), jnp.max(rest, axis=0, keepdims=True))
        top = jnp.exp(top - peak)
        rest = jnp.exp(rest - peak)
        scale = 1.0 / (column_sum(top) + column_sum(rest))
        probs = jnp.concatenate([top * scale, rest * scale], axis=0).astype(BF16)
        probs_ref[g, h] = probs
        return probs

    for g in range(group):
        qpad[g, :padded, :] = mixed[g * padded : (g + 1) * padded, :width]
    values_t = [mixed[g * padded : (g + 1) * padded, 2 * width :].T for g in range(group)]
    jobs = [(g, h) for g in range(group) for h in range(HEADS)]
    scores = {job: scores_of(*job) for job in jobs[:AHEAD]}
    outs, done = {}, {}
    for i, (g, h) in enumerate(jobs):
        if i + AHEAD < len(jobs):
            scores[jobs[i + AHEAD]] = scores_of(*jobs[i + AHEAD])
        done[g, h] = probs_of(g, h, scores.pop((g, h)))
        if i >= LAG:
            pg, ph = jobs[i - LAG]
            outs[pg, ph] = nn(values_t[pg][ph * HEAD : (ph + 1) * HEAD], done.pop((pg, ph)))
    for pg, ph in jobs[len(jobs) - LAG :]:
        outs[pg, ph] = nn(values_t[pg][ph * HEAD : (ph + 1) * HEAD], done.pop((pg, ph)))
    for g in range(group):
        context_t = jnp.concatenate([outs[g, h] for h in range(HEADS)], axis=0).astype(BF16)
        context_ref[g * padded : (g + 1) * padded, :] = context_t.T[:padded]


def attend(facts, images, small, small_other, mine, other, hidden, group):
    blocks, length, width = images.shape
    padded = up_to(length, 16)
    lanes = up_to(length, 128)
    return pl.pallas_call(
        functools.partial(attend_kernel, length, group),
        grid=(blocks // group,),
        in_specs=[
            SCALARS,
            pl.BlockSpec((group, length, width), lambda i: (i, 0, 0)),
            once(small.shape),
            once(small.shape),
            once(mine.shape),
            once(other.shape),
        ],
        out_specs=[
            pl.BlockSpec((group * padded, 3 * width), lambda i: (i, 0)),
            pl.BlockSpec((group, HEADS, padded, lanes), lambda i: (i, 0, 0, 0)),
            pl.BlockSpec((group * padded, width), lambda i: (i, 0)),
            once((8, width)),
            once((1, hidden)),
        ],
        out_shape=[
            jax.ShapeDtypeStruct((blocks * padded, 3 * width), BF16),
            jax.ShapeDtypeStruct((blocks, HEADS, padded, lanes), BF16),
            jax.ShapeDtypeStruct((blocks * padded, width), BF16),
            jax.ShapeDtypeStruct((8, width), F32),
            jax.ShapeDtypeStruct((1, hidden), F32),
        ],
        scratch_shapes=[
            pltpu.VMEM((group * padded, width), F32),
            pltpu.VMEM((group, lanes, width), BF16),
            pltpu.VMEM((width, 3 * width), BF16),
        ],
        compiler_params=params(56),
        cost_estimate=pl.CostEstimate(flops=10**10, bytes_accessed=3 * 10**7, transcendentals=0),
        name="attend",
    )(facts, images, small, small_other, mine, other)


def feed_kernel(length, group, facts, x_ref, cot_ref, context_ref, vec_ref, up_bias_ref,
                proj_mine, proj_other, up_mine, up_other, down_mine, down_other,
                resid_ref, active_ref, dresid_ref, dcontext_ref, keep_ref, send_ref,
                rows, cots, proj, up, down, up_g, down_g, proj_g, sums, up_sum, *left):
    padded = rows.shape[0] // group
    width = rows.shape[1]
    hidden_size = up.shape[1]
    step = pl.program_id(0)

    @pl.when(step == 0)
    def _():
        for ref in (rows, cots, up_g, down_g, proj_g, sums, up_sum):
            ref[...] = jnp.zeros_like(ref)
        join_halves(proj, proj_mine, proj_other, facts[1])
        join_halves(up, up_mine, up_other, facts[1])
        join_halves(down, down_mine, down_other, facts[1])

    for g in range(group):
        live = jnp.where(step * group + g < facts[0], 1.0, 0.0)
        rows[g * padded : g * padded + length, :] = x_ref[g].astype(F32)
        cots[g * padded : g * padded + length, :] = cot_ref[g].astype(F32) * live
    context = context_ref[...]
    resid = rows[...] + nn(context, proj[...]) + vec_ref[4:5, :]
    resid_ref[...] = resid
    hat, inv = normalize(resid)
    gain = vec_ref[5:6, :]
    normed = (hat * gain + vec_ref[6:7, :]).astype(BF16)
    dout = cots[...]
    dout_low = dout.astype(BF16)
    actives, dhiddens = [], []
    for at in range(0, hidden_size, CHUNK):
        cols = slice(at, at + CHUNK)
        hidden = nn(normed, up[:, cols]) + up_bias_ref[:, cols]
        active, slope = gelu_parts(hidden)
        actives.append(active.astype(BF16))
        active_ref[:, cols] = actives[-1]
        dhidden = nt(dout_low, down[cols, :]) * slope
        up_sum[0:1, cols] += column_sum(dhidden)
        dhiddens.append(dhidden.astype(BF16))
    active = jnp.concatenate(actives, axis=1)
    dhidden = jnp.concatenate(dhiddens, axis=1)
    dnormed = nt(dhidden, up[...])
    dresid = dout + normalize_back(hat, inv, dnormed * gain)
    dresid_ref[...] = dresid
    dresid_low = dresid.astype(BF16)
    dcontext_ref[...] = nt(dresid_low, proj[...]).astype(BF16)
    sums[0:1, :] += column_sum(dresid)
    sums[1:2, :] += column_sum(dnormed * hat)
    sums[2:3, :] += column_sum(dnormed)
    sums[3:4, :] += column_sum(dout)
    full = normed.shape[0] // DEPTH * DEPTH
    up_g[...] += tn(normed[:full], dhidden[:full])
    down_g[...] += tn(dout_low[:full], active[:full])
    proj_g[...] += tn(context[:full], dresid_low[:full])
    keep_rest(left, (normed, dhidden, dout_low, active, context, dresid_low), full)

    @pl.when(step == pl.num_programs(0) - 1)
    def _():
        if left:
            up_g[...] += tn(left[0][...], left[1][...])
            down_g[...] += tn(left[2][...], left[3][...])
            proj_g[...] += tn(left[4][...], left[5][...])
        half, part = width // 2, hidden_size // 4 * 3
        extra, third, own = hidden_size - part, width // 6, hidden_size // 2
        tall, last = half + third, part + own + width
        split = width - tall

        def put(k, ref):
            mine = slice(k * half, (k + 1) * half)
            ref[:half, :part] = up_g[mine, :part].astype(BF16)
            for j in range(3):
                strip = slice(k * half + j * third, k * half + (j + 1) * third)
                ref[half:, j * extra : (j + 1) * extra] = up_g[strip, part:].astype(BF16)
            ref[:, part : part + own] = down_g[:tall, k * own : (k + 1) * own].astype(BF16)
            for j in range(2):
                cols = slice(k * own + j * width, k * own + (j + 1) * width)
                ref[j * split : (j + 1) * split, part + own : last] = down_g[tall:, cols].astype(BF16)
            ref[:half, last:] = proj_g[mine, :].astype(BF16)
            totals = jnp.concatenate(
                [sums[0:4, :]]
                + [up_sum[0:1, j * width : (j + 1) * width] for j in range(hidden_size // width)]
                + [jnp.zeros((third - 4 - hidden_size // width, width), F32)],
                axis=0,
            )
            ref[half:, last:] = totals.astype(BF16)

        for k in range(2):
            @pl.when(facts[1] == k)
            def _(k=k):
                put(k, keep_ref)
                put(1 - k, send_ref)


def feed(facts, images, cotangent, context, vectors, up_bias, weights, group):
    blocks, length, width = images.shape
    padded = up_to(length, 16)
    hidden = up_bias.shape[1]
    row = lambda cols: pl.BlockSpec((group * padded, cols), lambda i: (i, 0))
    image = pl.BlockSpec((group, length, width), lambda i: (i, 0, 0))
    pack = (width // 2 + width // 6, hidden // 4 * 3 + hidden // 2 + 2 * width)
    return pl.pallas_call(
        functools.partial(feed_kernel, length, group),
        grid=(blocks // group,),
        in_specs=[SCALARS, image, image, row(width), once(vectors.shape), once(up_bias.shape)]
        + [once(weight.shape) for weight in weights],
        out_specs=[row(width), row(hidden), row(width), row(width), once(pack), once(pack)],
        out_shape=[
            jax.ShapeDtypeStruct((blocks * padded, width), F32),
            jax.ShapeDtypeStruct((blocks * padded, hidden), BF16),
            jax.ShapeDtypeStruct((blocks * padded, width), F32),
            jax.ShapeDtypeStruct((blocks * padded, width), BF16),
            jax.ShapeDtypeStruct(pack, BF16),
            jax.ShapeDtypeStruct(pack, BF16),
        ],
        scratch_shapes=[
            pltpu.VMEM((group * padded, width), F32),
            pltpu.VMEM((group * padded, width), F32),
            pltpu.VMEM((width, width), BF16),
            pltpu.VMEM((width, hidden), BF16),
            pltpu.VMEM((hidden, width), BF16),
            pltpu.VMEM((width, hidden), F32),
            pltpu.VMEM((width, hidden), F32),
            pltpu.VMEM((width, width), F32),
            pltpu.VMEM((8, width), F32),
            pltpu.VMEM((8, hidden), F32),
        ]
        + rest_space(blocks, group * padded, group, (width, hidden, width, hidden, width, width)),
        compiler_params=params(42),
        cost_estimate=pl.CostEstimate(flops=3 * 10**10, bytes_accessed=5 * 10**7, transcendentals=0),
        name="feed",
    )(facts, images, cotangent, context, vectors, up_bias, *weights)


def attend_back_kernel(length, group, facts, x_ref, mixed_ref, probs_ref, context_ref, dcontext_ref,
                       dmixed_ref, keep_ref, send_ref, rows, qpad, opad, turned, spread, qkv_g, sums, *left):
    padded = rows.shape[0] // group
    width = rows.shape[1]

    @pl.when(pl.program_id(0) == 0)
    def _():
        for ref in (rows, qpad, opad, turned, qkv_g, sums):
            ref[...] = jnp.zeros_like(ref)
        head_of = lax.broadcasted_iota(jnp.int32, spread.shape, 0) // HEAD
        column = lax.broadcasted_iota(jnp.int32, spread.shape, 1)
        spread[...] = jnp.where((column == head_of) | (column == head_of + 8), 1.0, 0.0).astype(BF16)

    low, high = pair_masks(BF16)
    lane = lax.broadcasted_iota(jnp.int32, (1, PAIR), 1)
    keys_t, queries_t, douts_t = [], [], []
    for g in range(group):
        rows[g * padded : g * padded + length, :] = x_ref[g].astype(F32)
        span = slice(g * padded, (g + 1) * padded)
        qpad[g, :padded, :] = mixed_ref[span, :width]
        dcontext = dcontext_ref[span, :]
        opad[g, :padded, :width] = dcontext
        delta = nn((dcontext.astype(F32) * context_ref[span, :].astype(F32)).astype(BF16), spread[...])
        coarse = delta.astype(BF16).astype(F32)
        opad[g, :padded, width:] = jnp.where(lane < 8, coarse, delta - coarse).astype(BF16)
        keys_t.append(mixed_ref[span, width : 2 * width].T)
        queries_t.append(qpad[g].T)
        douts_t.append(opad[g, :, :width].T)

    def dprobs_of(g, h):
        span = slice(g * padded, (g + 1) * padded)
        at = h // 2 * PAIR
        mask = low if h % 2 == 0 else high
        pick = jnp.where((lane == h) | (lane == h + 8), -1.0, 0.0).astype(BF16)
        value = mixed_ref[span, 2 * width + at : 2 * width + at + PAIR] * mask
        value = jnp.concatenate([value, jnp.broadcast_to(pick, value.shape)], axis=1)
        douter = jnp.concatenate([opad[g, :, at : at + PAIR], opad[g, :, width:]], axis=1)
        return nt(value, douter)

    def finish(g, h, dscores):
        own = slice(h * HEAD, (h + 1) * HEAD)
        turned[g, own, :] = (nn(keys_t[g][own], dscores) * 0.125).astype(BF16)
        dkey = nt(queries_t[g][own], dscores) * 0.125
        turned[g, width + h * HEAD : width + (h + 1) * HEAD, :padded] = dkey.astype(BF16)
        dvalue = nt(douts_t[g][own], probs_ref[g, h])
        turned[g, 2 * width + h * HEAD : 2 * width + (h + 1) * HEAD, :padded] = dvalue.astype(BF16)

    jobs = [(g, h) for g in range(group) for h in range(HEADS)]
    dprobs = {job: dprobs_of(*job) for job in jobs[:AHEAD3]}
    done = {}
    for i, job in enumerate(jobs):
        if i + AHEAD3 < len(jobs):
            dprobs[jobs[i + AHEAD3]] = dprobs_of(*jobs[i + AHEAD3])
        done[job] = (probs_ref[job[0], job[1]].astype(F32) * dprobs.pop(job)).astype(BF16)
        if i >= LAG3:
            finish(*jobs[i - LAG3], done.pop(jobs[i - LAG3]))
    for job in jobs[len(jobs) - LAG3 :]:
        finish(*job, done.pop(job))
    for g in range(group):
        dmixed_ref[g * padded : (g + 1) * padded, :] = turned[g].T[:padded]
    hat, _ = normalize(rows[...])
    dmixed = dmixed_ref[...]
    sums[0:1, :] += column_sum(dmixed.astype(F32))
    hat = hat.astype(BF16)
    full = hat.shape[0] // DEPTH * DEPTH
    qkv_g[...] += tn(hat[:full], dmixed[:full])
    keep_rest(left, (hat, dmixed), full)

    @pl.when(pl.program_id(0) == pl.num_programs(0) - 1)
    def _():
        if left:
            qkv_g[...] += tn(left[0][...], left[1][...])
        half, third = width // 2, width // 6
        part = 7 * PAIR
        rest = 3 * width - part

        def put(k, ref):
            ref[:half, :part] = qkv_g[k * half : (k + 1) * half, :part].astype(BF16)
            for j in range(3):
                strip = slice(k * half + j * third, k * half + (j + 1) * third)
                ref[half:, j * rest : (j + 1) * rest] = qkv_g[strip, part:].astype(BF16)
            totals = jnp.concatenate(
                [sums[0:1, j * PAIR : (j + 1) * PAIR] for j in range(3 * width // PAIR)]
                + [jnp.zeros((third - 3 * width // PAIR, PAIR), F32)],
                axis=0,
            )
            ref[half:, 3 * rest :] = totals.astype(BF16)

        for k in range(2):
            @pl.when(facts[1] == k)
            def _(k=k):
                put(k, keep_ref)
                put(1 - k, send_ref)


def attend_back(facts, images, mixed, probs, context, dcontext, group):
    blocks, length, width = images.shape
    padded = up_to(length, 16)
    lanes = up_to(length, 128)
    row = lambda cols: pl.BlockSpec((group * padded, cols), lambda i: (i, 0))
    pack = (width // 2 + width // 6, 7 * PAIR)
    return pl.pallas_call(
        functools.partial(attend_back_kernel, length, group),
        grid=(blocks // group,),
        in_specs=[
            SCALARS,
            pl.BlockSpec((group, length, width), lambda i: (i, 0, 0)),
            row(3 * width),
            pl.BlockSpec((group, HEADS, padded, lanes), lambda i: (i, 0, 0, 0)),
            row(width),
            row(width),
        ],
        out_specs=[row(3 * width), once(pack), once(pack)],
        out_shape=[
            jax.ShapeDtypeStruct((blocks * padded, 3 * width), BF16),
            jax.ShapeDtypeStruct(pack, BF16),
            jax.ShapeDtypeStruct(pack, BF16),
        ],
        scratch_shapes=[
            pltpu.VMEM((group * padded, width), F32),
            pltpu.VMEM((group, lanes, width), BF16),
            pltpu.VMEM((group, lanes, width + PAIR), BF16),
            pltpu.VMEM((group, 3 * width, lanes), BF16),
            pltpu.VMEM((width, PAIR), BF16),
            pltpu.VMEM((width, 3 * width), F32),
            pltpu.VMEM((8, 3 * width), F32),
        ]
        + rest_space(blocks, group * padded, group, (width, 3 * width)),
        compiler_params=params(50),
        cost_estimate=pl.CostEstimate(flops=2 * 10**10, bytes_accessed=3 * 10**7, transcendentals=0),
        name="attend_back",
    )(facts, images, mixed, probs, context, dcontext)


def layer_out_kernel(length, group, facts, resid_ref, active_ref, vec_ref, down_mine, down_other, out_ref, down):
    padded = resid_ref.shape[0] // group
    step = pl.program_id(0)

    @pl.when(step == 0)
    def _():
        join_halves(down, down_mine, down_other, facts[1])

    result = resid_ref[...] + nn(active_ref[...], down[...]) + vec_ref[7:8, :]
    for g in range(group):
        live = jnp.where(step * group + g < facts[0], 1.0, 0.0)
        out_ref[g] = (result[g * padded : g * padded + length] * live).astype(BF16)


def layer_output(facts, images, resid, active, vectors, mine, other, group):
    blocks, length, width = images.shape
    padded = up_to(length, 16)
    hidden = active.shape[1]
    row = lambda cols: pl.BlockSpec((group * padded, cols), lambda i: (i, 0))
    return pl.pallas_call(
        functools.partial(layer_out_kernel, length, group),
        grid=(blocks // group,),
        in_specs=[SCALARS, row(width), row(hidden), once(vectors.shape), once(mine.shape), once(other.shape)],
        out_specs=pl.BlockSpec((group, length, width), lambda i: (i, 0, 0)),
        out_shape=jax.ShapeDtypeStruct((blocks, length, width), BF16),
        scratch_shapes=[pltpu.VMEM((hidden, width), BF16)],
        compiler_params=params(46),
        cost_estimate=pl.CostEstimate(flops=10**10, bytes_accessed=2 * 10**7, transcendentals=0),
        name="layer_output",
    )(facts, resid, active, vectors, mine, other)


def input_grad_kernel(length, group, facts, x_ref, dresid_ref, dmixed_ref, vec_ref, qkv_mine, qkv_other,
                      dx_ref, rows, qkv):
    padded = rows.shape[0] // group

    @pl.when(pl.program_id(0) == 0)
    def _():
        rows[...] = jnp.zeros_like(rows)
        join_halves(qkv, qkv_mine, qkv_other, facts[1])

    for g in range(group):
        rows[g * padded : g * padded + length, :] = x_ref[g].astype(F32)
    dnormed = nt(dmixed_ref[...], qkv[...])
    hat, inv = normalize(rows[...])
    dx = dresid_ref[...] + normalize_back(hat, inv, dnormed * vec_ref[0:1, :])
    for g in range(group):
        dx_ref[g] = dx[g * padded : g * padded + length]


def input_grad(facts, images, dresid, dmixed, vectors, mine, other, start, count, group):
    _, length, width = images.shape
    padded = up_to(length, 16)
    base = start // group
    return pl.pallas_call(
        functools.partial(input_grad_kernel, length, group),
        grid=(count // group,),
        in_specs=[
            SCALARS,
            pl.BlockSpec((group, length, width), lambda i: (base + i, 0, 0)),
            pl.BlockSpec((group * padded, width), lambda i: (base + i, 0)),
            pl.BlockSpec((group * padded, 3 * width), lambda i: (base + i, 0)),
            once(vectors.shape),
            once(mine.shape),
            once(other.shape),
        ],
        out_specs=pl.BlockSpec((group, length, width), lambda i: (i, 0, 0)),
        out_shape=jax.ShapeDtypeStruct((count, length, width), F32),
        scratch_shapes=[
            pltpu.VMEM((group * padded, width), F32),
            pltpu.VMEM((width, 3 * width), BF16),
        ],
        compiler_params=params(14),
        cost_estimate=pl.CostEstimate(flops=10**9 * count, bytes_accessed=2 * 10**6 * count, transcendentals=0),
        name="input_grad",
    )(facts, images, dresid, dmixed, vectors, mine, other)


def unpack_feed_kernel(factor, facts, pack_ref, up_ref, down_ref, proj_ref, up_bias_ref, *vec_refs):
    half, hidden = up_ref.shape
    width = proj_ref.shape[1]
    part, third, own = hidden // 4 * 3, width // 6, hidden // 2
    extra, tall = hidden - part, half + third
    split = width - tall
    last = part + own + width
    whole = pack_ref[...].astype(F32) * factor
    up_ref[:, :part] = whole[:half, :part]
    for j in range(3):
        up_ref[j * third : (j + 1) * third, part:] = whole[half:, j * extra : (j + 1) * extra]
    down_ref[:, :tall] = whole[:, part : part + own].T
    for j in range(2):
        down_ref[j * width : (j + 1) * width, tall:] = whole[j * split : (j + 1) * split, part + own : last].T
    proj_ref[...] = whole[:half, last:]
    totals = whole[half : half + 8, last:]
    first = facts[1] == 0
    own_totals = jnp.where(first, totals[:, :half], totals[:, half:])
    for k, ref in enumerate(vec_refs):
        ref[...] = own_totals[k : k + 1, :].reshape(half)
    pieces = [totals[4 + j : 5 + j, :] for j in range(hidden // width)]
    near, far = jnp.concatenate(pieces[:2], axis=1), jnp.concatenate(pieces[2:], axis=1)
    up_bias_ref[...] = jnp.where(first, near, far).reshape(own)


def unpack_feed(facts, pack, factor, half, hidden):
    width = 2 * half
    return pl.pallas_call(
        functools.partial(unpack_feed_kernel, factor),
        in_specs=[SCALARS, VMEM_WHOLE],
        out_specs=[VMEM_WHOLE] * 8,
        out_shape=[
            jax.ShapeDtypeStruct((half, hidden), F32),
            jax.ShapeDtypeStruct((hidden // 2, width), F32),
            jax.ShapeDtypeStruct((half, width), F32),
            jax.ShapeDtypeStruct((hidden // 2,), F32),
        ]
        + [jax.ShapeDtypeStruct((half,), F32)] * 4,
        compiler_params=params(20),
        name="unpack_feed",
    )(facts, pack)


def unpack_attend_kernel(factor, facts, pack_ref, weight_ref, small_ref, qkv_ref, *vec_refs):
    half, wide = qkv_ref.shape
    width = wide // 3
    third, part = width // 6, 7 * PAIR
    rest = wide - part
    whole = pack_ref[...].astype(F32) * factor
    lower = [whole[half:, j * rest : (j + 1) * rest] for j in range(3)]
    product = jnp.concatenate([whole[:half, :part], jnp.concatenate(lower, axis=0)], axis=1)
    totals = jnp.concatenate(
        [whole[half + j : half + j + 1, 3 * rest :] for j in range(wide // PAIR)], axis=1
    )
    columns = small_ref[:8, :].T
    qkv_ref[...] = product * columns[:, 0:1] + totals * columns[:, 1:2]
    weight = weight_ref[...].astype(F32)

    def row_totals(values):
        lanes = sum(values[:, at : at + PAIR] for at in range(0, wide, PAIR))
        return column_sum(lanes.T)

    gain = row_totals(weight * product)
    shift = row_totals(weight * totals)
    first = facts[1] == 0
    query = jnp.where(first, totals[:, :half], totals[:, half:width])
    value = jnp.where(first, totals[:, 2 * width : 2 * width + half], totals[:, 2 * width + half :])
    for ref, row in zip(vec_refs, (gain, shift, query, value)):
        ref[...] = row.reshape(half)


def unpack_attend(facts, pack, weight, small, factor):
    half, wide = weight.shape
    return pl.pallas_call(
        functools.partial(unpack_attend_kernel, factor),
        in_specs=[SCALARS] + [VMEM_WHOLE] * 3,
        out_specs=[VMEM_WHOLE] * 5,
        out_shape=[jax.ShapeDtypeStruct((half, wide), F32)] + [jax.ShapeDtypeStruct((half,), F32)] * 4,
        compiler_params=params(12),
        name="unpack_attend",
    )(facts, pack, weight, small)


def swap(values):
    return lax.ppermute(values, "shard", [(0, 1), (1, 0)])


def partners(devices, stride, size, flip):
    pairs = []
    for position in range(devices):
        digit = position // stride % size
        pairs.append((position, position + ((digit ^ flip) - digit) * stride))
    return pairs


def tree_sum(terms):
    terms = [term.astype(F32) for term in terms]
    while len(terms) > 1:
        terms = [terms[k] + terms[k + 1] for k in range(0, len(terms), 2)]
    return terms[0].astype(BF16)


def splits(devices):
    plan = []
    stride = 1
    while stride < devices:
        size = 4 if devices // stride % 4 == 0 else 2
        plan.append((stride, size, stride * size < devices))
        stride *= size
    return plan


def doublings(devices):
    return [(1, 4, True)] + [(4 << k, 2, False) for k in reversed(range((devices // 4).bit_length() - 1))]


def phase_count(plan):
    return 1 + len(plan) + sum(scattered for _, _, scattered in plan)


def exchange(keep, pack, devices, plan):
    got = yield [(pack, None)]
    value = tree_sum([keep, got[0]])
    index = lax.axis_index("dp")
    kept = []
    for stride, size, scattered in plan:
        digit = index // stride % size
        pairs = [partners(devices, stride, size, flip) for flip in range(1, size)]
        if not scattered:
            got = yield [(value, pair) for pair in pairs]
            value = tree_sum([value] + got)
        else:
            rows, columns = value.shape
            chunks = value.reshape(size, rows // size, columns)
            mine = lax.dynamic_index_in_dim(chunks, digit, 0, keepdims=False)
            got = yield [
                (lax.dynamic_index_in_dim(chunks, digit ^ flip, 0, keepdims=False), pairs[flip - 1])
                for flip in range(1, size)
            ]
            value = tree_sum([mine] + got)
            kept.append((size, digit, pairs))
    for size, digit, pairs in reversed(kept):
        got = yield [(value, pair) for pair in pairs]
        rows, columns = value.shape
        whole = jnp.zeros((size, rows, columns), BF16)
        for flip, piece in enumerate([value] + got):
            whole = lax.dynamic_update_index_in_dim(whole, piece, digit ^ flip, 0)
        value = whole.reshape(size * rows, columns)
    return value


def transfer(items):
    return [swap(value) if pairs is None else lax.ppermute(value, "dp", pairs) for value, pairs in items]


def resume(steps, got):
    try:
        return steps.send(got), None
    except StopIteration as stop:
        return None, stop.value


def tie(items, token):
    values, token = lax.optimization_barrier(([value for value, _ in items], token))
    return [(value, pairs) for value, (_, pairs) in zip(values, items)], token


def beside(got, work, token, under_way=()):
    return lax.optimization_barrier((got, under_way, work(token)))


def skip_phases(steps, items, count):
    for _ in range(count):
        items, _ = resume(steps, transfer(items))
    return items


def on_device(
    images,
    counts,
    cotangent,
    attn_gain,
    attn_shift,
    qkv_weight,
    query_bias,
    value_bias,
    proj_weight,
    proj_bias,
    mlp_gain,
    mlp_shift,
    up_weight,
    up_bias,
    down_weight,
    down_bias,
):
    blocks, length, width = images.shape
    half = attn_gain.shape[0]
    hidden = 2 * up_bias.shape[0]
    devices = lax.axis_size("dp")
    me = lax.axis_index("shard")
    facts = jnp.stack([counts[0], me.astype(jnp.int32)])
    qkv_other = swap(qkv_weight)
    small = pack_small(
        [attn_gain, attn_shift, query_bias, value_bias, proj_bias, mlp_gain, mlp_shift, down_bias, up_bias]
    )
    small_other = swap(small)
    proj_other, up_other, down_other = swap(proj_weight), swap(up_weight), swap(down_weight)

    mixed, probs, context, vectors, up_bias_row = attend(
        facts, images, small, small_other, qkv_weight, qkv_other, hidden, 4
    )
    resid, active, dresid, dcontext, keep, pack = feed(
        facts,
        images,
        cotangent,
        context,
        vectors,
        up_bias_row,
        (proj_weight, proj_other, up_weight, up_other, down_weight, down_other),
        4,
    )

    def write_layer(token):
        rows = layer_output(token, images, resid, active, vectors, down_weight, down_other, 4)
        return jnp.transpose(rows, (1, 0, 2))

    def back(token):
        return attend_back(token, images, mixed, probs, context, dcontext, 4)

    factor = 1.0 / math.sqrt(blocks * length * devices * lax.axis_size("shard"))
    count = blocks // 2
    feed_plan, plan = doublings(devices), splits(devices)

    def grads(start):
        return lambda token: input_grad(
            token, images, dresid, dmixed, vectors, qkv_weight, qkv_other, start, count, 4
        )

    feed_steps = exchange(keep, pack, devices, feed_plan)
    feed_items, _ = resume(feed_steps, transfer(next(feed_steps)))
    feed_items, token = tie(feed_items, facts)
    got, _, (dmixed, keep, pack) = beside(transfer(feed_items), back, token)

    feed_items, _ = resume(feed_steps, got)
    feed_items, token = tie(feed_items, facts)
    feed_got = transfer(feed_items)
    steps = exchange(keep, pack, devices, plan)
    got, feed_got, (layer_out, first_grads) = beside(
        transfer(next(steps)), lambda token: (write_layer(token), grads(0)(token)), token, feed_got
    )

    feed_items, _ = resume(feed_steps, feed_got)
    feed_items, token = tie(feed_items, facts)
    feed_got = transfer(feed_items)
    items, _ = resume(steps, got)
    items, token = tie(items, token)
    got, feed_got, last_grads = beside(transfer(items), grads(count), token, feed_got)

    feed_items, _ = resume(feed_steps, feed_got)
    feed_items = skip_phases(feed_steps, feed_items, phase_count(feed_plan) - 5)
    items, _ = resume(steps, got)
    items, both = tie(items, (first_grads, last_grads))
    got = transfer(items)
    feed_items, both = tie(feed_items, both)
    feed_arriving = transfer(feed_items)
    got, _, images_grad = beside(
        got, lambda both: jnp.transpose(jnp.concatenate(both, axis=0), (1, 0, 2)), both
    )

    items, _ = resume(steps, got)
    items = skip_phases(steps, items, phase_count(plan) - 4)
    _, feed_total = resume(feed_steps, feed_arriving)
    items, token = tie(items, facts)
    got, _, unpacked = beside(
        transfer(items), lambda token: unpack_feed(token, feed_total, factor, half, hidden), token
    )
    _, attend_total = resume(steps, got)
    layer_out = jnp.transpose(layer_out, (1, 0, 2))
    up_g, down_g, proj_g, up_bias_g, proj_bias_g, mlp_gain_g, mlp_shift_g, down_bias_g = unpacked
    images_grad = jnp.transpose(images_grad, (1, 0, 2))
    qkv_g, attn_gain_g, attn_shift_g, query_bias_g, value_bias_g = unpack_attend(
        facts, attend_total, qkv_weight, small, factor
    )
    return (
        layer_out,
        images_grad,
        attn_gain_g,
        attn_shift_g,
        qkv_g,
        query_bias_g,
        value_bias_g,
        proj_g,
        proj_bias_g,
        mlp_gain_g,
        mlp_shift_g,
        up_g,
        up_bias_g,
        down_g,
        down_bias_g,
    )


def solution(mesh):
    placed = (
        P(("dp", "shard"), None, None),
        P(("dp", "shard")),
        P(("dp", "shard"), None, None),
        P("shard"),
        P("shard"),
        P("shard", None),
        P("shard"),
        P("shard"),
        P("shard", None),
        P("shard"),
        P("shard"),
        P("shard"),
        P("shard", None),
        P("shard"),
        P("shard", None),
        P("shard"),
    )
    return jax.shard_map(
        on_device,
        mesh=mesh,
        in_specs=placed,
        out_specs=(
            P(("dp", "shard"), None, None),
            P(("dp", "shard"), None, None),
            P("shard"),
            P("shard"),
            P("shard", None),
            P("shard"),
            P("shard"),
            P("shard", None),
            P("shard"),
            P("shard"),
            P("shard"),
            P("shard", None),
            P("shard"),
            P("shard", None),
            P("shard"),
        ),
        check_vma=False,
    )
```

```python
import functools
import math

import jax
import jax.numpy as jnp
from jax import lax
from jax.experimental import pallas as pl
from jax.experimental.layout import Layout, with_layout_constraint
from jax.experimental.pallas import tpu as pltpu
from jax.sharding import PartitionSpec as P

HEADS = 6
HEAD = 64
PAIR = 2 * HEAD
EPS = 1e-06
CHUNK = 256
DEPTH = 256
AHEAD3 = 3
LAG3 = 2
AHEAD = 3
LAG = 2
F32 = jnp.float32
BF16 = jnp.bfloat16
INV_SQRT_2PI = 1.0 / math.sqrt(2.0 * math.pi)


def up_to(size, step):
    return -(-size // step) * step


def nn(a, b):
    return lax.dot_general(a, b, (((1,), (0,)), ((), ())), preferred_element_type=F32)


def nt(a, b):
    return lax.dot_general(a, b, (((1,), (1,)), ((), ())), preferred_element_type=F32)


def tn(a, b):
    return lax.dot_general(a, b, (((0,), (0,)), ((), ())), preferred_element_type=F32)


def normalize(rows):
    center = jnp.mean(rows, axis=-1, keepdims=True)
    centered = rows - center
    inv = lax.rsqrt(jnp.mean(centered * centered, axis=-1, keepdims=True) + EPS)
    return centered * inv, inv


def normalize_back(hat, inv, dhat):
    first = jnp.mean(dhat, axis=-1, keepdims=True)
    second = jnp.mean(dhat * hat, axis=-1, keepdims=True)
    return inv * (dhat - first - hat * second)


def column_sum(rows):
    return jnp.sum(rows, axis=0, keepdims=True)


def pair_masks(dtype):
    lane = lax.broadcasted_iota(jnp.int32, (1, PAIR), 1)
    low = jnp.where(lane < HEAD, 1.0, 0.0)
    return low.astype(dtype), (1.0 - low).astype(dtype)


def gelu_parts(hidden):
    cdf = 0.5 + 0.5 * lax.erf(hidden * math.sqrt(0.5))
    return hidden * cdf, cdf + hidden * jnp.exp(hidden * hidden * -0.5) * INV_SQRT_2PI


def join_halves(whole, mine, other, me):
    half = mine.shape[0]
    whole[pl.ds(pl.multiple_of(me * half, 16), half), :] = mine[...]
    whole[pl.ds(pl.multiple_of((1 - me) * half, 16), half), :] = other[...]


def keep_rest(left, values, full):
    rest = values[0].shape[0] - full
    if rest:
        at = pl.ds(pl.multiple_of(pl.program_id(0) * rest, 16), rest)
        for ref, value in zip(left, values):
            ref[at, :] = value[full:]


def rest_space(blocks, rows, group, widths):
    rest = rows % DEPTH * (blocks // group)
    return [pltpu.VMEM((rest, width), BF16) for width in widths] if rest else []


def once(shape):
    return pl.BlockSpec(shape, lambda i: (0,) * len(shape), pipeline_mode=pl.Buffered(1))


SCALARS = pl.BlockSpec(memory_space=pltpu.SMEM)


def params(mebibytes):
    return pltpu.CompilerParams(vmem_limit_bytes=mebibytes * 2**20)


VMEM_WHOLE = pl.BlockSpec(memory_space=pltpu.VMEM)


def pack_small_kernel(*refs):
    out = refs[-1]
    half = out.shape[1]
    out[...] = jnp.zeros_like(out)
    for k, ref in enumerate(refs[:8]):
        out[k : k + 1, :] = ref[...].astype(F32).reshape(1, half)
    long = refs[8][...].astype(F32)
    for k in range(long.shape[0] // half):
        out[8 + k : 9 + k, :] = long[k * half : (k + 1) * half].reshape(1, half)


def pack_small(vectors):
    half = vectors[0].shape[0]
    return pl.pallas_call(
        pack_small_kernel,
        in_specs=[VMEM_WHOLE] * 9,
        out_specs=VMEM_WHOLE,
        out_shape=jax.ShapeDtypeStruct((16, half), F32),
        name="pack_small",
    )(*vectors)


def join_small(first, mine, other, vec_ref, up_bias_ref):
    near, far = jnp.where(first, mine, other), jnp.where(first, other, mine)
    vec_ref[...] = jnp.concatenate([near[:8], far[:8]], axis=1)
    count = up_bias_ref.shape[1] // mine.shape[1] // 2
    rows = [near[8 + k : 9 + k] for k in range(count)] + [far[8 + k : 9 + k] for k in range(count)]
    up_bias_ref[...] = jnp.concatenate(rows, axis=1)


def attend_kernel(length, group, facts, x_ref, small_mine, small_other, mine_ref, other_ref,
                  mixed_ref, probs_ref, context_ref, vec_ref, up_bias_ref, rows, qpad, weight):
    padded = rows.shape[0] // group
    width = rows.shape[1]

    @pl.when(pl.program_id(0) == 0)
    def _():
        rows[...] = jnp.zeros_like(rows)
        qpad[...] = jnp.zeros_like(qpad)
        join_halves(weight, mine_ref, other_ref, facts[1])
        join_small(facts[1] == 0, small_mine[...], small_other[...], vec_ref, up_bias_ref)

    for g in range(group):
        rows[g * padded : g * padded + length, :] = x_ref[g].astype(F32)
    hat, _ = normalize(rows[...])
    normed = (hat * vec_ref[0:1, :] + vec_ref[1:2, :]).astype(BF16)
    bias = jnp.concatenate([vec_ref[2:3, :], jnp.zeros((1, width), F32), vec_ref[3:4, :]], axis=1)
    mixed = (nn(normed, weight[...]) + bias).astype(BF16)
    mixed_ref[...] = mixed
    low, high = pair_masks(BF16)
    cut = length // 8 * 8
    live_key = lax.broadcasted_iota(jnp.int32, (padded - cut, 1), 0) < length - cut

    def scores_of(g, h):
        at = h // 2 * PAIR
        key = mixed[g * padded : (g + 1) * padded, width + at : width + at + PAIR] * (low if h % 2 == 0 else high)
        return nt(key, qpad[g, :, at : at + PAIR]) * 0.125

    def probs_of(g, h, scores):
        top = scores[:cut]
        rest = jnp.where(live_key, scores[cut:], -jnp.inf)
        peak = jnp.maximum(jnp.max(top, axis=0, keepdims=True), jnp.max(rest, axis=0, keepdims=True))
        top = jnp.exp(top - peak)
        rest = jnp.exp(rest - peak)
        scale = 1.0 / (column_sum(top) + column_sum(rest))
        probs = jnp.concatenate([top * scale, rest * scale], axis=0).astype(BF16)
        probs_ref[g, h] = probs
        return probs

    for g in range(group):
        qpad[g, :padded, :] = mixed[g * padded : (g + 1) * padded, :width]
    values_t = [mixed[g * padded : (g + 1) * padded, 2 * width :].T for g in range(group)]
    jobs = [(g, h) for g in range(group) for h in range(HEADS)]
    scores = {job: scores_of(*job) for job in jobs[:AHEAD]}
    outs, done = {}, {}
    for i, (g, h) in enumerate(jobs):
        if i + AHEAD < len(jobs):
            scores[jobs[i + AHEAD]] = scores_of(*jobs[i + AHEAD])
        done[g, h] = probs_of(g, h, scores.pop((g, h)))
        if i >= LAG:
            pg, ph = jobs[i - LAG]
            outs[pg, ph] = nn(values_t[pg][ph * HEAD : (ph + 1) * HEAD], done.pop((pg, ph)))
    for pg, ph in jobs[len(jobs) - LAG :]:
        outs[pg, ph] = nn(values_t[pg][ph * HEAD : (ph + 1) * HEAD], done.pop((pg, ph)))
    for g in range(group):
        context_t = jnp.concatenate([outs[g, h] for h in range(HEADS)], axis=0).astype(BF16)
        context_ref[g * padded : (g + 1) * padded, :] = context_t.T[:padded]


def attend(facts, images, small, small_other, mine, other, hidden, group):
    blocks, length, width = images.shape
    padded = up_to(length, 16)
    lanes = up_to(length, 128)
    return pl.pallas_call(
        functools.partial(attend_kernel, length, group),
        grid=(blocks // group,),
        in_specs=[
            SCALARS,
            pl.BlockSpec((group, length, width), lambda i: (i, 0, 0)),
            once(small.shape),
            once(small.shape),
            once(mine.shape),
            once(other.shape),
        ],
        out_specs=[
            pl.BlockSpec((group * padded, 3 * width), lambda i: (i, 0)),
            pl.BlockSpec((group, HEADS, padded, lanes), lambda i: (i, 0, 0, 0)),
            pl.BlockSpec((group * padded, width), lambda i: (i, 0)),
            once((8, width)),
            once((1, hidden)),
        ],
        out_shape=[
            jax.ShapeDtypeStruct((blocks * padded, 3 * width), BF16),
            jax.ShapeDtypeStruct((blocks, HEADS, padded, lanes), BF16),
            jax.ShapeDtypeStruct((blocks * padded, width), BF16),
            jax.ShapeDtypeStruct((8, width), F32),
            jax.ShapeDtypeStruct((1, hidden), F32),
        ],
        scratch_shapes=[
            pltpu.VMEM((group * padded, width), F32),
            pltpu.VMEM((group, lanes, width), BF16),
            pltpu.VMEM((width, 3 * width), BF16),
        ],
        compiler_params=params(50),
        cost_estimate=pl.CostEstimate(flops=10**10, bytes_accessed=3 * 10**7, transcendentals=0),
        name="attend",
    )(facts, images, small, small_other, mine, other)


def feed_kernel(length, group, facts, x_ref, cot_ref, context_ref, vec_ref, up_bias_ref,
                proj_mine, proj_other, up_mine, up_other, down_mine, down_other,
                resid_ref, active_ref, dresid_ref, dcontext_ref, keep_ref, send_ref,
                rows, cots, proj, up, down, up_g, down_g, proj_g, sums, up_sum, *left):
    padded = rows.shape[0] // group
    width = rows.shape[1]
    hidden_size = up.shape[1]
    step = pl.program_id(0)

    @pl.when(step == 0)
    def _():
        for ref in (rows, cots, up_g, down_g, proj_g, sums, up_sum):
            ref[...] = jnp.zeros_like(ref)
        join_halves(proj, proj_mine, proj_other, facts[1])
        join_halves(up, up_mine, up_other, facts[1])
        join_halves(down, down_mine, down_other, facts[1])

    for g in range(group):
        live = jnp.where(step * group + g < facts[0], 1.0, 0.0)
        rows[g * padded : g * padded + length, :] = x_ref[g].astype(F32)
        cots[g * padded : g * padded + length, :] = cot_ref[g].astype(F32) * live
    context = context_ref[...]
    resid = rows[...] + nn(context, proj[...]) + vec_ref[4:5, :]
    resid_ref[...] = resid.astype(BF16)
    hat, inv = normalize(resid)
    gain = vec_ref[5:6, :]
    normed = (hat * gain + vec_ref[6:7, :]).astype(BF16)
    dout = cots[...]
    dout_low = dout.astype(BF16)
    actives, dhiddens = [], []
    for at in range(0, hidden_size, CHUNK):
        cols = slice(at, at + CHUNK)
        hidden = nn(normed, up[:, cols]) + up_bias_ref[:, cols]
        active, slope = gelu_parts(hidden)
        actives.append(active.astype(BF16))
        active_ref[:, cols] = actives[-1]
        dhidden = nt(dout_low, down[cols, :]) * slope
        up_sum[0:1, cols] += column_sum(dhidden)
        dhiddens.append(dhidden.astype(BF16))
    active = jnp.concatenate(actives, axis=1)
    dhidden = jnp.concatenate(dhiddens, axis=1)
    dnormed = nt(dhidden, up[...])
    dresid = dout + normalize_back(hat, inv, dnormed * gain)
    dresid_low = dresid.astype(BF16)
    dresid_ref[...] = dresid_low
    dcontext_ref[...] = nt(dresid_low, proj[...]).astype(BF16)
    sums[0:1, :] += column_sum(dresid)
    sums[1:2, :] += column_sum(dnormed * hat)
    sums[2:3, :] += column_sum(dnormed)
    sums[3:4, :] += column_sum(dout)
    full = normed.shape[0] // DEPTH * DEPTH
    up_g[...] += tn(normed[:full], dhidden[:full])
    down_g[...] += tn(dout_low[:full], active[:full])
    proj_g[...] += tn(context[:full], dresid_low[:full])
    keep_rest(left, (normed, dhidden, dout_low, active, context, dresid_low), full)

    @pl.when(step == pl.num_programs(0) - 1)
    def _():
        if left:
            up_g[...] += tn(left[0][...], left[1][...])
            down_g[...] += tn(left[2][...], left[3][...])
            proj_g[...] += tn(left[4][...], left[5][...])
        half, part = width // 2, hidden_size // 4 * 3
        extra, third, own = hidden_size - part, width // 6, hidden_size // 2
        tall, last = half + third, part + own + width
        split = width - tall

        def put(k, ref):
            mine = slice(k * half, (k + 1) * half)
            ref[:half, :part] = up_g[mine, :part].astype(BF16)
            for j in range(3):
                strip = slice(k * half + j * third, k * half + (j + 1) * third)
                ref[half:, j * extra : (j + 1) * extra] = up_g[strip, part:].astype(BF16)
            ref[:, part : part + own] = down_g[:tall, k * own : (k + 1) * own].astype(BF16)
            for j in range(2):
                cols = slice(k * own + j * width, k * own + (j + 1) * width)
                ref[j * split : (j + 1) * split, part + own : last] = down_g[tall:, cols].astype(BF16)
            ref[:half, last:] = proj_g[mine, :].astype(BF16)
            totals = jnp.concatenate(
                [sums[0:4, :]]
                + [up_sum[0:1, j * width : (j + 1) * width] for j in range(hidden_size // width)]
                + [jnp.zeros((third - 4 - hidden_size // width, width), F32)],
                axis=0,
            )
            ref[half:, last:] = totals.astype(BF16)

        for k in range(2):
            @pl.when(facts[1] == k)
            def _(k=k):
                put(k, keep_ref)
                put(1 - k, send_ref)


def feed(facts, images, cotangent, context, vectors, up_bias, weights, group):
    blocks, length, width = images.shape
    padded = up_to(length, 16)
    hidden = up_bias.shape[1]
    row = lambda cols: pl.BlockSpec((group * padded, cols), lambda i: (i, 0))
    image = pl.BlockSpec((group, length, width), lambda i: (i, 0, 0))
    pack = (width // 2 + width // 6, hidden // 4 * 3 + hidden // 2 + 2 * width)
    return pl.pallas_call(
        functools.partial(feed_kernel, length, group),
        grid=(blocks // group,),
        in_specs=[SCALARS, image, image, row(width), once(vectors.shape), once(up_bias.shape)]
        + [once(weight.shape) for weight in weights],
        out_specs=[row(width), row(hidden), row(width), row(width), once(pack), once(pack)],
        out_shape=[
            jax.ShapeDtypeStruct((blocks * padded, width), BF16),
            jax.ShapeDtypeStruct((blocks * padded, hidden), BF16),
            jax.ShapeDtypeStruct((blocks * padded, width), BF16),
            jax.ShapeDtypeStruct((blocks * padded, width), BF16),
            jax.ShapeDtypeStruct(pack, BF16),
            jax.ShapeDtypeStruct(pack, BF16),
        ],
        scratch_shapes=[
            pltpu.VMEM((group * padded, width), F32),
            pltpu.VMEM((group * padded, width), F32),
            pltpu.VMEM((width, width), BF16),
            pltpu.VMEM((width, hidden), BF16),
            pltpu.VMEM((hidden, width), BF16),
            pltpu.VMEM((width, hidden), F32),
            pltpu.VMEM((width, hidden), F32),
            pltpu.VMEM((width, width), F32),
            pltpu.VMEM((8, width), F32),
            pltpu.VMEM((8, hidden), F32),
        ]
        + rest_space(blocks, group * padded, group, (width, hidden, width, hidden, width, width)),
        compiler_params=params(42),
        cost_estimate=pl.CostEstimate(flops=3 * 10**10, bytes_accessed=5 * 10**7, transcendentals=0),
        name="feed",
    )(facts, images, cotangent, context, vectors, up_bias, *weights)


def attend_back_kernel(length, group, facts, x_ref, mixed_ref, probs_ref, context_ref, dcontext_ref,
                       dmixed_ref, keep_ref, send_ref, rows, qpad, opad, turned, spread, qkv_g, sums, *left):
    padded = rows.shape[0] // group
    width = rows.shape[1]

    @pl.when(pl.program_id(0) == 0)
    def _():
        for ref in (rows, qpad, opad, turned, qkv_g, sums):
            ref[...] = jnp.zeros_like(ref)
        head_of = lax.broadcasted_iota(jnp.int32, spread.shape, 0) // HEAD
        column = lax.broadcasted_iota(jnp.int32, spread.shape, 1)
        spread[...] = jnp.where((column == head_of) | (column == head_of + 8), 1.0, 0.0).astype(BF16)

    low, high = pair_masks(BF16)
    lane = lax.broadcasted_iota(jnp.int32, (1, PAIR), 1)
    keys_t, queries_t, douts_t = [], [], []
    for g in range(group):
        rows[g * padded : g * padded + length, :] = x_ref[g].astype(F32)
        span = slice(g * padded, (g + 1) * padded)
        qpad[g, :padded, :] = mixed_ref[span, :width]
        dcontext = dcontext_ref[span, :]
        opad[g, :padded, :width] = dcontext
        delta = nn((dcontext.astype(F32) * context_ref[span, :].astype(F32)).astype(BF16), spread[...])
        coarse = delta.astype(BF16).astype(F32)
        opad[g, :padded, width:] = jnp.where(lane < 8, coarse, delta - coarse).astype(BF16)
        keys_t.append(mixed_ref[span, width : 2 * width].T)
        queries_t.append(qpad[g].T)
        douts_t.append(opad[g, :, :width].T)

    def dprobs_of(g, h):
        span = slice(g * padded, (g + 1) * padded)
        at = h // 2 * PAIR
        mask = low if h % 2 == 0 else high
        pick = jnp.where((lane == h) | (lane == h + 8), -1.0, 0.0).astype(BF16)
        value = mixed_ref[span, 2 * width + at : 2 * width + at + PAIR] * mask
        value = jnp.concatenate([value, jnp.broadcast_to(pick, value.shape)], axis=1)
        douter = jnp.concatenate([opad[g, :, at : at + PAIR], opad[g, :, width:]], axis=1)
        return nt(value, douter)

    def finish(g, h, dscores):
        own = slice(h * HEAD, (h + 1) * HEAD)
        turned[g, own, :] = (nn(keys_t[g][own], dscores) * 0.125).astype(BF16)
        dkey = nt(queries_t[g][own], dscores) * 0.125
        turned[g, width + h * HEAD : width + (h + 1) * HEAD, :padded] = dkey.astype(BF16)
        dvalue = nt(douts_t[g][own], probs_ref[g, h])
        turned[g, 2 * width + h * HEAD : 2 * width + (h + 1) * HEAD, :padded] = dvalue.astype(BF16)

    jobs = [(g, h) for g in range(group) for h in range(HEADS)]
    dprobs = {job: dprobs_of(*job) for job in jobs[:AHEAD3]}
    done = {}
    for i, job in enumerate(jobs):
        if i + AHEAD3 < len(jobs):
            dprobs[jobs[i + AHEAD3]] = dprobs_of(*jobs[i + AHEAD3])
        done[job] = (probs_ref[job[0], job[1]].astype(F32) * dprobs.pop(job)).astype(BF16)
        if i >= LAG3:
            finish(*jobs[i - LAG3], done.pop(jobs[i - LAG3]))
    for job in jobs[len(jobs) - LAG3 :]:
        finish(*job, done.pop(job))
    for g in range(group):
        dmixed_ref[g * padded : (g + 1) * padded, :] = turned[g].T[:padded]
    hat, _ = normalize(rows[...])
    dmixed = dmixed_ref[...]
    sums[0:1, :] += column_sum(dmixed.astype(F32))
    hat = hat.astype(BF16)
    full = hat.shape[0] // DEPTH * DEPTH
    qkv_g[...] += tn(hat[:full], dmixed[:full])
    keep_rest(left, (hat, dmixed), full)

    @pl.when(pl.program_id(0) == pl.num_programs(0) - 1)
    def _():
        if left:
            qkv_g[...] += tn(left[0][...], left[1][...])
        half, third = width // 2, width // 6
        part = 7 * PAIR
        rest = 3 * width - part

        def put(k, ref):
            ref[:half, :part] = qkv_g[k * half : (k + 1) * half, :part].astype(BF16)
            for j in range(3):
                strip = slice(k * half + j * third, k * half + (j + 1) * third)
                ref[half:, j * rest : (j + 1) * rest] = qkv_g[strip, part:].astype(BF16)
            totals = jnp.concatenate(
                [sums[0:1, j * PAIR : (j + 1) * PAIR] for j in range(3 * width // PAIR)]
                + [jnp.zeros((third - 3 * width // PAIR, PAIR), F32)],
                axis=0,
            )
            ref[half:, 3 * rest :] = totals.astype(BF16)

        for k in range(2):
            @pl.when(facts[1] == k)
            def _(k=k):
                put(k, keep_ref)
                put(1 - k, send_ref)


def attend_back(facts, images, mixed, probs, context, dcontext, group):
    blocks, length, width = images.shape
    padded = up_to(length, 16)
    lanes = up_to(length, 128)
    row = lambda cols: pl.BlockSpec((group * padded, cols), lambda i: (i, 0))
    pack = (width // 2 + width // 6, 7 * PAIR)
    return pl.pallas_call(
        functools.partial(attend_back_kernel, length, group),
        grid=(blocks // group,),
        in_specs=[
            SCALARS,
            pl.BlockSpec((group, length, width), lambda i: (i, 0, 0)),
            row(3 * width),
            pl.BlockSpec((group, HEADS, padded, lanes), lambda i: (i, 0, 0, 0)),
            row(width),
            row(width),
        ],
        out_specs=[row(3 * width), once(pack), once(pack)],
        out_shape=[
            jax.ShapeDtypeStruct((blocks * padded, 3 * width), BF16),
            jax.ShapeDtypeStruct(pack, BF16),
            jax.ShapeDtypeStruct(pack, BF16),
        ],
        scratch_shapes=[
            pltpu.VMEM((group * padded, width), F32),
            pltpu.VMEM((group, lanes, width), BF16),
            pltpu.VMEM((group, lanes, width + PAIR), BF16),
            pltpu.VMEM((group, 3 * width, lanes), BF16),
            pltpu.VMEM((width, PAIR), BF16),
            pltpu.VMEM((width, 3 * width), F32),
            pltpu.VMEM((8, 3 * width), F32),
        ]
        + rest_space(blocks, group * padded, group, (width, 3 * width)),
        compiler_params=params(50),
        cost_estimate=pl.CostEstimate(flops=2 * 10**10, bytes_accessed=3 * 10**7, transcendentals=0),
        name="attend_back",
    )(facts, images, mixed, probs, context, dcontext)


def layer_out_kernel(length, group, facts, resid_ref, active_ref, vec_ref, down_mine, down_other, out_ref, down):
    padded = resid_ref.shape[0] // group
    step = pl.program_id(0)

    @pl.when(step == 0)
    def _():
        join_halves(down, down_mine, down_other, facts[1])

    result = resid_ref[...].astype(F32) + nn(active_ref[...], down[...]) + vec_ref[7:8, :]
    for g in range(group):
        live = jnp.where(step * group + g < facts[0], 1.0, 0.0)
        out_ref[g] = (result[g * padded : g * padded + length] * live).astype(BF16)


def layer_output(facts, images, resid, active, vectors, mine, other, group):
    blocks, length, width = images.shape
    padded = up_to(length, 16)
    hidden = active.shape[1]
    row = lambda cols: pl.BlockSpec((group * padded, cols), lambda i: (i, 0))
    return pl.pallas_call(
        functools.partial(layer_out_kernel, length, group),
        grid=(blocks // group,),
        in_specs=[SCALARS, row(width), row(hidden), once(vectors.shape), once(mine.shape), once(other.shape)],
        out_specs=pl.BlockSpec((group, length, width), lambda i: (i, 0, 0)),
        out_shape=jax.ShapeDtypeStruct((blocks, length, width), BF16),
        scratch_shapes=[pltpu.VMEM((hidden, width), BF16)],
        compiler_params=params(46),
        cost_estimate=pl.CostEstimate(flops=10**10, bytes_accessed=2 * 10**7, transcendentals=0),
        name="layer_output",
    )(facts, resid, active, vectors, mine, other)


def input_grad_kernel(length, group, facts, x_ref, dresid_ref, dmixed_ref, vec_ref, qkv_mine, qkv_other,
                      dx_ref, rows, qkv):
    padded = rows.shape[0] // group

    @pl.when(pl.program_id(0) == 0)
    def _():
        rows[...] = jnp.zeros_like(rows)
        join_halves(qkv, qkv_mine, qkv_other, facts[1])

    for g in range(group):
        rows[g * padded : g * padded + length, :] = x_ref[g].astype(F32)
    dnormed = nt(dmixed_ref[...], qkv[...])
    hat, inv = normalize(rows[...])
    dx = dresid_ref[...].astype(F32) + normalize_back(hat, inv, dnormed * vec_ref[0:1, :])
    for g in range(group):
        dx_ref[g] = dx[g * padded : g * padded + length]


def input_grad(facts, images, dresid, dmixed, vectors, mine, other, start, count, group):
    _, length, width = images.shape
    padded = up_to(length, 16)
    base = start // group
    return pl.pallas_call(
        functools.partial(input_grad_kernel, length, group),
        grid=(count // group,),
        in_specs=[
            SCALARS,
            pl.BlockSpec((group, length, width), lambda i: (base + i, 0, 0)),
            pl.BlockSpec((group * padded, width), lambda i: (base + i, 0)),
            pl.BlockSpec((group * padded, 3 * width), lambda i: (base + i, 0)),
            once(vectors.shape),
            once(mine.shape),
            once(other.shape),
        ],
        out_specs=pl.BlockSpec((group, length, width), lambda i: (i, 0, 0)),
        out_shape=jax.ShapeDtypeStruct((count, length, width), F32),
        scratch_shapes=[
            pltpu.VMEM((group * padded, width), F32),
            pltpu.VMEM((width, 3 * width), BF16),
        ],
        compiler_params=params(58),
        cost_estimate=pl.CostEstimate(flops=10**9 * count, bytes_accessed=2 * 10**6 * count, transcendentals=0),
        name="input_grad",
    )(facts, images, dresid, dmixed, vectors, mine, other)


def unpack_feed_kernel(factor, facts, pack_ref, up_ref, down_ref, proj_ref, up_bias_ref, *vec_refs):
    half, hidden = up_ref.shape
    width = proj_ref.shape[1]
    part, third, own = hidden // 4 * 3, width // 6, hidden // 2
    extra, tall = hidden - part, half + third
    split = width - tall
    last = part + own + width
    whole = pack_ref[...].astype(F32) * factor
    up_ref[:, :part] = whole[:half, :part]
    for j in range(3):
        up_ref[j * third : (j + 1) * third, part:] = whole[half:, j * extra : (j + 1) * extra]
    down_ref[:, :tall] = whole[:, part : part + own].T
    for j in range(2):
        down_ref[j * width : (j + 1) * width, tall:] = whole[j * split : (j + 1) * split, part + own : last].T
    proj_ref[...] = whole[:half, last:]
    totals = whole[half : half + 8, last:]
    first = facts[1] == 0
    own_totals = jnp.where(first, totals[:, :half], totals[:, half:])
    for k, ref in enumerate(vec_refs):
        ref[...] = own_totals[k : k + 1, :].reshape(half)
    pieces = [totals[4 + j : 5 + j, :] for j in range(hidden // width)]
    near, far = jnp.concatenate(pieces[:2], axis=1), jnp.concatenate(pieces[2:], axis=1)
    up_bias_ref[...] = jnp.where(first, near, far).reshape(own)


def unpack_feed(facts, pack, factor, half, hidden):
    width = 2 * half
    return pl.pallas_call(
        functools.partial(unpack_feed_kernel, factor),
        in_specs=[SCALARS, VMEM_WHOLE],
        out_specs=[VMEM_WHOLE] * 8,
        out_shape=[
            jax.ShapeDtypeStruct((half, hidden), F32),
            jax.ShapeDtypeStruct((hidden // 2, width), F32),
            jax.ShapeDtypeStruct((half, width), F32),
            jax.ShapeDtypeStruct((hidden // 2,), F32),
        ]
        + [jax.ShapeDtypeStruct((half,), F32)] * 4,
        compiler_params=params(20),
        name="unpack_feed",
    )(facts, pack)


def unpack_attend_kernel(factor, facts, pack_ref, weight_ref, small_ref, qkv_ref, *vec_refs):
    half, wide = qkv_ref.shape
    width = wide // 3
    third, part = width // 6, 7 * PAIR
    rest = wide - part
    whole = pack_ref[...].astype(F32) * factor
    lower = [whole[half:, j * rest : (j + 1) * rest] for j in range(3)]
    product = jnp.concatenate([whole[:half, :part], jnp.concatenate(lower, axis=0)], axis=1)
    totals = jnp.concatenate(
        [whole[half + j : half + j + 1, 3 * rest :] for j in range(wide // PAIR)], axis=1
    )
    columns = small_ref[:8, :].T
    qkv_ref[...] = product * columns[:, 0:1] + totals * columns[:, 1:2]
    weight = weight_ref[...].astype(F32)

    def row_totals(values):
        lanes = sum(values[:, at : at + PAIR] for at in range(0, wide, PAIR))
        return column_sum(lanes.T)

    gain = row_totals(weight * product)
    shift = row_totals(weight * totals)
    first = facts[1] == 0
    query = jnp.where(first, totals[:, :half], totals[:, half:width])
    value = jnp.where(first, totals[:, 2 * width : 2 * width + half], totals[:, 2 * width + half :])
    for ref, row in zip(vec_refs, (gain, shift, query, value)):
        ref[...] = row.reshape(half)


def unpack_attend(facts, pack, weight, small, factor):
    half, wide = weight.shape
    return pl.pallas_call(
        functools.partial(unpack_attend_kernel, factor),
        in_specs=[SCALARS] + [VMEM_WHOLE] * 3,
        out_specs=[VMEM_WHOLE] * 5,
        out_shape=[jax.ShapeDtypeStruct((half, wide), F32)] + [jax.ShapeDtypeStruct((half,), F32)] * 4,
        compiler_params=params(12),
        name="unpack_attend",
    )(facts, pack, weight, small)


def swap(values):
    return lax.ppermute(values, "shard", [(0, 1), (1, 0)])


def partners(devices, stride, size, flip):
    pairs = []
    for position in range(devices):
        digit = position // stride % size
        pairs.append((position, position + ((digit ^ flip) - digit) * stride))
    return pairs


def tree_sum(terms):
    terms = [term.astype(F32) for term in terms]
    while len(terms) > 1:
        terms = [terms[k] + terms[k + 1] for k in range(0, len(terms), 2)]
    return terms[0].astype(BF16)


def splits(devices):
    plan = []
    stride = 1
    while stride < devices:
        size = 4 if devices // stride % 4 == 0 else 2
        plan.append((stride, size, stride * size < devices))
        stride *= size
    return plan


def doublings(devices):
    return [(1, 4, True)] + [(4 << k, 2, False) for k in reversed(range((devices // 4).bit_length() - 1))]


def phase_count(plan):
    return 1 + len(plan) + sum(scattered for _, _, scattered in plan)


def exchange(keep, pack, devices, plan):
    got = yield [(pack, None)]
    value = tree_sum([keep, got[0]])
    index = lax.axis_index("dp")
    kept = []
    for stride, size, scattered in plan:
        digit = index // stride % size
        pairs = [partners(devices, stride, size, flip) for flip in range(1, size)]
        if not scattered:
            got = yield [(value, pair) for pair in pairs]
            value = tree_sum([value] + got)
        else:
            rows, columns = value.shape
            chunks = value.reshape(size, rows // size, columns)
            mine = lax.dynamic_index_in_dim(chunks, digit, 0, keepdims=False)
            got = yield [
                (lax.dynamic_index_in_dim(chunks, digit ^ flip, 0, keepdims=False), pairs[flip - 1])
                for flip in range(1, size)
            ]
            value = tree_sum([mine] + got)
            kept.append((size, digit, pairs))
    for size, digit, pairs in reversed(kept):
        got = yield [(value, pair) for pair in pairs]
        rows, columns = value.shape
        whole = jnp.zeros((size, rows, columns), BF16)
        for flip, piece in enumerate([value] + got):
            whole = lax.dynamic_update_index_in_dim(whole, piece, digit ^ flip, 0)
        value = whole.reshape(size * rows, columns)
    return value


def transfer(items):
    return [swap(value) if pairs is None else lax.ppermute(value, "dp", pairs) for value, pairs in items]


def resume(steps, got):
    try:
        return steps.send(got), None
    except StopIteration as stop:
        return None, stop.value


def tie(items, token):
    values, token = lax.optimization_barrier(([value for value, _ in items], token))
    return [(value, pairs) for value, (_, pairs) in zip(values, items)], token


def token_major(images):
    return with_layout_constraint(jnp.transpose(images, (1, 0, 2)), Layout((0, 1, 2)))


def beside(got, work, token, under_way=()):
    return lax.optimization_barrier((got, under_way, work(token)))


def skip_phases(steps, items, count):
    for _ in range(count):
        items, _ = resume(steps, transfer(items))
    return items


def on_device(
    images,
    counts,
    cotangent,
    attn_gain,
    attn_shift,
    qkv_weight,
    query_bias,
    value_bias,
    proj_weight,
    proj_bias,
    mlp_gain,
    mlp_shift,
    up_weight,
    up_bias,
    down_weight,
    down_bias,
):
    blocks, length, width = images.shape
    half = attn_gain.shape[0]
    hidden = 2 * up_bias.shape[0]
    devices = lax.axis_size("dp")
    me = lax.axis_index("shard")
    facts = jnp.stack([counts[0], me.astype(jnp.int32)])
    qkv_other = swap(qkv_weight)
    small = pack_small(
        [attn_gain, attn_shift, query_bias, value_bias, proj_bias, mlp_gain, mlp_shift, down_bias, up_bias]
    )
    small_other = swap(small)
    proj_other, up_other, down_other = swap(proj_weight), swap(up_weight), swap(down_weight)

    mixed, probs, context, vectors, up_bias_row = attend(
        facts, images, small, small_other, qkv_weight, qkv_other, hidden, 4
    )
    resid, active, dresid, dcontext, keep, pack = feed(
        facts,
        images,
        cotangent,
        context,
        vectors,
        up_bias_row,
        (proj_weight, proj_other, up_weight, up_other, down_weight, down_other),
        4,
    )

    def write_layer(token):
        rows = layer_output(token, images, resid, active, vectors, down_weight, down_other, 4)
        return token_major(rows)

    def back(token):
        return attend_back(token, images, mixed, probs, context, dcontext, 4)

    factor = 1.0 / math.sqrt(blocks * length * devices * lax.axis_size("shard"))
    count = blocks // 2
    feed_plan, plan = doublings(devices), splits(devices)

    def grads(start):
        return lambda token: input_grad(
            token, images, dresid, dmixed, vectors, qkv_weight, qkv_other, start, count, 4
        )

    feed_steps = exchange(keep, pack, devices, feed_plan)
    feed_items, _ = resume(feed_steps, transfer(next(feed_steps)))
    feed_items, token = tie(feed_items, facts)
    got, _, (dmixed, keep, pack) = beside(transfer(feed_items), back, token)

    feed_items, _ = resume(feed_steps, got)
    feed_items, token = tie(feed_items, facts)
    feed_got = transfer(feed_items)
    steps = exchange(keep, pack, devices, plan)
    got, feed_got, (layer_out, first_grads) = beside(
        transfer(next(steps)), lambda token: (write_layer(token), grads(0)(token)), token, feed_got
    )

    feed_items, _ = resume(feed_steps, feed_got)
    feed_items, token = tie(feed_items, facts)
    feed_got = transfer(feed_items)
    items, _ = resume(steps, got)
    items, token = tie(items, token)
    got, feed_got, last_grads = beside(transfer(items), grads(count), token, feed_got)

    feed_items, _ = resume(feed_steps, feed_got)
    feed_items = skip_phases(feed_steps, feed_items, phase_count(feed_plan) - 5)
    items, _ = resume(steps, got)
    items, both = tie(items, (first_grads, last_grads))
    got = transfer(items)
    feed_items, both = tie(feed_items, both)
    feed_arriving = transfer(feed_items)
    got, _, images_grad = beside(
        got, lambda both: token_major(jnp.concatenate(both, axis=0)), both
    )

    items, _ = resume(steps, got)
    items = skip_phases(steps, items, phase_count(plan) - 4)
    _, feed_total = resume(feed_steps, feed_arriving)
    items, token = tie(items, facts)
    got, _, unpacked = beside(
        transfer(items), lambda token: unpack_feed(token, feed_total, factor, half, hidden), token
    )
    _, attend_total = resume(steps, got)
    layer_out = jnp.transpose(layer_out, (1, 0, 2))
    up_g, down_g, proj_g, up_bias_g, proj_bias_g, mlp_gain_g, mlp_shift_g, down_bias_g = unpacked
    images_grad = jnp.transpose(images_grad, (1, 0, 2))
    qkv_g, attn_gain_g, attn_shift_g, query_bias_g, value_bias_g = unpack_attend(
        facts, attend_total, qkv_weight, small, factor
    )
    return (
        layer_out,
        images_grad,
        attn_gain_g,
        attn_shift_g,
        qkv_g,
        query_bias_g,
        value_bias_g,
        proj_g,
        proj_bias_g,
        mlp_gain_g,
        mlp_shift_g,
        up_g,
        up_bias_g,
        down_g,
        down_bias_g,
    )


def solution(mesh):
    placed = (
        P(("dp", "shard"), None, None),
        P(("dp", "shard")),
        P(("dp", "shard"), None, None),
        P("shard"),
        P("shard"),
        P("shard", None),
        P("shard"),
        P("shard"),
        P("shard", None),
        P("shard"),
        P("shard"),
        P("shard"),
        P("shard", None),
        P("shard"),
        P("shard", None),
        P("shard"),
    )
    return jax.shard_map(
        on_device,
        mesh=mesh,
        in_specs=placed,
        out_specs=(
            P(("dp", "shard"), None, None),
            P(("dp", "shard"), None, None),
            P("shard"),
            P("shard"),
            P("shard", None),
            P("shard"),
            P("shard"),
            P("shard", None),
            P("shard"),
            P("shard"),
            P("shard"),
            P("shard", None),
            P("shard"),
            P("shard", None),
            P("shard"),
        ),
        check_vma=False,
    )
```

```python
import functools
import math

import jax
import jax.numpy as jnp
from jax import lax
from jax.experimental import pallas as pl
from jax.experimental.layout import Layout, with_layout_constraint
from jax.experimental.pallas import tpu as pltpu
from jax.sharding import PartitionSpec as P

HEADS = 6
HEAD = 64
PAIR = 2 * HEAD
EPS = 1e-06
CHUNK = 256
DEPTH = 256
AHEAD3 = 3
LAG3 = 2
AHEAD = 3
LAG = 2
F32 = jnp.float32
BF16 = jnp.bfloat16
INV_SQRT_2PI = 1.0 / math.sqrt(2.0 * math.pi)


def up_to(size, step):
    return -(-size // step) * step


def nn(a, b):
    return lax.dot_general(a, b, (((1,), (0,)), ((), ())), preferred_element_type=F32)


def nt(a, b):
    return lax.dot_general(a, b, (((1,), (1,)), ((), ())), preferred_element_type=F32)


def tn(a, b):
    return lax.dot_general(a, b, (((0,), (0,)), ((), ())), preferred_element_type=F32)


def normalize(rows):
    center = jnp.mean(rows, axis=-1, keepdims=True)
    centered = rows - center
    inv = lax.rsqrt(jnp.mean(centered * centered, axis=-1, keepdims=True) + EPS)
    return centered * inv, inv


def normalize_back(hat, inv, dhat):
    first = jnp.mean(dhat, axis=-1, keepdims=True)
    second = jnp.mean(dhat * hat, axis=-1, keepdims=True)
    return inv * (dhat - first - hat * second)


def column_sum(rows):
    return jnp.sum(rows, axis=0, keepdims=True)


def pair_masks(dtype):
    lane = lax.broadcasted_iota(jnp.int32, (1, PAIR), 1)
    low = jnp.where(lane < HEAD, 1.0, 0.0)
    return low.astype(dtype), (1.0 - low).astype(dtype)


def gelu_parts(hidden):
    cdf = 0.5 + 0.5 * lax.erf(hidden * math.sqrt(0.5))
    return hidden * cdf, cdf + hidden * jnp.exp(hidden * hidden * -0.5) * INV_SQRT_2PI


def join_halves(whole, mine, other, me):
    half = mine.shape[0]
    whole[pl.ds(pl.multiple_of(me * half, 16), half), :] = mine[...]
    whole[pl.ds(pl.multiple_of((1 - me) * half, 16), half), :] = other[...]


def keep_rest(left, values, full):
    rest = values[0].shape[0] - full
    if rest:
        at = pl.ds(pl.multiple_of(pl.program_id(0) * rest, 16), rest)
        for ref, value in zip(left, values):
            ref[at, :] = value[full:]


def rest_space(blocks, rows, group, widths):
    rest = rows % DEPTH * (blocks // group)
    return [pltpu.VMEM((rest, width), BF16) for width in widths] if rest else []


def once(shape):
    return pl.BlockSpec(shape, lambda i: (0,) * len(shape), pipeline_mode=pl.Buffered(1))


SCALARS = pl.BlockSpec(memory_space=pltpu.SMEM)


def params(mebibytes):
    return pltpu.CompilerParams(vmem_limit_bytes=mebibytes * 2**20)


VMEM_WHOLE = pl.BlockSpec(memory_space=pltpu.VMEM)


def pack_small_kernel(*refs):
    out = refs[-1]
    half = out.shape[1]
    out[...] = jnp.zeros_like(out)
    for k, ref in enumerate(refs[:8]):
        out[k : k + 1, :] = ref[...].astype(F32).reshape(1, half)
    long = refs[8][...].astype(F32)
    for k in range(long.shape[0] // half):
        out[8 + k : 9 + k, :] = long[k * half : (k + 1) * half].reshape(1, half)


def pack_small(vectors):
    half = vectors[0].shape[0]
    return pl.pallas_call(
        pack_small_kernel,
        in_specs=[VMEM_WHOLE] * 9,
        out_specs=VMEM_WHOLE,
        out_shape=jax.ShapeDtypeStruct((16, half), F32),
        name="pack_small",
    )(*vectors)


def join_small(first, mine, other, vec_ref, up_bias_ref):
    near, far = jnp.where(first, mine, other), jnp.where(first, other, mine)
    vec_ref[...] = jnp.concatenate([near[:8], far[:8]], axis=1)
    count = up_bias_ref.shape[1] // mine.shape[1] // 2
    rows = [near[8 + k : 9 + k] for k in range(count)] + [far[8 + k : 9 + k] for k in range(count)]
    up_bias_ref[...] = jnp.concatenate(rows, axis=1)


def attend_kernel(length, group, facts, x_ref, small_mine, small_other, mine_ref, other_ref,
                  mixed_ref, probs_ref, context_ref, vec_ref, up_bias_ref, rows, qpad, weight):
    padded = rows.shape[0] // group
    width = rows.shape[1]

    @pl.when(pl.program_id(0) == 0)
    def _():
        rows[...] = jnp.zeros_like(rows)
        qpad[...] = jnp.zeros_like(qpad)
        join_halves(weight, mine_ref, other_ref, facts[1])
        join_small(facts[1] == 0, small_mine[...], small_other[...], vec_ref, up_bias_ref)

    for g in range(group):
        rows[g * padded : g * padded + length, :] = x_ref[g].astype(F32)
    hat, _ = normalize(rows[...])
    normed = (hat * vec_ref[0:1, :] + vec_ref[1:2, :]).astype(BF16)
    bias = jnp.concatenate([vec_ref[2:3, :], jnp.zeros((1, width), F32), vec_ref[3:4, :]], axis=1)
    mixed = (nn(normed, weight[...]) + bias).astype(BF16)
    mixed_ref[...] = mixed
    low, high = pair_masks(BF16)
    cut = length // 8 * 8
    live_key = lax.broadcasted_iota(jnp.int32, (padded - cut, 1), 0) < length - cut

    def scores_of(g, h):
        at = h // 2 * PAIR
        key = mixed[g * padded : (g + 1) * padded, width + at : width + at + PAIR] * (low if h % 2 == 0 else high)
        return nt(key, qpad[g, :, at : at + PAIR]) * 0.125

    def probs_of(g, h, scores):
        top = scores[:cut]
        rest = jnp.where(live_key, scores[cut:], -jnp.inf)
        peak = jnp.maximum(jnp.max(top, axis=0, keepdims=True), jnp.max(rest, axis=0, keepdims=True))
        top = jnp.exp(top - peak)
        rest = jnp.exp(rest - peak)
        scale = 1.0 / (column_sum(top) + column_sum(rest))
        probs = jnp.concatenate([top * scale, rest * scale], axis=0).astype(BF16)
        probs_ref[g, h] = probs
        return probs

    for g in range(group):
        qpad[g, :padded, :] = mixed[g * padded : (g + 1) * padded, :width]
    values_t = [mixed[g * padded : (g + 1) * padded, 2 * width :].T for g in range(group)]
    jobs = [(g, h) for g in range(group) for h in range(HEADS)]
    scores = {job: scores_of(*job) for job in jobs[:AHEAD]}
    outs, done = {}, {}
    for i, (g, h) in enumerate(jobs):
        if i + AHEAD < len(jobs):
            scores[jobs[i + AHEAD]] = scores_of(*jobs[i + AHEAD])
        done[g, h] = probs_of(g, h, scores.pop((g, h)))
        if i >= LAG:
            pg, ph = jobs[i - LAG]
            outs[pg, ph] = nn(values_t[pg][ph * HEAD : (ph + 1) * HEAD], done.pop((pg, ph)))
    for pg, ph in jobs[len(jobs) - LAG :]:
        outs[pg, ph] = nn(values_t[pg][ph * HEAD : (ph + 1) * HEAD], done.pop((pg, ph)))
    for g in range(group):
        context_t = jnp.concatenate([outs[g, h] for h in range(HEADS)], axis=0).astype(BF16)
        context_ref[g * padded : (g + 1) * padded, :] = context_t.T[:padded]


def attend(facts, images, small, small_other, mine, other, hidden, group):
    blocks, length, width = images.shape
    padded = up_to(length, 16)
    lanes = up_to(length, 128)
    return pl.pallas_call(
        functools.partial(attend_kernel, length, group),
        grid=(blocks // group,),
        in_specs=[
            SCALARS,
            pl.BlockSpec((group, length, width), lambda i: (i, 0, 0)),
            once(small.shape),
            once(small.shape),
            once(mine.shape),
            once(other.shape),
        ],
        out_specs=[
            pl.BlockSpec((group * padded, 3 * width), lambda i: (i, 0)),
            pl.BlockSpec((group, HEADS, padded, lanes), lambda i: (i, 0, 0, 0)),
            pl.BlockSpec((group * padded, width), lambda i: (i, 0)),
            once((8, width)),
            once((1, hidden)),
        ],
        out_shape=[
            jax.ShapeDtypeStruct((blocks * padded, 3 * width), BF16),
            jax.ShapeDtypeStruct((blocks, HEADS, padded, lanes), BF16),
            jax.ShapeDtypeStruct((blocks * padded, width), BF16),
            jax.ShapeDtypeStruct((8, width), F32),
            jax.ShapeDtypeStruct((1, hidden), F32),
        ],
        scratch_shapes=[
            pltpu.VMEM((group * padded, width), F32),
            pltpu.VMEM((group, lanes, width), BF16),
            pltpu.VMEM((width, 3 * width), BF16),
        ],
        compiler_params=params(50),
        cost_estimate=pl.CostEstimate(flops=10**10, bytes_accessed=3 * 10**7, transcendentals=0),
        name="attend",
    )(facts, images, small, small_other, mine, other)


def feed_kernel(length, group, facts, x_ref, cot_ref, context_ref, vec_ref, up_bias_ref,
                proj_mine, proj_other, up_mine, up_other, down_mine, down_other,
                resid_ref, active_ref, dresid_ref, dcontext_ref, keep_ref, send_ref,
                rows, cots, proj, up, down, up_g, down_g, proj_g, sums, up_sum, *left):
    padded = rows.shape[0] // group
    width = rows.shape[1]
    hidden_size = up.shape[1]
    step = pl.program_id(0)

    @pl.when(step == 0)
    def _():
        for ref in (rows, cots, up_g, down_g, proj_g, sums, up_sum):
            ref[...] = jnp.zeros_like(ref)
        join_halves(proj, proj_mine, proj_other, facts[1])
        join_halves(up, up_mine, up_other, facts[1])
        join_halves(down, down_mine, down_other, facts[1])

    for g in range(group):
        live = jnp.where(step * group + g < facts[0], 1.0, 0.0)
        rows[g * padded : g * padded + length, :] = x_ref[g].astype(F32)
        cots[g * padded : g * padded + length, :] = cot_ref[g].astype(F32) * live
    context = context_ref[...]
    resid = rows[...] + nn(context, proj[...]) + vec_ref[4:5, :]
    resid_ref[...] = resid.astype(BF16)
    hat, inv = normalize(resid)
    gain = vec_ref[5:6, :]
    normed = (hat * gain + vec_ref[6:7, :]).astype(BF16)
    dout = cots[...]
    dout_low = dout.astype(BF16)
    actives, dhiddens = [], []
    for at in range(0, hidden_size, CHUNK):
        cols = slice(at, at + CHUNK)
        hidden = nn(normed, up[:, cols]) + up_bias_ref[:, cols]
        active, slope = gelu_parts(hidden)
        actives.append(active.astype(BF16))
        active_ref[:, cols] = actives[-1]
        dhidden = nt(dout_low, down[cols, :]) * slope
        up_sum[0:1, cols] += column_sum(dhidden)
        dhiddens.append(dhidden.astype(BF16))
    active = jnp.concatenate(actives, axis=1)
    dhidden = jnp.concatenate(dhiddens, axis=1)
    dnormed = nt(dhidden, up[...])
    dresid = dout + normalize_back(hat, inv, dnormed * gain)
    dresid_low = dresid.astype(BF16)
    dresid_ref[...] = dresid_low
    dcontext_ref[...] = nt(dresid_low, proj[...]).astype(BF16)
    sums[0:1, :] += column_sum(dresid)
    sums[1:2, :] += column_sum(dnormed * hat)
    sums[2:3, :] += column_sum(dnormed)
    sums[3:4, :] += column_sum(dout)
    full = normed.shape[0] // DEPTH * DEPTH
    up_g[...] += tn(normed[:full], dhidden[:full])
    down_g[...] += tn(dout_low[:full], active[:full])
    proj_g[...] += tn(context[:full], dresid_low[:full])
    keep_rest(left, (normed, dhidden, dout_low, active, context, dresid_low), full)

    @pl.when(step == pl.num_programs(0) - 1)
    def _():
        if left:
            up_g[...] += tn(left[0][...], left[1][...])
            down_g[...] += tn(left[2][...], left[3][...])
            proj_g[...] += tn(left[4][...], left[5][...])
        half, part = width // 2, hidden_size // 4 * 3
        extra, third, own = hidden_size - part, width // 6, hidden_size // 2
        tall, last = half + third, part + own + width
        split = width - tall

        def put(k, ref):
            mine = slice(k * half, (k + 1) * half)
            ref[:half, :part] = up_g[mine, :part].astype(BF16)
            for j in range(3):
                strip = slice(k * half + j * third, k * half + (j + 1) * third)
                ref[half:, j * extra : (j + 1) * extra] = up_g[strip, part:].astype(BF16)
            ref[:, part : part + own] = down_g[:tall, k * own : (k + 1) * own].astype(BF16)
            for j in range(2):
                cols = slice(k * own + j * width, k * own + (j + 1) * width)
                ref[j * split : (j + 1) * split, part + own : last] = down_g[tall:, cols].astype(BF16)
            ref[:half, last:] = proj_g[mine, :].astype(BF16)
            totals = jnp.concatenate(
                [sums[0:4, :]]
                + [up_sum[0:1, j * width : (j + 1) * width] for j in range(hidden_size // width)]
                + [jnp.zeros((third - 4 - hidden_size // width, width), F32)],
                axis=0,
            )
            ref[half:, last:] = totals.astype(BF16)

        for k in range(2):
            @pl.when(facts[1] == k)
            def _(k=k):
                put(k, keep_ref)
                put(1 - k, send_ref)


def feed(facts, images, cotangent, context, vectors, up_bias, weights, group):
    blocks, length, width = images.shape
    padded = up_to(length, 16)
    hidden = up_bias.shape[1]
    row = lambda cols: pl.BlockSpec((group * padded, cols), lambda i: (i, 0))
    image = pl.BlockSpec((group, length, width), lambda i: (i, 0, 0))
    pack = (width // 2 + width // 6, hidden // 4 * 3 + hidden // 2 + 2 * width)
    return pl.pallas_call(
        functools.partial(feed_kernel, length, group),
        grid=(blocks // group,),
        in_specs=[SCALARS, image, image, row(width), once(vectors.shape), once(up_bias.shape)]
        + [once(weight.shape) for weight in weights],
        out_specs=[row(width), row(hidden), row(width), row(width), once(pack), once(pack)],
        out_shape=[
            jax.ShapeDtypeStruct((blocks * padded, width), BF16),
            jax.ShapeDtypeStruct((blocks * padded, hidden), BF16),
            jax.ShapeDtypeStruct((blocks * padded, width), BF16),
            jax.ShapeDtypeStruct((blocks * padded, width), BF16),
            jax.ShapeDtypeStruct(pack, BF16),
            jax.ShapeDtypeStruct(pack, BF16),
        ],
        scratch_shapes=[
            pltpu.VMEM((group * padded, width), F32),
            pltpu.VMEM((group * padded, width), F32),
            pltpu.VMEM((width, width), BF16),
            pltpu.VMEM((width, hidden), BF16),
            pltpu.VMEM((hidden, width), BF16),
            pltpu.VMEM((width, hidden), F32),
            pltpu.VMEM((width, hidden), F32),
            pltpu.VMEM((width, width), F32),
            pltpu.VMEM((8, width), F32),
            pltpu.VMEM((8, hidden), F32),
        ]
        + rest_space(blocks, group * padded, group, (width, hidden, width, hidden, width, width)),
        compiler_params=params(42),
        cost_estimate=pl.CostEstimate(flops=3 * 10**10, bytes_accessed=5 * 10**7, transcendentals=0),
        name="feed",
    )(facts, images, cotangent, context, vectors, up_bias, *weights)


def attend_back_kernel(length, group, facts, x_ref, mixed_ref, probs_ref, context_ref, dcontext_ref,
                       dmixed_ref, keep_ref, send_ref, rows, qpad, opad, turned, spread, qkv_g, sums, *left):
    padded = rows.shape[0] // group
    width = rows.shape[1]

    @pl.when(pl.program_id(0) == 0)
    def _():
        for ref in (rows, qpad, opad, turned, qkv_g, sums):
            ref[...] = jnp.zeros_like(ref)
        head_of = lax.broadcasted_iota(jnp.int32, spread.shape, 0) // HEAD
        column = lax.broadcasted_iota(jnp.int32, spread.shape, 1)
        spread[...] = jnp.where((column == head_of) | (column == head_of + 8), 1.0, 0.0).astype(BF16)

    low, high = pair_masks(BF16)
    lane = lax.broadcasted_iota(jnp.int32, (1, PAIR), 1)
    keys_t, queries_t, douts_t = [], [], []
    for g in range(group):
        rows[g * padded : g * padded + length, :] = x_ref[g].astype(F32)
        span = slice(g * padded, (g + 1) * padded)
        qpad[g, :padded, :] = mixed_ref[span, :width]
        dcontext = dcontext_ref[span, :]
        opad[g, :padded, :width] = dcontext
        delta = nn((dcontext.astype(F32) * context_ref[span, :].astype(F32)).astype(BF16), spread[...])
        coarse = delta.astype(BF16).astype(F32)
        opad[g, :padded, width:] = jnp.where(lane < 8, coarse, delta - coarse).astype(BF16)
        keys_t.append(mixed_ref[span, width : 2 * width].T)
        queries_t.append(qpad[g].T)
        douts_t.append(opad[g, :, :width].T)

    def dprobs_of(g, h):
        span = slice(g * padded, (g + 1) * padded)
        at = h // 2 * PAIR
        mask = low if h % 2 == 0 else high
        pick = jnp.where((lane == h) | (lane == h + 8), -1.0, 0.0).astype(BF16)
        value = mixed_ref[span, 2 * width + at : 2 * width + at + PAIR] * mask
        value = jnp.concatenate([value, jnp.broadcast_to(pick, value.shape)], axis=1)
        douter = jnp.concatenate([opad[g, :, at : at + PAIR], opad[g, :, width:]], axis=1)
        return nt(value, douter)

    def finish(g, h, dscores):
        own = slice(h * HEAD, (h + 1) * HEAD)
        turned[g, own, :] = (nn(keys_t[g][own], dscores) * 0.125).astype(BF16)
        dkey = nt(queries_t[g][own], dscores) * 0.125
        turned[g, width + h * HEAD : width + (h + 1) * HEAD, :padded] = dkey.astype(BF16)
        dvalue = nt(douts_t[g][own], probs_ref[g, h])
        turned[g, 2 * width + h * HEAD : 2 * width + (h + 1) * HEAD, :padded] = dvalue.astype(BF16)

    jobs = [(g, h) for g in range(group) for h in range(HEADS)]
    dprobs = {job: dprobs_of(*job) for job in jobs[:AHEAD3]}
    done = {}
    for i, job in enumerate(jobs):
        if i + AHEAD3 < len(jobs):
            dprobs[jobs[i + AHEAD3]] = dprobs_of(*jobs[i + AHEAD3])
        done[job] = (probs_ref[job[0], job[1]].astype(F32) * dprobs.pop(job)).astype(BF16)
        if i >= LAG3:
            finish(*jobs[i - LAG3], done.pop(jobs[i - LAG3]))
    for job in jobs[len(jobs) - LAG3 :]:
        finish(*job, done.pop(job))
    for g in range(group):
        dmixed_ref[g * padded : (g + 1) * padded, :] = turned[g].T[:padded]
    hat, _ = normalize(rows[...])
    dmixed = dmixed_ref[...]
    sums[0:1, :] += column_sum(dmixed.astype(F32))
    hat = hat.astype(BF16)
    full = hat.shape[0] // DEPTH * DEPTH
    qkv_g[...] += tn(hat[:full], dmixed[:full])
    keep_rest(left, (hat, dmixed), full)

    @pl.when(pl.program_id(0) == pl.num_programs(0) - 1)
    def _():
        if left:
            qkv_g[...] += tn(left[0][...], left[1][...])
        half, third = width // 2, width // 6
        part = 7 * PAIR
        rest = 3 * width - part

        def put(k, ref):
            ref[:half, :part] = qkv_g[k * half : (k + 1) * half, :part].astype(BF16)
            for j in range(3):
                strip = slice(k * half + j * third, k * half + (j + 1) * third)
                ref[half:, j * rest : (j + 1) * rest] = qkv_g[strip, part:].astype(BF16)
            totals = jnp.concatenate(
                [sums[0:1, j * PAIR : (j + 1) * PAIR] for j in range(3 * width // PAIR)]
                + [jnp.zeros((third - 3 * width // PAIR, PAIR), F32)],
                axis=0,
            )
            ref[half:, 3 * rest :] = totals.astype(BF16)

        for k in range(2):
            @pl.when(facts[1] == k)
            def _(k=k):
                put(k, keep_ref)
                put(1 - k, send_ref)


def attend_back(facts, images, mixed, probs, context, dcontext, group):
    blocks, length, width = images.shape
    padded = up_to(length, 16)
    lanes = up_to(length, 128)
    row = lambda cols: pl.BlockSpec((group * padded, cols), lambda i: (i, 0))
    pack = (width // 2 + width // 6, 7 * PAIR)
    return pl.pallas_call(
        functools.partial(attend_back_kernel, length, group),
        grid=(blocks // group,),
        in_specs=[
            SCALARS,
            pl.BlockSpec((group, length, width), lambda i: (i, 0, 0)),
            row(3 * width),
            pl.BlockSpec((group, HEADS, padded, lanes), lambda i: (i, 0, 0, 0)),
            row(width),
            row(width),
        ],
        out_specs=[row(3 * width), once(pack), once(pack)],
        out_shape=[
            jax.ShapeDtypeStruct((blocks * padded, 3 * width), BF16),
            jax.ShapeDtypeStruct(pack, BF16),
            jax.ShapeDtypeStruct(pack, BF16),
        ],
        scratch_shapes=[
            pltpu.VMEM((group * padded, width), F32),
            pltpu.VMEM((group, lanes, width), BF16),
            pltpu.VMEM((group, lanes, width + PAIR), BF16),
            pltpu.VMEM((group, 3 * width, lanes), BF16),
            pltpu.VMEM((width, PAIR), BF16),
            pltpu.VMEM((width, 3 * width), F32),
            pltpu.VMEM((8, 3 * width), F32),
        ]
        + rest_space(blocks, group * padded, group, (width, 3 * width)),
        compiler_params=params(50),
        cost_estimate=pl.CostEstimate(flops=2 * 10**10, bytes_accessed=3 * 10**7, transcendentals=0),
        name="attend_back",
    )(facts, images, mixed, probs, context, dcontext)


def layer_out_kernel(length, group, facts, resid_ref, active_ref, vec_ref, down_mine, down_other, out_ref, down):
    padded = resid_ref.shape[0] // group
    step = pl.program_id(0)

    @pl.when(step == 0)
    def _():
        join_halves(down, down_mine, down_other, facts[1])

    result = resid_ref[...].astype(F32) + nn(active_ref[...], down[...]) + vec_ref[7:8, :]
    for g in range(group):
        live = jnp.where(step * group + g < facts[0], 1.0, 0.0)
        out_ref[g] = (result[g * padded : g * padded + length] * live).astype(BF16)


def layer_output(facts, images, resid, active, vectors, mine, other, group):
    blocks, length, width = images.shape
    padded = up_to(length, 16)
    hidden = active.shape[1]
    row = lambda cols: pl.BlockSpec((group * padded, cols), lambda i: (i, 0))
    return pl.pallas_call(
        functools.partial(layer_out_kernel, length, group),
        grid=(blocks // group,),
        in_specs=[SCALARS, row(width), row(hidden), once(vectors.shape), once(mine.shape), once(other.shape)],
        out_specs=pl.BlockSpec((group, length, width), lambda i: (i, 0, 0)),
        out_shape=jax.ShapeDtypeStruct((blocks, length, width), BF16),
        scratch_shapes=[pltpu.VMEM((hidden, width), BF16)],
        compiler_params=params(46),
        cost_estimate=pl.CostEstimate(flops=10**10, bytes_accessed=2 * 10**7, transcendentals=0),
        name="layer_output",
    )(facts, resid, active, vectors, mine, other)


def input_grad_kernel(length, group, facts, x_ref, dresid_ref, dmixed_ref, vec_ref, qkv_mine, qkv_other,
                      dx_ref, rows, qkv):
    padded = rows.shape[0] // group

    @pl.when(pl.program_id(0) == 0)
    def _():
        rows[...] = jnp.zeros_like(rows)
        join_halves(qkv, qkv_mine, qkv_other, facts[1])

    for g in range(group):
        rows[g * padded : g * padded + length, :] = x_ref[g].astype(F32)
    dnormed = nt(dmixed_ref[...], qkv[...])
    hat, inv = normalize(rows[...])
    dx = dresid_ref[...].astype(F32) + normalize_back(hat, inv, dnormed * vec_ref[0:1, :])
    for g in range(group):
        dx_ref[g] = dx[g * padded : g * padded + length]


def input_grad(facts, images, dresid, dmixed, vectors, mine, other, start, count, group):
    _, length, width = images.shape
    padded = up_to(length, 16)
    base = start // group
    return pl.pallas_call(
        functools.partial(input_grad_kernel, length, group),
        grid=(count // group,),
        in_specs=[
            SCALARS,
            pl.BlockSpec((group, length, width), lambda i: (base + i, 0, 0)),
            pl.BlockSpec((group * padded, width), lambda i: (base + i, 0)),
            pl.BlockSpec((group * padded, 3 * width), lambda i: (base + i, 0)),
            once(vectors.shape),
            once(mine.shape),
            once(other.shape),
        ],
        out_specs=pl.BlockSpec((group, length, width), lambda i: (i, 0, 0)),
        out_shape=jax.ShapeDtypeStruct((count, length, width), F32),
        scratch_shapes=[
            pltpu.VMEM((group * padded, width), F32),
            pltpu.VMEM((width, 3 * width), BF16),
        ],
        compiler_params=params(58),
        cost_estimate=pl.CostEstimate(flops=10**9 * count, bytes_accessed=2 * 10**6 * count, transcendentals=0),
        name="input_grad",
    )(facts, images, dresid, dmixed, vectors, mine, other)


def unpack_feed_kernel(factor, facts, pack_ref, up_ref, down_ref, proj_ref, up_bias_ref, *vec_refs):
    half, hidden = up_ref.shape
    width = proj_ref.shape[1]
    part, third, own = hidden // 4 * 3, width // 6, hidden // 2
    extra, tall = hidden - part, half + third
    split = width - tall
    last = part + own + width
    whole = pack_ref[...].astype(F32) * factor
    up_ref[:, :part] = whole[:half, :part]
    for j in range(3):
        up_ref[j * third : (j + 1) * third, part:] = whole[half:, j * extra : (j + 1) * extra]
    down_ref[:, :tall] = whole[:, part : part + own].T
    for j in range(2):
        down_ref[j * width : (j + 1) * width, tall:] = whole[j * split : (j + 1) * split, part + own : last].T
    proj_ref[...] = whole[:half, last:]
    totals = whole[half : half + 8, last:]
    first = facts[1] == 0
    own_totals = jnp.where(first, totals[:, :half], totals[:, half:])
    for k, ref in enumerate(vec_refs):
        ref[...] = own_totals[k : k + 1, :].reshape(half)
    pieces = [totals[4 + j : 5 + j, :] for j in range(hidden // width)]
    near, far = jnp.concatenate(pieces[:2], axis=1), jnp.concatenate(pieces[2:], axis=1)
    up_bias_ref[...] = jnp.where(first, near, far).reshape(own)


def unpack_feed(facts, pack, factor, half, hidden):
    width = 2 * half
    return pl.pallas_call(
        functools.partial(unpack_feed_kernel, factor),
        in_specs=[SCALARS, VMEM_WHOLE],
        out_specs=[VMEM_WHOLE] * 8,
        out_shape=[
            jax.ShapeDtypeStruct((half, hidden), F32),
            jax.ShapeDtypeStruct((hidden // 2, width), F32),
            jax.ShapeDtypeStruct((half, width), F32),
            jax.ShapeDtypeStruct((hidden // 2,), F32),
        ]
        + [jax.ShapeDtypeStruct((half,), F32)] * 4,
        compiler_params=params(20),
        name="unpack_feed",
    )(facts, pack)


def unpack_attend_kernel(factor, facts, pack_ref, weight_ref, small_ref, qkv_ref, *vec_refs):
    half, wide = qkv_ref.shape
    width = wide // 3
    third, part = width // 6, 7 * PAIR
    rest = wide - part
    whole = pack_ref[...].astype(F32) * factor
    lower = [whole[half:, j * rest : (j + 1) * rest] for j in range(3)]
    product = jnp.concatenate([whole[:half, :part], jnp.concatenate(lower, axis=0)], axis=1)
    totals = jnp.concatenate(
        [whole[half + j : half + j + 1, 3 * rest :] for j in range(wide // PAIR)], axis=1
    )
    columns = small_ref[:8, :].T
    qkv_ref[...] = product * columns[:, 0:1] + totals * columns[:, 1:2]
    weight = weight_ref[...].astype(F32)

    def row_totals(values):
        lanes = sum(values[:, at : at + PAIR] for at in range(0, wide, PAIR))
        return column_sum(lanes.T)

    gain = row_totals(weight * product)
    shift = row_totals(weight * totals)
    first = facts[1] == 0
    query = jnp.where(first, totals[:, :half], totals[:, half:width])
    value = jnp.where(first, totals[:, 2 * width : 2 * width + half], totals[:, 2 * width + half :])
    for ref, row in zip(vec_refs, (gain, shift, query, value)):
        ref[...] = row.reshape(half)


def unpack_attend(facts, pack, weight, small, factor):
    half, wide = weight.shape
    return pl.pallas_call(
        functools.partial(unpack_attend_kernel, factor),
        in_specs=[SCALARS] + [VMEM_WHOLE] * 3,
        out_specs=[VMEM_WHOLE] * 5,
        out_shape=[jax.ShapeDtypeStruct((half, wide), F32)] + [jax.ShapeDtypeStruct((half,), F32)] * 4,
        compiler_params=params(12),
        name="unpack_attend",
    )(facts, pack, weight, small)


def swap(values):
    return lax.ppermute(values, "shard", [(0, 1), (1, 0)])


def partners(devices, stride, size, flip):
    pairs = []
    for position in range(devices):
        digit = position // stride % size
        pairs.append((position, position + ((digit ^ flip) - digit) * stride))
    return pairs


def tree_sum(terms):
    terms = [term.astype(F32) for term in terms]
    while len(terms) > 1:
        terms = [terms[k] + terms[k + 1] for k in range(0, len(terms), 2)]
    return terms[0].astype(BF16)


def splits(devices):
    plan = []
    stride = 1
    while stride < devices:
        size = 4 if devices // stride % 4 == 0 else 2
        plan.append((stride, size, stride * size < devices))
        stride *= size
    return plan


def doublings(devices):
    return [(1, 4, True)] + [(4 << k, 2, False) for k in reversed(range((devices // 4).bit_length() - 1))]


def phase_count(plan):
    return 1 + len(plan) + sum(scattered for _, _, scattered in plan)


def exchange(keep, pack, devices, plan):
    got = yield [(pack, None)]
    value = tree_sum([keep, got[0]])
    index = lax.axis_index("dp")
    kept = []
    for stride, size, scattered in plan:
        digit = index // stride % size
        pairs = [partners(devices, stride, size, flip) for flip in range(1, size)]
        if not scattered:
            got = yield [(value, pair) for pair in pairs]
            value = tree_sum([value] + got)
        else:
            rows, columns = value.shape
            chunks = value.reshape(size, rows // size, columns)
            mine = lax.dynamic_index_in_dim(chunks, digit, 0, keepdims=False)
            got = yield [
                (lax.dynamic_index_in_dim(chunks, digit ^ flip, 0, keepdims=False), pairs[flip - 1])
                for flip in range(1, size)
            ]
            value = tree_sum([mine] + got)
            kept.append((size, digit, pairs))
    for size, digit, pairs in reversed(kept):
        got = yield [(value, pair) for pair in pairs]
        rows, columns = value.shape
        whole = jnp.zeros((size, rows, columns), BF16)
        for flip, piece in enumerate([value] + got):
            whole = lax.dynamic_update_index_in_dim(whole, piece, digit ^ flip, 0)
        value = whole.reshape(size * rows, columns)
    return value


def transfer(items):
    return [swap(value) if pairs is None else lax.ppermute(value, "dp", pairs) for value, pairs in items]


def resume(steps, got):
    try:
        return steps.send(got), None
    except StopIteration as stop:
        return None, stop.value


def tie(items, token):
    values, token = lax.optimization_barrier(([value for value, _ in items], token))
    return [(value, pairs) for value, (_, pairs) in zip(values, items)], token


def token_major(images):
    return with_layout_constraint(jnp.transpose(images, (1, 0, 2)), Layout((0, 1, 2)))


def beside(got, work, token, under_way=()):
    return lax.optimization_barrier((got, under_way, work(token)))


def skip_phases(steps, items, count):
    for _ in range(count):
        items, _ = resume(steps, transfer(items))
    return items


def on_device(
    images,
    counts,
    cotangent,
    attn_gain,
    attn_shift,
    qkv_weight,
    query_bias,
    value_bias,
    proj_weight,
    proj_bias,
    mlp_gain,
    mlp_shift,
    up_weight,
    up_bias,
    down_weight,
    down_bias,
):
    blocks, length, width = images.shape
    half = attn_gain.shape[0]
    hidden = 2 * up_bias.shape[0]
    devices = lax.axis_size("dp")
    me = lax.axis_index("shard")
    facts = jnp.stack([counts[0], me.astype(jnp.int32)])
    qkv_other = swap(qkv_weight)
    small = pack_small(
        [attn_gain, attn_shift, query_bias, value_bias, proj_bias, mlp_gain, mlp_shift, down_bias, up_bias]
    )
    small_other = swap(small)
    proj_other, up_other, down_other = swap(proj_weight), swap(up_weight), swap(down_weight)

    mixed, probs, context, vectors, up_bias_row = attend(
        facts, images, small, small_other, qkv_weight, qkv_other, hidden, 4
    )
    resid, active, dresid, dcontext, keep, pack = feed(
        facts,
        images,
        cotangent,
        context,
        vectors,
        up_bias_row,
        (proj_weight, proj_other, up_weight, up_other, down_weight, down_other),
        4,
    )

    def write_layer(token):
        rows = layer_output(token, images, resid, active, vectors, down_weight, down_other, 4)
        return token_major(rows)

    def back(token):
        return attend_back(token, images, mixed, probs, context, dcontext, 4)

    factor = 1.0 / math.sqrt(blocks * length * devices * lax.axis_size("shard"))
    count = blocks // 2
    feed_plan, plan = doublings(devices), splits(devices)

    def grads(start):
        return lambda token: input_grad(
            token, images, dresid, dmixed, vectors, qkv_weight, qkv_other, start, count, 4
        )

    feed_steps = exchange(keep, pack, devices, feed_plan)
    feed_items, _ = resume(feed_steps, transfer(next(feed_steps)))
    feed_items, token = tie(feed_items, facts)
    got, _, (dmixed, keep, pack) = beside(transfer(feed_items), back, token)

    feed_items, _ = resume(feed_steps, got)
    feed_items, token = tie(feed_items, facts)
    feed_got = transfer(feed_items)
    steps = exchange(keep, pack, devices, plan)
    got, feed_got, (layer_out, first_grads) = beside(
        transfer(next(steps)), lambda token: (write_layer(token), grads(0)(token)), token, feed_got
    )

    feed_items, _ = resume(feed_steps, feed_got)
    feed_items, token = tie(feed_items, facts)
    feed_got = transfer(feed_items)
    items, _ = resume(steps, got)
    items, token = tie(items, token)
    got, feed_got, last_grads = beside(transfer(items), grads(count), token, feed_got)

    feed_items, _ = resume(feed_steps, feed_got)
    feed_items = skip_phases(feed_steps, feed_items, phase_count(feed_plan) - 5)
    items, _ = resume(steps, got)
    feed_items, both = tie(feed_items, (first_grads, last_grads))
    feed_arriving = transfer(feed_items)
    items, both = tie(items, both)
    got = transfer(items)
    got, feed_arriving, images_grad = beside(
        got, lambda both: token_major(jnp.concatenate(both, axis=0)), both, feed_arriving
    )

    items, _ = resume(steps, got)
    items = skip_phases(steps, items, phase_count(plan) - 4)
    _, feed_total = resume(feed_steps, feed_arriving)
    items, token = tie(items, facts)
    got, _, unpacked = beside(
        transfer(items), lambda token: unpack_feed(token, feed_total, factor, half, hidden), token
    )
    _, attend_total = resume(steps, got)
    layer_out = jnp.transpose(layer_out, (1, 0, 2))
    up_g, down_g, proj_g, up_bias_g, proj_bias_g, mlp_gain_g, mlp_shift_g, down_bias_g = unpacked
    images_grad = jnp.transpose(images_grad, (1, 0, 2))
    qkv_g, attn_gain_g, attn_shift_g, query_bias_g, value_bias_g = unpack_attend(
        facts, attend_total, qkv_weight, small, factor
    )
    return (
        layer_out,
        images_grad,
        attn_gain_g,
        attn_shift_g,
        qkv_g,
        query_bias_g,
        value_bias_g,
        proj_g,
        proj_bias_g,
        mlp_gain_g,
        mlp_shift_g,
        up_g,
        up_bias_g,
        down_g,
        down_bias_g,
    )


def solution(mesh):
    placed = (
        P(("dp", "shard"), None, None),
        P(("dp", "shard")),
        P(("dp", "shard"), None, None),
        P("shard"),
        P("shard"),
        P("shard", None),
        P("shard"),
        P("shard"),
        P("shard", None),
        P("shard"),
        P("shard"),
        P("shard"),
        P("shard", None),
        P("shard"),
        P("shard", None),
        P("shard"),
    )
    return jax.shard_map(
        on_device,
        mesh=mesh,
        in_specs=placed,
        out_specs=(
            P(("dp", "shard"), None, None),
            P(("dp", "shard"), None, None),
            P("shard"),
            P("shard"),
            P("shard", None),
            P("shard"),
            P("shard"),
            P("shard", None),
            P("shard"),
            P("shard"),
            P("shard"),
            P("shard", None),
            P("shard"),
            P("shard", None),
            P("shard"),
        ),
        check_vma=False,
    )
```
